256 devices in a mesh: row: 16 (over z, x_lo), col: 16 (over x_hi, y, core).
Axes of the slice: x: 4 (x_hi: 2, x_lo: 2; x = x_hi * 2 + x_lo), y: 4, z: 8, core: 2. Of those that a mesh axis runs over, the one named last changes fastest.
Arguments:
- patches: bfloat16 [512, 256, 768], P('row', 'col'), may hold values from -6 to 6
- norm_gain: float32 [768], replicated, may hold values from 0.25 to 1.75
- w_qkv: bfloat16 [768, 2304], replicated, may hold values from -0.21875 to 0.21875
- pool_q: float32 [9, 768], replicated, may hold values from -30 to 30, as said below
- pool_kv: float32 [9, 1536], replicated, may hold values from -2 to 2
- w_out: bfloat16 [768, 768], replicated, may hold values from -0.21875 to 0.21875
Outputs:
- mixed: bfloat16 [256, 128, 768], P('row', 'col')
The draws below stay inside these ranges and needn't reach their ends.
Inputs may be any that keep to these rules, and one draw needn't show every extreme that they name: `pool_q`: query pooling taps, nonzero, of either sign.
All inputs are finite; a program needn't handle non-finite values.
Results may differ from the reference program's by a relative error of at most 0.017.
The reference program's roundings to bfloat16 on the way (of `normed`, `projected`, `queries`, `keyvals`, `weights` and `attended`) count: a program that leaves them out, or rounds other values in their place, can miss the bound.
Values may be sent and summed in bfloat16 or wider, within the bound.
No kernel may reach another device: no remote copies, remote signals or barrier semaphores. Data moves between devices by JAX's collectives and lax.ppermute only.
A program may use at most 128 MiB of HBM per device.

```python
import math
import jax
import jax.numpy as jnp
from jax import lax

D = 768
HEADS = 12
HEAD = 64
ROWS = 512
COLS = 256
NQ = 32768


def draw_pool_q(key, part):
    sign_key = jax.random.fold_in(key, 11)
    size_key = jax.random.fold_in(key, 12)
    signs = jnp.where(jax.random.bernoulli(sign_key, 0.5, (9, D)), 1.0, -1.0)
    magnitude = jnp.exp(jax.random.uniform(size_key, (9, D), jnp.float32, math.log(0.1), math.log(0.6)))
    return (signs * magnitude).astype(jnp.float32)


def steps_of(stream_key, shape, pieces, smallest, top_value):
    def one(dim, blocks):
        heights = jax.random.uniform(jax.random.fold_in(jax.random.fold_in(stream_key, 6), dim), (blocks,), jnp.float32, smallest / len(pieces), top_value / len(pieces))
        return jnp.repeat(jnp.exp(heights), shape[dim] // blocks).reshape((-1,) + (1,) * (len(shape) - dim - 1))

    factor_of = one(*pieces[0])
    for cut in pieces[1:]:
        factor_of = factor_of * one(*cut)
    return factor_of


def gaussian(key, extent, deviation, bound, pieces=(), dtype=jnp.bfloat16):
    entries = deviation * jax.random.normal(key, extent, jnp.float32)
    if pieces:
        entries = entries * steps_of(key, extent, pieces, -0.22, 0.18)
    return jnp.clip(entries, -bound, bound).astype(dtype)


def setup_inputs(seed: int = 0) -> dict:
    splits = jax.random.split(jax.random.key(seed), 7)
    return {
        "patches": gaussian(splits[0], (ROWS, COLS, D), 1.0, 6.0, ((0, 16), (1, 16))),
        "norm_gain": jnp.clip(1.0 + 0.15 * jax.random.normal(splits[1], (D,), jnp.float32), 0.25, 1.75),
        "w_qkv": gaussian(splits[2], (D, 3 * D), D ** -0.5, 0.21875),
        "pool_q": draw_pool_q(jax.random.fold_in(splits[6], 71), 0),
        "pool_kv": gaussian(splits[4], (9, 2 * D), 0.35, 2.0, (), jnp.float32),
        "w_out": gaussian(splits[5], (D, D), D ** -0.5, 0.21875),
    }


def layer_norm(patches, norm_gain):
    values = patches.astype(jnp.float32)
    center = values - lax.optimization_barrier(jnp.mean(values, axis=-1, keepdims=True))
    spread = lax.optimization_barrier(jnp.mean(center * center, axis=-1, keepdims=True))
    return (center * lax.rsqrt(spread + 1e-06) * norm_gain).astype(jnp.bfloat16)

def pool_grid(padded, kernel, stride, out_rows, out_cols):
    summed = jnp.zeros((out_rows, out_cols, padded.shape[-1]), jnp.float32)
    for row_off in range(3):
        for col_off in range(3):
            window = padded[row_off:row_off + stride * out_rows:stride, col_off:col_off + stride * out_cols:stride]
            summed = summed + kernel[3 * row_off + col_off] * window.astype(jnp.float32)
    return summed.astype(jnp.bfloat16)

def reference(patches, norm_gain, w_qkv, pool_q, pool_kv, w_out):
    normed = layer_norm(patches, norm_gain)
    projected = jnp.dot(normed.reshape(-1, D), w_qkv, preferred_element_type=jnp.float32)
    projected = projected.astype(jnp.bfloat16).reshape(ROWS, COLS, 3 * D)
    padded = jnp.pad(projected, ((1, 0), (1, 0), (0, 0)))
    queries = pool_grid(padded[..., :D], pool_q, 2, ROWS // 2, COLS // 2).reshape(-1, HEADS, HEAD)
    keyvals = pool_grid(padded[..., D:], pool_kv, 4, ROWS // 4, COLS // 4).reshape(-1, 2 * D)
    key_heads = keyvals[:, :D].reshape(-1, HEADS, HEAD).astype(jnp.float32)
    val_heads = keyvals[:, D:].reshape(-1, HEADS, HEAD).astype(jnp.float32)
    scale = float(HEAD) ** (-0.5)
    q_block = math.gcd(512, NQ)
    blocks = queries.reshape(NQ // q_block, q_block, HEADS, HEAD)

    def attend(block):
        scores = jnp.einsum('qhd,khd->hqk', block.astype(jnp.float32), key_heads) * scale
        row_max = lax.optimization_barrier(jnp.max(scores, axis=-1))
        expo = jnp.exp(scores - row_max[..., None])
        total = lax.optimization_barrier(jnp.sum(expo, axis=-1))
        weights = expo.astype(jnp.bfloat16).astype(jnp.float32)
        numer = jnp.einsum('hqk,khd->hqd', weights, val_heads)
        result = numer / total[..., None]
        return result.transpose(1, 0, 2).reshape(q_block, D).astype(jnp.bfloat16)
    attended = lax.map(attend, blocks).reshape(NQ, D)
    mixed = jnp.dot(attended, w_out, preferred_element_type=jnp.float32).astype(jnp.bfloat16)
    return mixed.reshape(ROWS // 2, COLS // 2, D)
```

```python
import functools
import math

import jax
import jax.numpy as jnp
from jax import lax
from jax.experimental import pallas as pl
from jax.experimental.pallas import tpu as pltpu
from jax.sharding import Mesh
from jax.sharding import PartitionSpec as P

AXES = ("za", "zl", "xl", "xh", "y", "core")
ROW = ("za", "zl", "xl")
COL = ("xh", "y", "core")
HEAD = 64
GROUP = 3
WIDE = GROUP * HEAD
SCALE = HEAD**-0.5 * math.log2(math.e)
STATS = 16
bf16, f32 = jnp.bfloat16, jnp.float32


def shifted(block, axis, distance):
    count = lax.axis_size(axis)
    return lax.ppermute(block, axis, [(i, (i + distance) % count) for i in range(count)])


def shifted_x(block, distance):
    place = lambda i: (i % 2) * 2 + i // 2
    route = [(place(i), place((i + distance) % 4)) for i in range(4)]
    return lax.ppermute(block, ("xl", "xh"), route)


def passed_along(block, axis):
    count = lax.axis_size(axis)
    return lax.ppermute(block, axis, [(i - 1, i) for i in range(1, count)])


def corner(block):
    rows, cols = lax.axis_size(ROW), lax.axis_size(COL)
    route = [((r - 1) * cols + c - 1, r * cols + c) for r in range(1, rows) for c in range(1, cols)]
    return lax.ppermute(block, AXES, route)


def layer_norm(patches, norm_gain):
    values = patches.astype(f32)
    center = values - jnp.mean(values, axis=-1, keepdims=True)
    spread = jnp.mean(center * center, axis=-1, keepdims=True)
    return (center * lax.rsqrt(spread + 1e-06) * norm_gain).astype(bf16)


def pool_grid(padded, kernel, stride, out_rows, out_cols):
    summed = jnp.zeros((out_rows, out_cols, padded.shape[-1]), f32)
    for row_off in range(3):
        for col_off in range(3):
            window = padded[
                row_off : row_off + stride * out_rows : stride,
                col_off : col_off + stride * out_cols : stride,
            ]
            summed = summed + kernel[3 * row_off + col_off] * window.astype(f32)
    return summed.astype(bf16)


def attend_kernel(first, last, block, qb, q_ref, kv_ref, *refs):
    if first:
        carry_in = None
    else:
        carry_in, refs = refs[:2], refs[2:]
    outs, (qz, stat, acc) = refs[:-3], refs[-3:]
    step = pl.program_id(0)
    tiles = q_ref.shape[0]
    count = tiles * 128

    @pl.when(step == 0)
    def _():
        zero = jnp.zeros((HEAD, count), bf16)
        q = jnp.concatenate([q_ref[t] for t in range(tiles)], axis=1)
        qz[0] = jnp.concatenate([q[:HEAD], zero], 0)
        qz[1] = jnp.concatenate([zero, q[HEAD : 2 * HEAD]], 0)
        qz[2] = jnp.concatenate([q[2 * HEAD :], zero], 0)
        if first:
            stat[0:8] = jnp.full((8, count), -1e30, f32)
            stat[8:16] = jnp.zeros((8, count), f32)
            acc[...] = jnp.zeros_like(acc)
        else:
            stat[...] = carry_in[0][...]
            acc[...] = carry_in[1][...]

    values = kv_ref[:, 128:384].T
    ones = jnp.ones((16, block), bf16)
    jobs = [(h, j) for j in range(count // qb) for h in range(GROUP)]

    def scores(h, j):
        keys = kv_ref[:, 0:128] if h < 2 else kv_ref[:, 128:256]
        return jnp.dot(keys, qz[h, :, j * qb : (j + 1) * qb], preferred_element_type=f32)

    ready = scores(*jobs[0])
    for place, (h, j) in enumerate(jobs):
        now = ready
        if place + 1 < len(jobs):
            ready = scores(*jobs[place + 1])
        lanes = slice(j * qb, (j + 1) * qb)
        old = stat[h : h + 1, lanes]
        new = jnp.maximum(old, jnp.max(now, axis=0, keepdims=True))
        factor = jnp.exp2((old - new) * SCALE)
        weights = jnp.exp2((now - new) * SCALE).astype(bf16)
        stat[h : h + 1, lanes] = new
        value = jnp.concatenate([values[HEAD * (h + 1) : HEAD * (h + 2)], ones], 0)
        part = jnp.dot(value, weights, preferred_element_type=f32)
        rows = slice(HEAD * h, HEAD * (h + 1))
        stat[8 + h : 9 + h, lanes] = stat[8 + h : 9 + h, lanes] * factor + part[HEAD : HEAD + 1]
        acc[rows, lanes] = acc[rows, lanes] * factor + part[:HEAD]

    @pl.when(step == pl.num_programs(0) - 1)
    def _():
        if not last:
            outs[0][...] = stat[...]
            outs[1][...] = acc[...]
            return
        total = stat[8:16]
        logs = stat[0:8] * SCALE + jnp.log2(jnp.maximum(total, 1e-30))
        high = logs.astype(bf16)
        left = logs - high.astype(f32)
        middle = left.astype(bf16)
        low = (left - middle.astype(f32)).astype(bf16)
        three = [a.astype(f32)[:GROUP] for a in (high, middle, low)]
        packed = jnp.concatenate(three + [jnp.zeros((STATS - 9, count), f32)], 0).astype(bf16)
        for t in range(tiles):
            lanes = slice(t * 128, (t + 1) * 128)
            for h in range(GROUP):
                rows = slice(HEAD * h, HEAD * (h + 1))
                outs[0][t, rows] = (acc[rows, lanes] / total[h : h + 1, lanes]).astype(bf16)
            outs[0][t, WIDE:] = packed[:, lanes]


def attend(queries, keyvals, carry, last, block=512, qb=512):
    tiles = queries.shape[0]
    count = tiles * 128
    keys = keyvals.shape[0]
    block = min(block, keys)
    whole = lambda shape: pl.BlockSpec(shape, lambda i: (0,) * len(shape))
    carry_shapes = [(16, count), (WIDE, count)]
    carry_specs = [whole(s) for s in carry_shapes]
    if last:
        out_shape = jax.ShapeDtypeStruct((tiles, WIDE + STATS, 128), bf16)
        out_specs = whole(out_shape.shape)
    else:
        out_shape = [jax.ShapeDtypeStruct(s, f32) for s in carry_shapes]
        out_specs = carry_specs
    work = GROUP * count * keys
    return pl.pallas_call(
        functools.partial(attend_kernel, carry is None, last, block, qb),
        grid=(keys // block,),
        in_specs=[whole(queries.shape), pl.BlockSpec((block, 2 * WIDE), lambda i: (i, 0))]
        + ([] if carry is None else carry_specs),
        out_specs=out_specs,
        out_shape=out_shape,
        scratch_shapes=[
            pltpu.VMEM((GROUP, 128, count), bf16),
            pltpu.VMEM((16, count), f32),
            pltpu.VMEM((WIDE, count), f32),
        ],
        compiler_params=pltpu.CompilerParams(vmem_limit_bytes=48 * 2**20),
        cost_estimate=pl.CostEstimate(
            flops=work * 1024, bytes_accessed=keys * 768, transcendentals=work
        ),
    )(queries, keyvals, *(carry or ()))


def finish_kernel(parts_ref, w_ref, out_ref):
    groups = parts_ref.shape[0] // 2
    pieces = []
    for g in range(groups):
        pair = [parts_ref[g], parts_ref[groups + g]]
        logs = []
        for p in pair:
            s = p[WIDE:].astype(f32)
            logs.append((s[0:3] + s[3:6]) + s[6:9])
        top = jnp.maximum(logs[0], logs[1])
        shares = [jnp.exp2(a - top) for a in logs]
        total = shares[0] + shares[1]
        for h in range(GROUP):
            rows = slice(HEAD * h, HEAD * (h + 1))
            both = sum(p[rows].astype(f32) * (s[h : h + 1] / total[h : h + 1]) for p, s in zip(pair, shares))
            pieces.append(both)
    attended = jnp.concatenate(pieces, 0).T.astype(bf16)
    out_ref[...] = jnp.dot(attended, w_ref[...], preferred_element_type=f32).astype(bf16)


def finish(parts, w_out):
    return pl.pallas_call(
        finish_kernel,
        out_shape=jax.ShapeDtypeStruct((parts.shape[2], w_out.shape[1]), bf16),
        compiler_params=pltpu.CompilerParams(vmem_limit_bytes=48 * 2**20),
    )(parts, w_out)


def on_device(patches, norm_gain, w_qkv, pool_q, pool_kv, w_out):
    tile_rows, tile_cols, width = patches.shape
    upper = passed_along(patches[-1:], ROW)
    left = passed_along(patches[:, -1:], COL)
    above_left = corner(patches[-1:, -1:])
    extended = jnp.concatenate(
        [jnp.concatenate([above_left, upper], 1), jnp.concatenate([left, patches], 1)], 0
    )
    normed = layer_norm(extended, norm_gain)
    projected = jnp.dot(normed.reshape(-1, width), w_qkv, preferred_element_type=f32)
    projected = projected.astype(bf16).reshape(tile_rows + 1, tile_cols + 1, 3 * width)
    queries = pool_grid(projected[..., :width], pool_q, 2, tile_rows // 2, tile_cols // 2)
    keyvals = pool_grid(projected[..., width:], pool_kv, 4, tile_rows // 4, tile_cols // 4)
    groups = lax.axis_size("zl")
    turned = queries.reshape(-1, width).T.reshape(groups, WIDE, -1)
    flat = keyvals.reshape(-1, 2, groups, WIDE).transpose(2, 0, 1, 3).reshape(groups, -1, 2 * WIDE)
    own = lax.all_to_all(flat, "zl", 0, 0, tiled=True).reshape(-1, 2 * WIDE)
    every_query = lax.all_to_all(
        jnp.concatenate([turned, turned], 0), ("za", "zl"), 0, 0, tiled=True
    )
    line = jnp.concatenate([own, shifted_x(own, 1), shifted_x(own, -1), shifted_x(own, 2)], 0)
    swap = lambda block: shifted(block, "core", 1)
    after, before = shifted(line, "y", 1), shifted(line, "y", -1)
    half = line.shape[0] // 2
    far = [shifted(after[:half], "y", 1), shifted(before[half:], "y", -1)]
    carry = attend(every_query, line, None, False)
    carry = attend(every_query, swap(line), carry, False)
    for block in (after, swap(after), before, swap(before)):
        carry = attend(every_query, block, carry, False)
    far = jnp.concatenate(far, 0)
    carry = attend(every_query, far, carry, False)
    partial = attend(every_query, swap(far), carry, True)
    parts = lax.all_to_all(partial, ("za", "zl"), 0, 0, tiled=True)
    mixed = finish(parts, w_out)
    return mixed.reshape(tile_rows // 2, tile_cols // 2, width)


def solution(mesh):
    fine = Mesh(mesh.devices.reshape(2, 4, 2, 2, 4, 2), AXES)
    tiles = P(ROW, COL, None)
    return jax.shard_map(
        on_device,
        mesh=fine,
        in_specs=(tiles, P(), P(), P(), P(), P()),
        out_specs=tiles,
        check_vma=False,
    )
```

```python
import functools
import math

import jax
import jax.numpy as jnp
from jax import lax
from jax.experimental import pallas as pl
from jax.experimental.pallas import tpu as pltpu
from jax.sharding import Mesh
from jax.sharding import PartitionSpec as P

AXES = ("za", "zl", "xl", "xh", "y", "core")
ROW = ("za", "zl", "xl")
COL = ("xh", "y", "core")
HEAD = 64
GROUP = 3
WIDE = GROUP * HEAD
SCALE = HEAD**-0.5 * math.log2(math.e)
STATS = 16
bf16, f32 = jnp.bfloat16, jnp.float32


def shifted(block, axis, distance):
    count = lax.axis_size(axis)
    return lax.ppermute(block, axis, [(i, (i + distance) % count) for i in range(count)])


def shifted_x(block, distance):
    place = lambda i: (i % 2) * 2 + i // 2
    route = [(place(i), place((i + distance) % 4)) for i in range(4)]
    return lax.ppermute(block, ("xl", "xh"), route)


def passed_along(block, axis):
    count = lax.axis_size(axis)
    return lax.ppermute(block, axis, [(i - 1, i) for i in range(1, count)])


def corner(block):
    rows, cols = lax.axis_size(ROW), lax.axis_size(COL)
    route = [((r - 1) * cols + c - 1, r * cols + c) for r in range(1, rows) for c in range(1, cols)]
    return lax.ppermute(block, AXES, route)


def normalised(values, gain):
    center = values - jnp.mean(values, axis=-1, keepdims=True)
    spread = jnp.mean(center * center, axis=-1, keepdims=True)
    return (center * lax.rsqrt(spread + 1e-06) * gain).astype(bf16)


def project(tokens, weights):
    return jnp.dot(tokens, weights, preferred_element_type=f32).astype(bf16)


ORDER = (0, 1, 3, 4, 5, 7, 8, 9, 11, 12, 13, 2, 6, 10, 14, 15)
KEY_COLUMNS = 11


def keep(plain, values):
    for k in range(plain.shape[0]):
        plain[k] = values[:, 128 * k : 128 * (k + 1)]


def every_nth(plain, start, step):
    picked = [plain[k, pl.ds(start, 8, stride=step), :] for k in range(plain.shape[0])]
    return jnp.concatenate(picked, 1)


def own_kernel(patches_ref, gain_ref, wq_ref, wk_ref, wv_ref, q_ref, kv_ref, plain, tokens):
    rows, cols, width = patches_ref.shape
    keep(plain, patches_ref[...].astype(f32).reshape(rows * cols, width))
    gain = gain_ref[...]
    for place, c in enumerate(ORDER):
        parts = [every_nth(plain, 16 * r + c, 64) for r in range(4)]
        tokens[pl.ds(32 * place, 32), :] = normalised(jnp.concatenate(parts, 0), gain)
    few = tokens[: 32 * KEY_COLUMNS]
    kv_ref[:, :width] = project(few, wk_ref[...])
    kv_ref[:, width:] = project(few, wv_ref[...])
    q_ref[...] = project(tokens[...], wq_ref[...])


def column_of_w(i):
    return pl.BlockSpec((768, 768), lambda _: (0, i))


def whole(shape):
    return pl.BlockSpec(shape, lambda _: (0,) * len(shape))


def project_own(patches, gain, w_qkv):
    rows, cols, width = patches.shape
    count = rows * cols
    shapes = [(count, width), (32 * KEY_COLUMNS, 2 * width)]
    return pl.pallas_call(
        own_kernel,
        grid=(1,),
        in_specs=[whole(patches.shape), whole(gain.shape)] + [column_of_w(i) for i in range(3)],
        out_specs=[whole(s) for s in shapes],
        out_shape=[jax.ShapeDtypeStruct(s, bf16) for s in shapes],
        scratch_shapes=[pltpu.VMEM((width // 128, count, 128), f32), pltpu.VMEM((count, width), bf16)],
        compiler_params=pltpu.CompilerParams(vmem_limit_bytes=48 * 2**20),
        cost_estimate=pl.CostEstimate(flops=1_400_000_000, bytes_accessed=6_000_000, transcendentals=0),
    )(patches, gain, w_qkv, w_qkv, w_qkv)


def halo_tokens(upper_ref, left_ref, corner_ref, gain_ref, plain):
    keep(plain, left_ref[...].astype(f32))
    left = jnp.concatenate([every_nth(plain, r, 4) for r in range(4)], 0)
    rest = jnp.zeros((15, left.shape[1]), f32)
    every = [left, upper_ref[...].astype(f32), corner_ref[...].astype(f32), rest]
    return normalised(jnp.concatenate(every, 0), gain_ref[...])


def columns_of(own_ref, halo, columns):
    first = lax.broadcasted_iota(jnp.int32, (8, own_ref.shape[1]), 0) == 0
    groups = {}
    for c in columns:
        if c < 0:
            block, above = halo[0:32], halo[48:49]
        else:
            place = ORDER.index(c)
            block, above = own_ref[pl.ds(32 * place, 32), :].astype(f32), halo[32 + c : 33 + c]
        four = [block[8 * r : 8 * r + 8] for r in range(4)]
        groups[c] = [jnp.where(first, above, pltpu.roll(four[3], 1, 0))] + four
    return groups


def pooled(groups, taps, column, row):
    total = None
    for a in range(3):
        for b in range(3):
            term = taps[3 * a + b] * groups[column + b - 1][row + a]
            total = term if total is None else total + term
    return total


def keyvals_kernel(own_ref, upper_ref, left_ref, corner_ref, gain_ref, wk_ref, wv_ref, pool_ref, out_ref, plain):
    tokens = halo_tokens(upper_ref, left_ref, corner_ref, gain_ref, plain)
    width = wk_ref.shape[1]
    both = []
    for part, w_ref in enumerate((wk_ref, wv_ref)):
        cols = pl.ds(part * width, width)
        halo = project(tokens, w_ref[...]).astype(f32)
        taps = [pool_ref[t : t + 1, cols] for t in range(9)]
        groups = columns_of(own_ref.at[:, cols], halo, (-1,) + ORDER[:KEY_COLUMNS])
        both.append(jnp.concatenate([pooled(groups, taps, 4 * j, 0) for j in range(4)], 0))
    for g in range(out_ref.shape[0]):
        lanes = slice(g * WIDE, (g + 1) * WIDE)
        out_ref[g] = jnp.concatenate([p[:, lanes] for p in both], 1).astype(bf16)


def queries_kernel(own_ref, upper_ref, left_ref, corner_ref, gain_ref, w_ref, pool_ref, out_ref, plain):
    tokens = halo_tokens(upper_ref, left_ref, corner_ref, gain_ref, plain)
    halo = project(tokens, w_ref[...]).astype(f32)
    taps = [pool_ref[t : t + 1, :] for t in range(9)]
    groups = columns_of(own_ref, halo, range(-1, 16))
    rows = [pooled(groups, taps, 2 * j, 2 * p) for j in range(8) for p in range(2)]
    turned = jnp.concatenate(rows, 0).T.astype(bf16)
    count = out_ref.shape[0] // 2
    for g in range(count):
        block = turned[g * WIDE : (g + 1) * WIDE]
        out_ref[g] = block
        out_ref[count + g] = block


def pool_call(kernel, own, halo, gain, w_qkv, parts, taps, out_shape):
    return pl.pallas_call(
        kernel,
        grid=(1,),
        in_specs=[whole(a.shape) for a in (own, *halo, gain)]
        + [column_of_w(i) for i in parts]
        + [whole(taps.shape)],
        out_specs=whole(out_shape),
        out_shape=jax.ShapeDtypeStruct(out_shape, bf16),
        scratch_shapes=[pltpu.VMEM((gain.shape[1] // 128, 32, 128), f32)],
        compiler_params=pltpu.CompilerParams(vmem_limit_bytes=48 * 2**20),
        cost_estimate=pl.CostEstimate(flops=200_000_000, bytes_accessed=4_000_000, transcendentals=0),
    )(own, *halo, gain, *([w_qkv] * len(parts)), taps)


def attend_kernel(first, last, block, qb, q_ref, kv_ref, *refs):
    if first:
        carry_in = None
    else:
        carry_in, refs = refs[:2], refs[2:]
    outs, (qz, stat, acc) = refs[:-3], refs[-3:]
    step = pl.program_id(0)
    tiles = q_ref.shape[0]
    count = tiles * 128

    @pl.when(step == 0)
    def _():
        zero = jnp.zeros((HEAD, count), bf16)
        q = jnp.concatenate([q_ref[t] for t in range(tiles)], axis=1)
        qz[0] = jnp.concatenate([q[:HEAD], zero], 0)
        qz[1] = jnp.concatenate([zero, q[HEAD : 2 * HEAD]], 0)
        qz[2] = jnp.concatenate([q[2 * HEAD :], zero], 0)
        if first:
            stat[0:8] = jnp.full((8, count), -1e30, f32)
            stat[8:16] = jnp.zeros((8, count), f32)
            acc[...] = jnp.zeros_like(acc)
        else:
            stat[...] = carry_in[0][...]
            acc[...] = carry_in[1][...]

    values = kv_ref[:, 128:384].T
    ones = jnp.ones((16, block), bf16)
    jobs = [(h, j) for j in range(count // qb) for h in range(GROUP)]

    def scores(h, j):
        keys = kv_ref[:, 0:128] if h < 2 else kv_ref[:, 128:256]
        return jnp.dot(keys, qz[h, :, j * qb : (j + 1) * qb], preferred_element_type=f32)

    ready = scores(*jobs[0])
    for place, (h, j) in enumerate(jobs):
        now = ready
        if place + 1 < len(jobs):
            ready = scores(*jobs[place + 1])
        lanes = slice(j * qb, (j + 1) * qb)
        old = stat[h : h + 1, lanes]
        new = jnp.maximum(old, jnp.max(now, axis=0, keepdims=True))
        factor = jnp.exp2((old - new) * SCALE)
        weights = jnp.exp2((now - new) * SCALE).astype(bf16)
        stat[h : h + 1, lanes] = new
        value = jnp.concatenate([values[HEAD * (h + 1) : HEAD * (h + 2)], ones], 0)
        part = jnp.dot(value, weights, preferred_element_type=f32)
        rows = slice(HEAD * h, HEAD * (h + 1))
        stat[8 + h : 9 + h, lanes] = stat[8 + h : 9 + h, lanes] * factor + part[HEAD : HEAD + 1]
        acc[rows, lanes] = acc[rows, lanes] * factor + part[:HEAD]

    @pl.when(step == pl.num_programs(0) - 1)
    def _():
        if not last:
            outs[0][...] = stat[...]
            outs[1][...] = acc[...]
            return
        total = stat[8:16]
        logs = stat[0:8] * SCALE + jnp.log2(jnp.maximum(total, 1e-30))
        high = logs.astype(bf16)
        left = logs - high.astype(f32)
        middle = left.astype(bf16)
        low = (left - middle.astype(f32)).astype(bf16)
        three = [a.astype(f32)[:GROUP] for a in (high, middle, low)]
        packed = jnp.concatenate(three + [jnp.zeros((STATS - 9, count), f32)], 0).astype(bf16)
        for t in range(tiles):
            lanes = slice(t * 128, (t + 1) * 128)
            for h in range(GROUP):
                rows = slice(HEAD * h, HEAD * (h + 1))
                outs[0][t, rows] = (acc[rows, lanes] / total[h : h + 1, lanes]).astype(bf16)
            outs[0][t, WIDE:] = packed[:, lanes]


def attend(queries, keyvals, carry, last, block=512, qb=512):
    tiles = queries.shape[0]
    count = tiles * 128
    keys = keyvals.shape[0]
    block = min(block, keys)
    carry_shapes = [(16, count), (WIDE, count)]
    carry_specs = [whole(s) for s in carry_shapes]
    if last:
        out_shape = jax.ShapeDtypeStruct((tiles, WIDE + STATS, 128), bf16)
        out_specs = whole(out_shape.shape)
    else:
        out_shape = [jax.ShapeDtypeStruct(s, f32) for s in carry_shapes]
        out_specs = carry_specs
    work = GROUP * count * keys
    return pl.pallas_call(
        functools.partial(attend_kernel, carry is None, last, block, qb),
        grid=(keys // block,),
        in_specs=[whole(queries.shape), pl.BlockSpec((block, 2 * WIDE), lambda i: (i, 0))]
        + ([] if carry is None else carry_specs),
        out_specs=out_specs,
        out_shape=out_shape,
        scratch_shapes=[
            pltpu.VMEM((GROUP, 128, count), bf16),
            pltpu.VMEM((16, count), f32),
            pltpu.VMEM((WIDE, count), f32),
        ],
        compiler_params=pltpu.CompilerParams(vmem_limit_bytes=48 * 2**20),
        cost_estimate=pl.CostEstimate(
            flops=work * 1024, bytes_accessed=keys * 768, transcendentals=work
        ),
    )(queries, keyvals, *(carry or ()))


def finish_kernel(parts_ref, w_ref, out_ref, rows):
    groups = parts_ref.shape[0] // 2
    pieces = []
    for g in range(groups):
        pair = [parts_ref[g], parts_ref[groups + g]]
        logs = []
        for p in pair:
            s = p[WIDE:].astype(f32)
            logs.append((s[0:3] + s[3:6]) + s[6:9])
        top = jnp.maximum(logs[0], logs[1])
        shares = [jnp.exp2(a - top) for a in logs]
        total = shares[0] + shares[1]
        for h in range(GROUP):
            head = slice(HEAD * h, HEAD * (h + 1))
            both = [p[head].astype(f32) * (s[h : h + 1] / total[h : h + 1]) for p, s in zip(pair, shares)]
            pieces.append(both[0] + both[1])
    attended = jnp.concatenate(pieces, 0).T.astype(bf16)
    keep(rows, jnp.dot(attended, w_ref[...], preferred_element_type=f32))
    for r in range(out_ref.shape[0]):
        start = 8 * (r % 2) + r // 2
        out_ref[r] = every_nth(rows, start, 16).astype(bf16)


def finish(parts, w_out):
    shape = (parts.shape[2], w_out.shape[1])
    return pl.pallas_call(
        finish_kernel,
        out_shape=jax.ShapeDtypeStruct((16, 8, shape[1]), bf16),
        scratch_shapes=[pltpu.VMEM((shape[1] // 128, shape[0], 128), f32)],
        compiler_params=pltpu.CompilerParams(vmem_limit_bytes=48 * 2**20),
    )(parts, w_out)


def on_device(patches, norm_gain, w_qkv, pool_q, pool_kv, w_out):
    upper = passed_along(patches[-1:], ROW)
    left = passed_along(patches[:, -1:], COL)
    above_left = corner(patches[-1:, -1:])
    gain = norm_gain[None]
    own_q, own_kv = project_own(patches, gain, w_qkv)
    halo = (upper[0], left[:, 0], above_left[0])
    groups = lax.axis_size("zl")
    flat = pool_call(keyvals_kernel, own_kv, halo, gain, w_qkv, (1, 2), pool_kv, (groups, 32, 2 * WIDE))
    own = lax.all_to_all(flat, "zl", 0, 0, tiled=True).reshape(-1, 2 * WIDE)
    turned = pool_call(queries_kernel, own_q, halo, gain, w_qkv, (0,), pool_q, (2 * groups, WIDE, 128))
    every_query = lax.all_to_all(turned, ("za", "zl"), 0, 0, tiled=True)
    line = jnp.concatenate([own, shifted_x(own, 1), shifted_x(own, -1), shifted_x(own, 2)], 0)
    swap = lambda block: shifted(block, "core", 1)
    after, before = shifted(line, "y", 1), shifted(line, "y", -1)
    half = line.shape[0] // 2
    far = [shifted(after[:half], "y", 1), shifted(before[half:], "y", -1)]
    carry = attend(every_query, line, None, False)
    carry = attend(every_query, swap(line), carry, False)
    for block in (after, swap(after), before, swap(before)):
        carry = attend(every_query, block, carry, False)
    far = jnp.concatenate(far, 0)
    carry = attend(every_query, far, carry, False)
    partial = attend(every_query, swap(far), carry, True)
    parts = lax.all_to_all(partial, ("za", "zl"), 0, 0, tiled=True)
    return finish(parts, w_out)


def solution(mesh):
    fine = Mesh(mesh.devices.reshape(2, 4, 2, 2, 4, 2), AXES)
    tiles = P(ROW, COL, None)
    return jax.shard_map(
        on_device,
        mesh=fine,
        in_specs=(tiles, P(), P(), P(), P(), P()),
        out_specs=tiles,
        check_vma=False,
    )
```

```python
import functools
import math

import jax
import jax.numpy as jnp
from jax import lax
from jax.experimental import pallas as pl
from jax.experimental.pallas import tpu as pltpu
from jax.sharding import Mesh
from jax.sharding import PartitionSpec as P

AXES = ("zq", "zc", "xl", "xh", "y", "core")
ROW = ("zq", "zc", "xl")
COL = ("xh", "y", "core")
HEAD = 64
GROUP = 3
WIDE = GROUP * HEAD
SCALE = HEAD**-0.5 * math.log2(math.e)
STATS = 16
bf16, f32 = jnp.bfloat16, jnp.float32


def shifted(block, axis, distance):
    count = lax.axis_size(axis)
    return lax.ppermute(block, axis, [(i, (i + distance) % count) for i in range(count)])


def shifted_x(block, distance):
    place = lambda i: (i % 2) * 2 + i // 2
    route = [(place(i), place((i + distance) % 4)) for i in range(4)]
    return lax.ppermute(block, ("xl", "xh"), route)


def passed_along(block, axis):
    count = lax.axis_size(axis)
    return lax.ppermute(block, axis, [(i - 1, i) for i in range(1, count)])


def corner(block):
    rows, cols = lax.axis_size(ROW), lax.axis_size(COL)
    route = [((r - 1) * cols + c - 1, r * cols + c) for r in range(1, rows) for c in range(1, cols)]
    return lax.ppermute(block, AXES, route)


def normalised(values, gain):
    center = values - jnp.mean(values, axis=-1, keepdims=True)
    spread = jnp.mean(center * center, axis=-1, keepdims=True)
    return (center * lax.rsqrt(spread + 1e-06) * gain).astype(bf16)


def project(tokens, weights):
    return jnp.dot(tokens, weights, preferred_element_type=f32).astype(bf16)


ORDER = (0, 1, 3, 4, 5, 7, 8, 9, 11, 12, 13, 2, 6, 10, 14, 15)
KEY_COLUMNS = 11


def keep(plain, values):
    for k in range(plain.shape[0]):
        plain[k] = values[:, 128 * k : 128 * (k + 1)]


def every_nth(plain, start, step):
    picked = [plain[k, pl.ds(start, 8, stride=step), :] for k in range(plain.shape[0])]
    return jnp.concatenate(picked, 1)


def edge_kernel(right_ref, low_ref, column_ref, row_ref, corner_ref, plain):
    rows, cols, width = right_ref.shape
    keep(plain, right_ref[...].astype(f32).reshape(rows * cols, width))
    column = jnp.concatenate([every_nth(plain, 8 * r + cols - 1, 32) for r in range(4)], 0)
    column_ref[...] = column.astype(bf16)
    last = low_ref[0]
    row_ref[...] = last
    corner_ref[...] = last[-1:]


def edges(patches):
    rows, cols, width = patches.shape
    shapes = [(rows, width), (cols, width), (1, width)]
    return pl.pallas_call(
        edge_kernel,
        grid=(1,),
        in_specs=[
            pl.BlockSpec((rows, 8, width), lambda _: (0, cols // 8 - 1, 0)),
            pl.BlockSpec((1, cols, width), lambda _: (rows - 1, 0, 0)),
        ],
        out_specs=[whole(s) for s in shapes],
        out_shape=[jax.ShapeDtypeStruct(s, bf16) for s in shapes],
        scratch_shapes=[pltpu.VMEM((width // 128, 8 * rows, 128), f32)],
        compiler_params=pltpu.CompilerParams(vmem_limit_bytes=60 * 2**20),
        cost_estimate=pl.CostEstimate(flops=0, bytes_accessed=1_000_000, transcendentals=0),
    )(patches, patches)


def own_kernel(patches_ref, gain_ref, w_ref, q_ref, kv_ref, patches, weights, plain, tokens, sems):
    rows, cols, width = patches.shape
    copies = [
        pltpu.make_async_copy(patches_ref, patches, sems.at[0]),
        pltpu.make_async_copy(w_ref, weights, sems.at[1]),
    ]
    for copy in copies:
        copy.start()
    copies[0].wait()
    keep(plain, patches[...].astype(f32).reshape(rows * cols, width))
    gain = gain_ref[...]
    for place, c in enumerate(ORDER):
        parts = [every_nth(plain, 16 * r + c, 64) for r in range(4)]
        tokens[pl.ds(32 * place, 32), :] = normalised(jnp.concatenate(parts, 0), gain)
    few = tokens[: 32 * KEY_COLUMNS]
    copies[1].wait()
    kv_ref[...] = project(few, weights[:, width:])
    q_ref[...] = project(tokens[...], weights[:, :width])


def column_of_w(i):
    return pl.BlockSpec((768, 768), lambda _: (0, i))


def whole(shape):
    return pl.BlockSpec(shape, lambda _: (0,) * len(shape))


def project_own(patches, gain, w_qkv):
    rows, cols, width = patches.shape
    count = rows * cols
    shapes = [(count, width), (32 * KEY_COLUMNS, 2 * width)]
    return pl.pallas_call(
        own_kernel,
        grid=(1,),
        in_specs=[pl.BlockSpec(memory_space=pl.ANY), whole(gain.shape), pl.BlockSpec(memory_space=pl.ANY)],
        out_specs=[whole(s) for s in shapes],
        out_shape=[jax.ShapeDtypeStruct(s, bf16) for s in shapes],
        scratch_shapes=[
            pltpu.VMEM(patches.shape, bf16),
            pltpu.VMEM(w_qkv.shape, bf16),
            pltpu.VMEM((width // 128, count, 128), f32),
            pltpu.VMEM((count, width), bf16),
            pltpu.SemaphoreType.DMA((2,)),
        ],
        compiler_params=pltpu.CompilerParams(vmem_limit_bytes=60 * 2**20),
        cost_estimate=pl.CostEstimate(flops=3_000_000_000, bytes_accessed=6_000_000, transcendentals=0),
    )(patches, gain, w_qkv)


def halo_tokens(upper_ref, left_ref, corner_ref, gain_ref):
    every = [left_ref[...].astype(f32), upper_ref[...].astype(f32), corner_ref[...].astype(f32)]
    every.append(jnp.zeros((15, every[0].shape[1]), f32))
    return normalised(jnp.concatenate(every, 0), gain_ref[...])


def columns_of(own_ref, halo, columns):
    first = lax.broadcasted_iota(jnp.int32, (8, own_ref.shape[1]), 0) == 0
    groups = {}
    for c in columns:
        if c < 0:
            block, above = halo[0:32], halo[48:49]
        else:
            place = ORDER.index(c)
            block, above = own_ref[pl.ds(32 * place, 32), :].astype(f32), halo[32 + c : 33 + c]
        four = [block[8 * r : 8 * r + 8] for r in range(4)]
        groups[c] = [jnp.where(first, above, pltpu.roll(four[3], 1, 0))] + four
    return groups


def pooled(groups, taps, column, row):
    total = None
    for a in range(3):
        for b in range(3):
            term = taps[3 * a + b] * groups[column + b - 1][row + a]
            total = term if total is None else total + term
    return total


def keyvals_kernel(own_ref, upper_ref, left_ref, corner_ref, gain_ref, wk_ref, wv_ref, pool_ref, out_ref):
    tokens = halo_tokens(upper_ref, left_ref, corner_ref, gain_ref)
    width = wk_ref.shape[1]
    both = []
    for part, w_ref in enumerate((wk_ref, wv_ref)):
        cols = pl.ds(part * width, width)
        halo = project(tokens, w_ref[...]).astype(f32)
        taps = [pool_ref[t : t + 1, cols] for t in range(9)]
        groups = columns_of(own_ref.at[:, cols], halo, (-1,) + ORDER[:KEY_COLUMNS])
        both.append(jnp.concatenate([pooled(groups, taps, 4 * j, 0) for j in range(4)], 0))
    for g in range(out_ref.shape[0]):
        lanes = slice(g * WIDE, (g + 1) * WIDE)
        out_ref[g] = jnp.concatenate([p[:, lanes] for p in both], 1).astype(bf16)


def queries_kernel(own_ref, upper_ref, left_ref, corner_ref, gain_ref, w_ref, pool_ref, out_ref):
    tokens = halo_tokens(upper_ref, left_ref, corner_ref, gain_ref)
    halo = project(tokens, w_ref[...]).astype(f32)
    taps = [pool_ref[t : t + 1, :] for t in range(9)]
    groups = columns_of(own_ref, halo, range(-1, 16))
    rows = [pooled(groups, taps, 2 * j, 2 * p) for j in range(8) for p in range(2)]
    turned = jnp.concatenate(rows, 0).T.astype(bf16)
    count = out_ref.shape[0] // 2
    for g in range(count):
        block = turned[g * WIDE : (g + 1) * WIDE]
        out_ref[g] = block
        out_ref[count + g] = block


def pool_call(kernel, own, halo, gain, w_qkv, parts, taps, out_shape):
    return pl.pallas_call(
        kernel,
        grid=(1,),
        in_specs=[whole(a.shape) for a in (own, *halo, gain)]
        + [column_of_w(i) for i in parts]
        + [whole(taps.shape)],
        out_specs=whole(out_shape),
        out_shape=jax.ShapeDtypeStruct(out_shape, bf16),
        compiler_params=pltpu.CompilerParams(vmem_limit_bytes=24 * 2**20),
        cost_estimate=pl.CostEstimate(flops=200_000_000, bytes_accessed=4_000_000, transcendentals=0),
    )(own, *halo, gain, *([w_qkv] * len(parts)), taps)


def attend_kernel(first, last, block, qb, q_ref, kv_ref, *refs):
    if first:
        carry_in = None
    else:
        carry_in, refs = refs[:2], refs[2:]
    outs, (qz, stat, acc) = refs[:-3], refs[-3:]
    step = pl.program_id(0)
    tiles = q_ref.shape[0]
    count = tiles * 128

    @pl.when(step == 0)
    def _():
        zero = jnp.zeros((HEAD, count), bf16)
        q = jnp.concatenate([q_ref[t] for t in range(tiles)], axis=1)
        qz[0] = jnp.concatenate([q[:HEAD], zero], 0)
        qz[1] = jnp.concatenate([zero, q[HEAD : 2 * HEAD]], 0)
        qz[2] = jnp.concatenate([q[2 * HEAD :], zero], 0)
        if first:
            stat[0:8] = jnp.full((8, count), -1e30, f32)
            stat[8:16] = jnp.zeros((8, count), f32)
            acc[...] = jnp.zeros_like(acc)
        else:
            stat[...] = carry_in[0][...]
            acc[...] = carry_in[1][...]

    values = kv_ref[:, 128:384].T
    ones = jnp.ones((16, block), bf16)
    jobs = [(h, j) for j in range(count // qb) for h in range(GROUP)]

    def scores(h, j):
        keys = kv_ref[:, 0:128] if h < 2 else kv_ref[:, 128:256]
        return jnp.dot(keys, qz[h, :, j * qb : (j + 1) * qb], preferred_element_type=f32)

    ready = scores(*jobs[0])
    for place, (h, j) in enumerate(jobs):
        now = ready
        if place + 1 < len(jobs):
            ready = scores(*jobs[place + 1])
        lanes = slice(j * qb, (j + 1) * qb)
        old = stat[h : h + 1, lanes]
        new = jnp.maximum(old, jnp.max(now, axis=0, keepdims=True))
        factor = jnp.exp2((old - new) * SCALE)
        weights = jnp.exp2((now - new) * SCALE).astype(bf16)
        stat[h : h + 1, lanes] = new
        value = jnp.concatenate([values[HEAD * (h + 1) : HEAD * (h + 2)], ones], 0)
        part = jnp.dot(value, weights, preferred_element_type=f32)
        rows = slice(HEAD * h, HEAD * (h + 1))
        stat[8 + h : 9 + h, lanes] = stat[8 + h : 9 + h, lanes] * factor + part[HEAD : HEAD + 1]
        acc[rows, lanes] = acc[rows, lanes] * factor + part[:HEAD]

    @pl.when(step == pl.num_programs(0) - 1)
    def _():
        if not last:
            outs[0][...] = stat[...]
            outs[1][...] = acc[...]
            return
        total = stat[8:16]
        logs = stat[0:8] * SCALE + jnp.log2(jnp.maximum(total, 1e-30))
        high = logs.astype(bf16)
        left = logs - high.astype(f32)
        middle = left.astype(bf16)
        low = (left - middle.astype(f32)).astype(bf16)
        three = [a.astype(f32)[:GROUP] for a in (high, middle, low)]
        packed = jnp.concatenate(three + [jnp.zeros((STATS - 9, count), f32)], 0).astype(bf16)
        for t in range(tiles):
            lanes = slice(t * 128, (t + 1) * 128)
            for h in range(GROUP):
                rows = slice(HEAD * h, HEAD * (h + 1))
                outs[0][t, rows] = (acc[rows, lanes] / total[h : h + 1, lanes]).astype(bf16)
            outs[0][t, WIDE:] = packed[:, lanes]


def attend(queries, keyvals, carry, last, block=512, qb=512):
    tiles = queries.shape[0]
    count = tiles * 128
    keys = keyvals.shape[0]
    block = min(block, keys)
    carry_shapes = [(16, count), (WIDE, count)]
    carry_specs = [whole(s) for s in carry_shapes]
    if last:
        out_shape = jax.ShapeDtypeStruct((tiles, WIDE + STATS, 128), bf16)
        out_specs = whole(out_shape.shape)
    else:
        out_shape = [jax.ShapeDtypeStruct(s, f32) for s in carry_shapes]
        out_specs = carry_specs
    work = GROUP * count * keys
    return pl.pallas_call(
        functools.partial(attend_kernel, carry is None, last, block, qb),
        grid=(keys // block,),
        in_specs=[whole(queries.shape), pl.BlockSpec((block, 2 * WIDE), lambda i: (i, 0))]
        + ([] if carry is None else carry_specs),
        out_specs=out_specs,
        out_shape=out_shape,
        scratch_shapes=[
            pltpu.VMEM((GROUP, 128, count), bf16),
            pltpu.VMEM((16, count), f32),
            pltpu.VMEM((WIDE, count), f32),
        ],
        compiler_params=pltpu.CompilerParams(vmem_limit_bytes=24 * 2**20),
        cost_estimate=pl.CostEstimate(
            flops=work * 1024, bytes_accessed=keys * 768, transcendentals=work
        ),
    )(queries, keyvals, *(() if carry is None else carry))


def finish_kernel(parts_ref, w_ref, out_ref, rows):
    groups = parts_ref.shape[0] // 2
    pieces = []
    for g in range(groups):
        pair = [parts_ref[g], parts_ref[groups + g]]
        logs = []
        for p in pair:
            s = p[WIDE:].astype(f32)
            logs.append((s[0:3] + s[3:6]) + s[6:9])
        top = jnp.maximum(logs[0], logs[1])
        shares = [jnp.exp2(a - top) for a in logs]
        total = shares[0] + shares[1]
        for h in range(GROUP):
            head = slice(HEAD * h, HEAD * (h + 1))
            both = [p[head].astype(f32) * (s[h : h + 1] / total[h : h + 1]) for p, s in zip(pair, shares)]
            pieces.append(both[0] + both[1])
    attended = jnp.concatenate(pieces, 0).T.astype(bf16)
    keep(rows, jnp.dot(attended, w_ref[...], preferred_element_type=f32))
    for r in range(out_ref.shape[0]):
        start = 8 * (r % 2) + r // 2
        out_ref[r] = every_nth(rows, start, 16).astype(bf16)


def finish(parts, w_out):
    shape = (parts.shape[2], w_out.shape[1])
    return pl.pallas_call(
        finish_kernel,
        out_shape=jax.ShapeDtypeStruct((16, 8, shape[1]), bf16),
        scratch_shapes=[pltpu.VMEM((shape[1] // 128, shape[0], 128), f32)],
        compiler_params=pltpu.CompilerParams(vmem_limit_bytes=24 * 2**20),
    )(parts, w_out)


def on_device(patches, norm_gain, w_qkv, pool_q, pool_kv, w_out):
    last_column, last_row, last_token = edges(patches)
    halo = (passed_along(last_row, ROW), passed_along(last_column, COL), corner(last_token))
    gain = norm_gain[None]
    own_q, own_kv = project_own(patches, gain, w_qkv)
    groups = lax.axis_size("y")
    flat = pool_call(keyvals_kernel, own_kv, halo, gain, w_qkv, (1, 2), pool_kv, (groups, 32, 2 * WIDE))
    own = lax.all_to_all(flat, "y", 0, 0, tiled=True).reshape(-1, 2 * WIDE)
    own, own_q = lax.optimization_barrier((own, own_q))
    line = [own, shifted(own, "zq", 2), shifted(own, "zq", 1), shifted(own, "zq", -1)]
    turned = pool_call(queries_kernel, own_q, halo, gain, w_qkv, (0,), pool_q, (2 * groups, WIDE, 128))
    every_query = lax.all_to_all(turned, ("zc", "y"), 0, 0, tiled=True)
    line = jnp.concatenate(line, 0)
    swap = lambda block: shifted(block, "core", 1)
    after, before = shifted_x(line, 1), shifted_x(line, -1)
    carry = attend(every_query, line, None, False)
    carry = attend(every_query, swap(line), carry, False)
    after, before, carry = lax.optimization_barrier((after, before, carry))
    half = line.shape[0] // 2
    far = [shifted_x(after[:half], 1), shifted_x(before[half:], -1)]
    for block in (after, swap(after), before, swap(before)):
        carry = attend(every_query, block, carry, False)
    far, carry = lax.optimization_barrier((far, carry))
    far = jnp.concatenate(far, 0)
    carry = attend(every_query, far, carry, False)
    partial = attend(every_query, swap(far), carry, True)
    parts = lax.all_to_all(partial, ("zc", "y"), 0, 0, tiled=True)
    return finish(parts, w_out)


def solution(mesh):
    fine = Mesh(mesh.devices.reshape(4, 2, 2, 2, 4, 2), AXES)
    tiles = P(ROW, COL, None)
    return jax.shard_map(
        on_device,
        mesh=fine,
        in_specs=(tiles, P(), P(), P(), P(), P()),
        out_specs=tiles,
        check_vma=False,
    )
```

```python
import functools
import math

import jax
import jax.numpy as jnp
from jax import lax
from jax.experimental import pallas as pl
from jax.experimental.pallas import tpu as pltpu
from jax.sharding import Mesh
from jax.sharding import PartitionSpec as P

AXES = ("zq", "zc", "xl", "xh", "y", "core")
ROW = ("zq", "zc", "xl")
COL = ("xh", "y", "core")
HEAD = 64
GROUP = 3
WIDE = GROUP * HEAD
SCALE = HEAD**-0.5 * math.log2(math.e)
STATS = 16
bf16, f32 = jnp.bfloat16, jnp.float32


def shifted(block, axis, distance):
    count = lax.axis_size(axis)
    return lax.ppermute(block, axis, [(i, (i + distance) % count) for i in range(count)])


def shifted_x(block, distance):
    place = lambda i: (i % 2) * 2 + i // 2
    route = [(place(i), place((i + distance) % 4)) for i in range(4)]
    return lax.ppermute(block, ("xl", "xh"), route)


def passed_along(block, axis):
    count = lax.axis_size(axis)
    return lax.ppermute(block, axis, [(i - 1, i) for i in range(1, count)])


def corner(block):
    rows, cols = lax.axis_size(ROW), lax.axis_size(COL)
    route = [((r - 1) * cols + c - 1, r * cols + c) for r in range(1, rows) for c in range(1, cols)]
    return lax.ppermute(block, AXES, route)


def normalised(values, gain):
    center = values - jnp.mean(values, axis=-1, keepdims=True)
    spread = jnp.mean(center * center, axis=-1, keepdims=True)
    return center * lax.rsqrt(spread + 1e-06) * gain


def project(tokens, weights):
    return jnp.dot(tokens, weights, preferred_element_type=f32).astype(bf16)


ORDER = (0, 1, 3, 4, 5, 7, 8, 9, 11, 12, 13, 2, 6, 10, 14, 15)
KEY_COLUMNS = 11


def keep(plain, values):
    for k in range(plain.shape[0]):
        plain[k] = values[:, 128 * k : 128 * (k + 1)]


def every_nth(plain, start, step):
    picked = [plain[k, pl.ds(start, 8, stride=step), :] for k in range(plain.shape[0])]
    return jnp.concatenate(picked, 1)


def tokens_kernel(patches_ref, gain_ref, tokens_ref, column_ref, row_ref, corner_ref, plain):
    rows, cols, width = patches_ref.shape
    keep(plain, patches_ref[...].astype(f32).reshape(rows * cols, width))
    gain = gain_ref[...]
    last = [None] * cols
    for place, c in enumerate(ORDER):
        parts = [every_nth(plain, cols * r + c, 4 * cols) for r in range(4)]
        column = normalised(jnp.concatenate(parts, 0), gain)
        tokens_ref[pl.ds(32 * place, 32), :] = column.astype(bf16)
        last[c] = column[31:]
    column_ref[...] = column.astype(bf16)
    row_ref[...] = jnp.concatenate(last, 0).astype(bf16)
    corner_ref[...] = last[-1].astype(bf16)


def whole(shape):
    return pl.BlockSpec(shape, lambda *_: (0,) * len(shape))


def normalised_tokens(patches, gain):
    rows, cols, width = patches.shape
    shapes = [(rows * cols, width), (rows, width), (cols, width), (1, width)]
    return pl.pallas_call(
        tokens_kernel,
        in_specs=[pl.BlockSpec(memory_space=pltpu.VMEM)] * 2,
        out_specs=[pl.BlockSpec(memory_space=pltpu.VMEM)] * 4,
        out_shape=[jax.ShapeDtypeStruct(s, bf16) for s in shapes],
        scratch_shapes=[pltpu.VMEM((width // 128, rows * cols, 128), f32)],
        compiler_params=pltpu.CompilerParams(vmem_limit_bytes=16 * 2**20),
        cost_estimate=pl.CostEstimate(flops=4_000_000_000, bytes_accessed=1_000_000, transcendentals=0),
    )(patches, gain)


def halo_tokens(upper_ref, left_ref, corner_ref):
    rest = jnp.zeros((15, left_ref.shape[1]), f32)
    every = [left_ref[...].astype(f32), upper_ref[...].astype(f32), corner_ref[...].astype(f32), rest]
    return jnp.concatenate(every, 0).astype(bf16)


def columns_of(own, halo, columns):
    first = lax.broadcasted_iota(jnp.int32, (8, own.shape[1]), 0) == 0
    groups = {}
    for c in columns:
        if c < 0:
            block, above = halo[0:32], halo[48:49]
        else:
            place = ORDER.index(c)
            block, above = own[32 * place : 32 * place + 32].astype(f32), halo[32 + c : 33 + c]
        four = [block[8 * r : 8 * r + 8] for r in range(4)]
        groups[c] = [jnp.where(first, above, pltpu.roll(four[3], 1, 0))] + four
    return groups


def pooled(groups, taps, column, row):
    total = None
    for a in range(3):
        for b in range(3):
            term = taps[3 * a + b] * groups[column + b - 1][row + a]
            total = term if total is None else total + term
    return total


def keyvals_kernel(tokens_ref, upper_ref, left_ref, corner_ref, w_ref, pool_ref, out_ref):
    halo_in = halo_tokens(upper_ref, left_ref, corner_ref)
    width = tokens_ref.shape[1]
    both = []
    for part in range(2):
        cols = pl.ds(part * width, width)
        weights = w_ref[:, (part + 1) * width : (part + 2) * width]
        halo = project(halo_in, weights).astype(f32)
        own = project(tokens_ref[: 32 * KEY_COLUMNS], weights)
        taps = [pool_ref[t : t + 1, cols] for t in range(9)]
        groups = columns_of(own, halo, (-1,) + ORDER[:KEY_COLUMNS])
        both.append(jnp.concatenate([pooled(groups, taps, 4 * j, 0) for j in range(4)], 0))
    count = width // WIDE
    for g in range(count):
        lanes = slice(g * WIDE, (g + 1) * WIDE)
        block = jnp.concatenate([p[:, lanes] for p in both], 1).astype(bf16)
        for copy in range(out_ref.shape[0] // count):
            out_ref[copy * count + g] = block


def queries_kernel(tokens_ref, upper_ref, left_ref, corner_ref, w_ref, pool_ref, out_ref):
    width = tokens_ref.shape[1]
    weights = w_ref[:, :width]
    halo = project(halo_tokens(upper_ref, left_ref, corner_ref), weights).astype(f32)
    own = project(tokens_ref[...], weights)
    taps = [pool_ref[t : t + 1, :] for t in range(9)]
    groups = columns_of(own, halo, range(-1, 16))
    rows = [pooled(groups, taps, 2 * j, 2 * p) for j in range(8) for p in range(2)]
    turned = jnp.concatenate(rows, 0).T.astype(bf16)
    count = width // WIDE
    for g in range(count):
        block = turned[g * WIDE : (g + 1) * WIDE]
        for copy in range(out_ref.shape[0] // count):
            out_ref[copy * count + g] = block


def pool_call(kernel, tokens, halo, w_qkv, taps, out_shape):
    return pl.pallas_call(
        kernel,
        in_specs=[pl.BlockSpec(memory_space=pltpu.VMEM)] * (3 + len(halo)),
        out_specs=pl.BlockSpec(memory_space=pltpu.VMEM),
        out_shape=jax.ShapeDtypeStruct(out_shape, bf16),
        compiler_params=pltpu.CompilerParams(vmem_limit_bytes=24 * 2**20),
        cost_estimate=pl.CostEstimate(flops=1_500_000_000, bytes_accessed=4_000_000, transcendentals=0),
    )(tokens, *halo, w_qkv, taps)


def attend_kernel(first, last, block, qb, q_ref, kv_ref, *refs):
    if first:
        stat_in, acc_in = None, None
    else:
        stat_in, acc_in, *refs = refs
    if last:
        out_ref, qz, stat, acc = refs
    else:
        stat, acc, qz = refs
    tiles = q_ref.shape[0]
    count = tiles * 128
    zero = jnp.zeros((HEAD, 128), bf16)
    for t in range(tiles):
        lanes = slice(t * 128, (t + 1) * 128)
        for h in range(GROUP):
            here = HEAD * (h % 2)
            qz[h, here : here + HEAD, lanes] = q_ref[t, HEAD * h : HEAD * (h + 1)]
            qz[h, HEAD - here : 2 * HEAD - here, lanes] = zero

    jobs = [
        (k, j, h)
        for k in range(kv_ref.shape[0] // block)
        for j in range(count // qb)
        for h in range(GROUP)
    ]
    ones = jnp.ones((16, block), bf16)
    values = [kv_ref[pl.ds(k * block, block), 128:384].T for k in range(kv_ref.shape[0] // block)]

    def scores(k, j, h):
        keys = kv_ref[pl.ds(k * block, block), 128 * (h // 2) : 128 * (h // 2) + 128]
        return jnp.dot(keys, qz[h, :, j * qb : (j + 1) * qb], preferred_element_type=f32)

    ready = scores(*jobs[0])
    for place, (k, j, h) in enumerate(jobs):
        now = ready
        if place + 1 < len(jobs):
            ready = scores(*jobs[place + 1])
        lanes = slice(j * qb, (j + 1) * qb)
        rows = slice(HEAD * h, HEAD * (h + 1))
        new = jnp.max(now, axis=0, keepdims=True)
        source = (stat_in, acc_in) if k == 0 else (stat, acc)
        carried = k > 0 or not first
        if carried:
            old = source[0][h : h + 1, lanes]
            new = jnp.maximum(old, new)
        weights = jnp.exp2((now - new) * SCALE).astype(bf16)
        value = jnp.concatenate([values[k][HEAD * (h + 1) : HEAD * (h + 2)], ones], 0)
        part = jnp.dot(value, weights, preferred_element_type=f32)
        total, numer = part[HEAD : HEAD + 1], part[:HEAD]
        if carried:
            factor = jnp.exp2((old - new) * SCALE)
            total = source[0][8 + h : 9 + h, lanes] * factor + total
            numer = source[1][rows, lanes] * factor + numer
        stat[h : h + 1, lanes] = new
        stat[8 + h : 9 + h, lanes] = total
        acc[rows, lanes] = numer

    if last:
        total = stat[8 : 8 + GROUP]
        logs = stat[0:GROUP] * SCALE + jnp.log2(total)
        high = logs.astype(bf16)
        left = logs - high.astype(f32)
        middle = left.astype(bf16)
        low = left - middle.astype(f32)
        three = [high.astype(f32), middle.astype(f32), low]
        packed = jnp.concatenate(three + [jnp.zeros((STATS - 9, count), f32)], 0).astype(bf16)
        for t in range(tiles):
            lanes = slice(t * 128, (t + 1) * 128)
            for h in range(GROUP):
                rows = slice(HEAD * h, HEAD * (h + 1))
                out_ref[t, rows] = (acc[rows, lanes] / total[h : h + 1, lanes]).astype(bf16)
            out_ref[t, WIDE:] = packed[:, lanes]


def attend(queries, keyvals, carry, last, block=512, qb=512):
    tiles = queries.shape[0]
    count = tiles * 128
    keys = keyvals.shape[0]
    carry_shapes = [(16, count), (WIDE, count)]
    if last:
        out_shape = [jax.ShapeDtypeStruct((tiles, WIDE + STATS, 128), bf16)]
        scratch = [pltpu.VMEM(s, f32) for s in carry_shapes]
    else:
        out_shape = [jax.ShapeDtypeStruct(s, f32) for s in carry_shapes]
        scratch = []
    carry = [] if carry is None else carry
    work = GROUP * count * keys
    outs = pl.pallas_call(
        functools.partial(attend_kernel, not carry, last, min(block, keys), qb),
        in_specs=[pl.BlockSpec(memory_space=pltpu.VMEM)] * (2 + len(carry)),
        out_specs=[pl.BlockSpec(memory_space=pltpu.VMEM)] * len(out_shape),
        out_shape=out_shape,
        input_output_aliases={} if last or not carry else {2: 0, 3: 1},
        scratch_shapes=[pltpu.VMEM((GROUP, 128, count), bf16)] + scratch,
        compiler_params=pltpu.CompilerParams(vmem_limit_bytes=24 * 2**20),
        cost_estimate=pl.CostEstimate(
            flops=work * 1024, bytes_accessed=keys * 768, transcendentals=work
        ),
    )(queries, keyvals, *carry)
    return outs[0] if last else outs


def finish_kernel(parts_ref, w_ref, out_ref, rows):
    groups = parts_ref.shape[0] // 2
    pieces = []
    for g in range(groups):
        pair = [parts_ref[g], parts_ref[groups + g]]
        logs = []
        for p in pair:
            s = p[WIDE:].astype(f32)
            logs.append((s[0:3] + s[3:6]) + s[6:9])
        top = jnp.maximum(logs[0], logs[1])
        shares = [jnp.exp2(a - top) for a in logs]
        total = shares[0] + shares[1]
        for h in range(GROUP):
            head = slice(HEAD * h, HEAD * (h + 1))
            both = [p[head].astype(f32) * (s[h : h + 1] / total[h : h + 1]) for p, s in zip(pair, shares)]
            pieces.append(both[0] + both[1])
    attended = jnp.concatenate(pieces, 0).T.astype(bf16)
    keep(rows, jnp.dot(attended, w_ref[...], preferred_element_type=f32))
    for r in range(out_ref.shape[0]):
        start = 8 * (r % 2) + r // 2
        out_ref[r] = every_nth(rows, start, 16).astype(bf16)


def finish(parts, w_out):
    shape = (parts.shape[2], w_out.shape[1])
    return pl.pallas_call(
        finish_kernel,
        out_shape=jax.ShapeDtypeStruct((16, 8, shape[1]), bf16),
        scratch_shapes=[pltpu.VMEM((shape[1] // 128, shape[0], 128), f32)],
        compiler_params=pltpu.CompilerParams(vmem_limit_bytes=24 * 2**20),
    )(parts, w_out)


def on_device(patches, norm_gain, w_qkv, pool_q, pool_kv, w_out):
    gain = norm_gain[None]
    tokens, last_column, last_row, last_token = normalised_tokens(patches, gain)
    halo = (passed_along(last_row, ROW), passed_along(last_column, COL), corner(last_token))
    groups = lax.axis_size("y")
    copies = lax.axis_size("zq")
    flat = pool_call(keyvals_kernel, tokens, halo, w_qkv, pool_kv, (copies * groups, 32, 2 * WIDE))
    line = lax.all_to_all(flat, ("zq", "y"), 0, 0, tiled=True).reshape(-1, 2 * WIDE)
    turned = pool_call(queries_kernel, tokens, halo, w_qkv, pool_q, (2 * groups, WIDE, 128))
    swap = lambda block: shifted(block, "core", 1)
    swapped, after, before = swap(line), shifted_x(line, 1), shifted_x(line, -1)
    swapped, turned = lax.optimization_barrier((swapped, turned))
    every_query = lax.all_to_all(turned, ("zc", "y"), 0, 0, tiled=True)
    carry = attend(every_query, line, None, False)
    carry = attend(every_query, swapped, carry, False)
    after, before, carry = lax.optimization_barrier((after, before, carry))
    half = line.shape[0] // 2
    far = [shifted_x(after[:half], 1), shifted_x(before[half:], -1)]
    for block in (after, swap(after), before, swap(before)):
        carry = attend(every_query, block, carry, False)
    far, carry = lax.optimization_barrier((far, carry))
    far = jnp.concatenate(far, 0)
    carry = attend(every_query, far, carry, False)
    partial = attend(every_query, swap(far), carry, True)
    parts = lax.all_to_all(partial, ("zc", "y"), 0, 0, tiled=True)
    return finish(parts, w_out)


def solution(mesh):
    fine = Mesh(mesh.devices.reshape(4, 2, 2, 2, 4, 2), AXES)
    tiles = P(ROW, COL, None)
    return jax.shard_map(
        on_device,
        mesh=fine,
        in_specs=(tiles, P(), P(), P(), P(), P()),
        out_specs=tiles,
        check_vma=False,
    )
```

```python
import functools
import math

import jax
import jax.numpy as jnp
from jax import lax
from jax.experimental import pallas as pl
from jax.experimental.pallas import tpu as pltpu
from jax.sharding import Mesh
from jax.sharding import PartitionSpec as P

AXES = ("zq", "zc", "xl", "xh", "y", "core")
ROW = ("zq", "zc", "xl")
COL = ("xh", "y", "core")
HEAD = 64
GROUP = 3
WIDE = GROUP * HEAD
SCALE = HEAD**-0.5 * math.log2(math.e)
STATS = 16
bf16, f32 = jnp.bfloat16, jnp.float32


def shifted(block, axis, distance):
    count = lax.axis_size(axis)
    return lax.ppermute(block, axis, [(i, (i + distance) % count) for i in range(count)])


def shifted_x(block, distance):
    place = lambda i: (i % 2) * 2 + i // 2
    route = [(place(i), place((i + distance) % 4)) for i in range(4)]
    return lax.ppermute(block, ("xl", "xh"), route)


def passed_along(block, axis):
    count = lax.axis_size(axis)
    return lax.ppermute(block, axis, [(i - 1, i) for i in range(1, count)])


def corner(block):
    rows, cols = lax.axis_size(ROW), lax.axis_size(COL)
    route = [((r - 1) * cols + c - 1, r * cols + c) for r in range(1, rows) for c in range(1, cols)]
    return lax.ppermute(block, AXES, route)


def normalised(values, gain):
    center = values - jnp.mean(values, axis=-1, keepdims=True)
    spread = jnp.mean(center * center, axis=-1, keepdims=True)
    return center * lax.rsqrt(spread + 1e-06) * gain


def project(tokens, weights):
    return jnp.dot(tokens, weights, preferred_element_type=f32).astype(bf16)


ORDER = (0, 1, 3, 4, 5, 7, 8, 9, 11, 12, 13, 2, 6, 10, 14, 15)
KEY_COLUMNS = 11


def keep(plain, values):
    for k in range(plain.shape[0]):
        plain[k] = values[:, 128 * k : 128 * (k + 1)]


def every_nth(plain, start, step):
    picked = [plain[k, pl.ds(start, 8, stride=step), :] for k in range(plain.shape[0])]
    return jnp.concatenate(picked, 1)


def tokens_kernel(patches_ref, gain_ref, tokens_ref, column_ref, row_ref, corner_ref, plain):
    rows, cols, width = patches_ref.shape
    keep(plain, patches_ref[...].astype(f32).reshape(rows * cols, width))
    gain = gain_ref[...]
    last = [None] * cols
    for place, c in enumerate(ORDER):
        parts = [every_nth(plain, cols * r + c, 4 * cols) for r in range(4)]
        column = normalised(jnp.concatenate(parts, 0), gain)
        tokens_ref[pl.ds(32 * place, 32), :] = column.astype(bf16)
        last[c] = column[31:]
    column_ref[...] = column.astype(bf16)
    row_ref[...] = jnp.concatenate(last, 0).astype(bf16)
    corner_ref[...] = last[-1].astype(bf16)


def whole(shape):
    return pl.BlockSpec(shape, lambda *_: (0,) * len(shape))


def normalised_tokens(patches, gain):
    rows, cols, width = patches.shape
    shapes = [(rows * cols, width), (rows, width), (cols, width), (1, width)]
    return pl.pallas_call(
        tokens_kernel,
        in_specs=[pl.BlockSpec(memory_space=pltpu.VMEM)] * 2,
        out_specs=[pl.BlockSpec(memory_space=pltpu.VMEM)] * 4,
        out_shape=[jax.ShapeDtypeStruct(s, bf16) for s in shapes],
        scratch_shapes=[pltpu.VMEM((width // 128, rows * cols, 128), f32)],
        compiler_params=pltpu.CompilerParams(vmem_limit_bytes=16 * 2**20),
        cost_estimate=pl.CostEstimate(flops=4_000_000_000, bytes_accessed=1_000_000, transcendentals=0),
    )(patches, gain)


def halo_tokens(upper_ref, left_ref, corner_ref):
    rest = jnp.zeros((15, left_ref.shape[1]), f32)
    every = [left_ref[...].astype(f32), upper_ref[...].astype(f32), corner_ref[...].astype(f32), rest]
    return jnp.concatenate(every, 0).astype(bf16)


def columns_of(own, halo, columns):
    first = lax.broadcasted_iota(jnp.int32, (8, own.shape[1]), 0) == 0
    groups = {}
    for c in columns:
        if c < 0:
            block, above = halo[0:32], halo[48:49]
        else:
            place = ORDER.index(c)
            block, above = own[32 * place : 32 * place + 32].astype(f32), halo[32 + c : 33 + c]
        four = [block[8 * r : 8 * r + 8] for r in range(4)]
        groups[c] = [jnp.where(first, above, pltpu.roll(four[3], 1, 0))] + four
    return groups


def pooled(groups, taps, column, row):
    total = None
    for a in range(3):
        for b in range(3):
            term = taps[3 * a + b] * groups[column + b - 1][row + a]
            total = term if total is None else total + term
    return total


def keyvals_kernel(tokens_ref, upper_ref, left_ref, corner_ref, w_ref, pool_ref, out_ref):
    halo_in = halo_tokens(upper_ref, left_ref, corner_ref)
    width = tokens_ref.shape[1]
    both = []
    for part in range(2):
        cols = pl.ds(part * width, width)
        weights = w_ref[:, (part + 1) * width : (part + 2) * width]
        halo = project(halo_in, weights).astype(f32)
        own = project(tokens_ref[: 32 * KEY_COLUMNS], weights)
        taps = [pool_ref[t : t + 1, cols] for t in range(9)]
        groups = columns_of(own, halo, (-1,) + ORDER[:KEY_COLUMNS])
        both.append(jnp.concatenate([pooled(groups, taps, 4 * j, 0) for j in range(4)], 0))
    count = width // WIDE
    for g in range(count):
        lanes = slice(g * WIDE, (g + 1) * WIDE)
        block = jnp.concatenate([p[:, lanes] for p in both], 1).astype(bf16)
        for copy in range(out_ref.shape[0] // count):
            out_ref[copy * count + g] = block


def queries_kernel(tokens_ref, upper_ref, left_ref, corner_ref, w_ref, pool_ref, out_ref):
    width = tokens_ref.shape[1]
    weights = w_ref[:, :width]
    halo = project(halo_tokens(upper_ref, left_ref, corner_ref), weights).astype(f32)
    own = project(tokens_ref[...], weights)
    taps = [pool_ref[t : t + 1, :] for t in range(9)]
    groups = columns_of(own, halo, range(-1, 16))
    rows = [pooled(groups, taps, 2 * j, 2 * p) for j in range(8) for p in range(2)]
    turned = jnp.concatenate(rows, 0).T.astype(bf16)
    count = width // WIDE
    for g in range(count):
        block = turned[g * WIDE : (g + 1) * WIDE]
        for copy in range(out_ref.shape[0] // count):
            out_ref[copy * count + g] = block


def pool_call(kernel, tokens, halo, w_qkv, taps, out_shape):
    return pl.pallas_call(
        kernel,
        in_specs=[pl.BlockSpec(memory_space=pltpu.VMEM)] * (3 + len(halo)),
        out_specs=pl.BlockSpec(memory_space=pltpu.VMEM),
        out_shape=jax.ShapeDtypeStruct(out_shape, bf16),
        compiler_params=pltpu.CompilerParams(vmem_limit_bytes=24 * 2**20),
        cost_estimate=pl.CostEstimate(flops=1_500_000_000, bytes_accessed=4_000_000, transcendentals=0),
    )(tokens, *halo, w_qkv, taps)


def attend_kernel(first, last, keep_block, qb, blocks, q_ref, *refs):
    block_refs, refs = refs[:blocks], refs[blocks:]
    if first:
        stat_in, acc_in = None, None
    else:
        stat_in, acc_in, *refs = refs
    if last:
        out_ref, qz, stat, acc = refs
    elif keep_block:
        stat, acc, block_ref, qz = refs
    else:
        stat, acc, qz = refs
    tiles = q_ref.shape[0]
    count = tiles * 128
    zero = jnp.zeros((HEAD, 128), bf16)
    for t in range(tiles):
        lanes = slice(t * 128, (t + 1) * 128)
        for h in range(GROUP):
            here = HEAD * (h % 2)
            qz[h, here : here + HEAD, lanes] = q_ref[t, HEAD * h : HEAD * (h + 1)]
            qz[h, HEAD - here : 2 * HEAD - here, lanes] = zero

    jobs = [(j, h) for j in range(count // qb) for h in range(GROUP)]
    block = jnp.concatenate([r[...] for r in block_refs], 0)
    if keep_block:
        block_ref[...] = block
    values = block[:, 128:].T
    ones = jnp.ones((16, block.shape[0]), bf16)

    def scores(j, h):
        keys = block[:, 128 * (h // 2) : 128 * (h // 2) + 128]
        return jnp.dot(keys, qz[h, :, j * qb : (j + 1) * qb], preferred_element_type=f32)

    ready = scores(*jobs[0])
    for place, (j, h) in enumerate(jobs):
        now = ready
        if place + 1 < len(jobs):
            ready = scores(*jobs[place + 1])
        lanes = slice(j * qb, (j + 1) * qb)
        rows = slice(HEAD * h, HEAD * (h + 1))
        new = jnp.max(now, axis=0, keepdims=True)
        if not first:
            old = stat_in[h : h + 1, lanes]
            new = jnp.maximum(old, new)
        weights = jnp.exp2((now - new) * SCALE).astype(bf16)
        value = jnp.concatenate([values[HEAD * (h + 1) : HEAD * (h + 2)], ones], 0)
        part = jnp.dot(value, weights, preferred_element_type=f32)
        total, numer = part[HEAD : HEAD + 1], part[:HEAD]
        if not first:
            factor = jnp.exp2((old - new) * SCALE)
            total = stat_in[8 + h : 9 + h, lanes] * factor + total
            numer = acc_in[rows, lanes] * factor + numer
        stat[h : h + 1, lanes] = new
        stat[8 + h : 9 + h, lanes] = total
        acc[rows, lanes] = numer

    if last:
        total = stat[8 : 8 + GROUP]
        logs = stat[0:GROUP] * SCALE + jnp.log2(total)
        high = logs.astype(bf16)
        left = logs - high.astype(f32)
        middle = left.astype(bf16)
        low = left - middle.astype(f32)
        three = [high.astype(f32), middle.astype(f32), low]
        packed = jnp.concatenate(three + [jnp.zeros((STATS - 9, count), f32)], 0).astype(bf16)
        for t in range(tiles):
            lanes = slice(t * 128, (t + 1) * 128)
            for h in range(GROUP):
                rows = slice(HEAD * h, HEAD * (h + 1))
                out_ref[t, rows] = (acc[rows, lanes] / total[h : h + 1, lanes]).astype(bf16)
            out_ref[t, WIDE:] = packed[:, lanes]


def attend(queries, blocks, carry, last=False, keep_block=False, qb=512):
    tiles = queries.shape[0]
    count = tiles * 128
    keys = sum(b.shape[0] for b in blocks)
    carry_shapes = [(16, count), (WIDE, count)]
    if last:
        out_shape = [jax.ShapeDtypeStruct((tiles, WIDE + STATS, 128), bf16)]
        scratch = [pltpu.VMEM(s, f32) for s in carry_shapes]
    else:
        out_shape = [jax.ShapeDtypeStruct(s, f32) for s in carry_shapes]
        scratch = []
        if keep_block:
            out_shape.append(jax.ShapeDtypeStruct((keys, 2 * WIDE), bf16))
    carry = [] if carry is None else carry
    work = GROUP * count * keys
    outs = pl.pallas_call(
        functools.partial(attend_kernel, not carry, last, keep_block, qb, len(blocks)),
        in_specs=[pl.BlockSpec(memory_space=pltpu.VMEM)] * (1 + len(blocks) + len(carry)),
        out_specs=[pl.BlockSpec(memory_space=pltpu.VMEM)] * len(out_shape),
        out_shape=out_shape,
        input_output_aliases={} if last or not carry else {1 + len(blocks): 0, 2 + len(blocks): 1},
        scratch_shapes=[pltpu.VMEM((GROUP, 128, count), bf16)] + scratch,
        compiler_params=pltpu.CompilerParams(vmem_limit_bytes=24 * 2**20),
        cost_estimate=pl.CostEstimate(
            flops=work * 1, bytes_accessed=1024, transcendentals=0
        ),
    )(queries, *blocks, *carry)
    return outs[0] if last else (outs[:2], *outs[2:])


def finish_kernel(parts_ref, w_ref, out_ref, rows):
    groups = parts_ref.shape[0] // 2
    pieces = []
    for g in range(groups):
        pair = [parts_ref[g], parts_ref[groups + g]]
        logs = []
        for p in pair:
            s = p[WIDE:].astype(f32)
            logs.append((s[0:3] + s[3:6]) + s[6:9])
        top = jnp.maximum(logs[0], logs[1])
        shares = [jnp.exp2(a - top) for a in logs]
        total = shares[0] + shares[1]
        for h in range(GROUP):
            head = slice(HEAD * h, HEAD * (h + 1))
            both = [p[head].astype(f32) * (s[h : h + 1] / total[h : h + 1]) for p, s in zip(pair, shares)]
            pieces.append(both[0] + both[1])
    attended = jnp.concatenate(pieces, 0).T.astype(bf16)
    keep(rows, jnp.dot(attended, w_ref[...], preferred_element_type=f32))
    for r in range(out_ref.shape[0]):
        start = 8 * (r % 2) + r // 2
        out_ref[r] = every_nth(rows, start, 16).astype(bf16)


def finish(parts, w_out):
    shape = (parts.shape[2], w_out.shape[1])
    return pl.pallas_call(
        finish_kernel,
        out_shape=jax.ShapeDtypeStruct((16, 8, shape[1]), bf16),
        scratch_shapes=[pltpu.VMEM((shape[1] // 128, shape[0], 128), f32)],
        compiler_params=pltpu.CompilerParams(vmem_limit_bytes=24 * 2**20),
    )(parts, w_out)


def on_device(patches, norm_gain, w_qkv, pool_q, pool_kv, w_out):
    gain = norm_gain[None]
    tokens, last_column, last_row, last_token = normalised_tokens(patches, gain)
    halo = (passed_along(last_row, ROW), passed_along(last_column, COL), corner(last_token))
    groups = lax.axis_size("y")
    flat = pool_call(keyvals_kernel, tokens, halo, w_qkv, pool_kv, (groups, 32, 2 * WIDE))
    own = lax.all_to_all(flat, "y", 0, 0, tiled=True).reshape(-1, 2 * WIDE)
    tie = lax.optimization_barrier
    own, tokens = tie((own, tokens))
    line = [own, shifted(own, "zq", 2), shifted(own, "zq", 1), shifted(own, "zq", -1)]
    turned = pool_call(queries_kernel, tokens, halo, w_qkv, pool_q, (2 * groups, WIDE, 128))
    every_query = lax.all_to_all(turned, ("zc", "y"), 0, 0, tiled=True)
    line = jnp.concatenate(line, 0)
    after, before = shifted_x(line, 1), shifted_x(line, -1)
    swap = lambda block: shifted(block, "core", 1)
    (carry,) = attend(every_query, [line], None)
    (carry,) = attend(every_query, [swap(line)], carry)
    after, before, carry = tie((after, before, carry))
    half = line.shape[0] // 2
    far = [shifted_x(after[:half], 1), shifted_x(before[half:], -1)]
    for block in (after, swap(after), before, swap(before)):
        (carry,) = attend(every_query, [block], carry)
    far, carry = tie((far, carry))
    swapped = [swap(block) for block in far]
    (carry,) = attend(every_query, far, carry)
    partial = attend(every_query, swapped, carry, last=True)
    parts = lax.all_to_all(partial, ("zc", "y"), 0, 0, tiled=True)
    return finish(parts, w_out)


def solution(mesh):
    fine = Mesh(mesh.devices.reshape(4, 2, 2, 2, 4, 2), AXES)
    tiles = P(ROW, COL, None)
    return jax.shard_map(
        on_device,
        mesh=fine,
        in_specs=(tiles, P(), P(), P(), P(), P()),
        out_specs=tiles,
        check_vma=False,
    )
```

```python
import functools
import math

import jax
import jax.numpy as jnp
from jax import lax
from jax.experimental import pallas as pl
from jax.experimental.pallas import tpu as pltpu
from jax.sharding import Mesh
from jax.sharding import PartitionSpec as P

AXES = ("zq", "zc", "xl", "xh", "y", "core")
ROW = ("zq", "zc", "xl")
COL = ("xh", "y", "core")
HEAD = 64
GROUP = 3
WIDE = GROUP * HEAD
SCALE = HEAD**-0.5 * math.log2(math.e)
STATS = 16
bf16, f32 = jnp.bfloat16, jnp.float32


def shifted(block, axis, distance):
    count = lax.axis_size(axis)
    return lax.ppermute(block, axis, [(i, (i + distance) % count) for i in range(count)])


def shifted_x(block, distance):
    place = lambda i: (i % 2) * 2 + i // 2
    route = [(place(i), place((i + distance) % 4)) for i in range(4)]
    return lax.ppermute(block, ("xl", "xh"), route)


def passed_along(block, axis):
    count = lax.axis_size(axis)
    return lax.ppermute(block, axis, [(i - 1, i) for i in range(1, count)])


def corner(block):
    rows, cols = lax.axis_size(ROW), lax.axis_size(COL)
    route = [((r - 1) * cols + c - 1, r * cols + c) for r in range(1, rows) for c in range(1, cols)]
    return lax.ppermute(block, AXES, route)


def normalised(values, gain):
    center = values - jnp.mean(values, axis=-1, keepdims=True)
    spread = jnp.mean(center * center, axis=-1, keepdims=True)
    return center * lax.rsqrt(spread + 1e-06) * gain


def project(tokens, weights):
    return jnp.dot(tokens, weights, preferred_element_type=f32).astype(bf16)


ORDER = (0, 1, 3, 4, 5, 7, 8, 9, 11, 12, 13, 2, 6, 10, 14, 15)
KEY_COLUMNS = 11


def keep(plain, values):
    for k in range(plain.shape[0]):
        plain[k] = values[:, 128 * k : 128 * (k + 1)]


def every_nth(plain, start, step):
    picked = [plain[k, pl.ds(start, 8, stride=step), :] for k in range(plain.shape[0])]
    return jnp.concatenate(picked, 1)


def tokens_kernel(patches_ref, gain_ref, tokens_ref, column_ref, row_ref, corner_ref, plain):
    rows, cols, width = patches_ref.shape
    keep(plain, patches_ref[...].astype(f32).reshape(rows * cols, width))
    gain = gain_ref[...].reshape(1, width)
    last = [None] * cols
    for place, c in enumerate(ORDER):
        parts = [every_nth(plain, cols * r + c, 4 * cols) for r in range(4)]
        column = normalised(jnp.concatenate(parts, 0), gain)
        tokens_ref[pl.ds(32 * place, 32), :] = column.astype(bf16)
        last[c] = column[31:]
    column_ref[...] = column.astype(bf16)
    row_ref[...] = jnp.concatenate(last, 0).astype(bf16)
    corner_ref[...] = last[-1].astype(bf16)


def whole(shape):
    return pl.BlockSpec(shape, lambda *_: (0,) * len(shape))


def normalised_tokens(patches, gain):
    rows, cols, width = patches.shape
    shapes = [(rows * cols, width), (rows, width), (cols, width), (1, width)]
    return pl.pallas_call(
        tokens_kernel,
        in_specs=[pl.BlockSpec(memory_space=pltpu.VMEM)] * 2,
        out_specs=[pl.BlockSpec(memory_space=pltpu.VMEM)] * 4,
        out_shape=[jax.ShapeDtypeStruct(s, bf16) for s in shapes],
        scratch_shapes=[pltpu.VMEM((width // 128, rows * cols, 128), f32)],
        compiler_params=pltpu.CompilerParams(vmem_limit_bytes=16 * 2**20),
        cost_estimate=pl.CostEstimate(flops=4_000_000_000, bytes_accessed=1_000_000, transcendentals=0),
    )(patches, gain)


def halo_tokens(upper_ref, left_ref, corner_ref):
    rest = jnp.zeros((15, left_ref.shape[1]), f32)
    every = [left_ref[...].astype(f32), upper_ref[...].astype(f32), corner_ref[...].astype(f32), rest]
    return jnp.concatenate(every, 0).astype(bf16)


def columns_of(own, halo, columns):
    first = lax.broadcasted_iota(jnp.int32, (8, own.shape[1]), 0) == 0
    groups = {}
    for c in columns:
        if c < 0:
            block, above = halo[0:32], halo[48:49]
        else:
            place = ORDER.index(c)
            block, above = own[32 * place : 32 * place + 32].astype(f32), halo[32 + c : 33 + c]
        four = [block[8 * r : 8 * r + 8] for r in range(4)]
        groups[c] = [jnp.where(first, above, pltpu.roll(four[3], 1, 0))] + four
    return groups


def pooled(groups, taps, column, row):
    total = None
    for a in range(3):
        for b in range(3):
            term = taps[3 * a + b] * groups[column + b - 1][row + a]
            total = term if total is None else total + term
    return total


def keyvals_kernel(tokens_ref, upper_ref, left_ref, corner_ref, w_ref, pool_ref, out_ref):
    halo_in = halo_tokens(upper_ref, left_ref, corner_ref)
    width = tokens_ref.shape[1]
    both = []
    for part in range(2):
        cols = pl.ds(part * width, width)
        weights = w_ref[:, (part + 1) * width : (part + 2) * width]
        halo = project(halo_in, weights).astype(f32)
        own = project(tokens_ref[: 32 * KEY_COLUMNS], weights)
        taps = [pool_ref[t : t + 1, cols] for t in range(9)]
        groups = columns_of(own, halo, (-1,) + ORDER[:KEY_COLUMNS])
        both.append(jnp.concatenate([pooled(groups, taps, 4 * j, 0) for j in range(4)], 0))
    count = width // WIDE
    for g in range(count):
        lanes = slice(g * WIDE, (g + 1) * WIDE)
        block = jnp.concatenate([p[:, lanes] for p in both], 1).astype(bf16)
        for copy in range(out_ref.shape[0] // count):
            out_ref[copy * count + g] = block


def queries_kernel(tokens_ref, upper_ref, left_ref, corner_ref, w_ref, pool_ref, out_ref):
    width = tokens_ref.shape[1]
    weights = w_ref[:, :width]
    halo = project(halo_tokens(upper_ref, left_ref, corner_ref), weights).astype(f32)
    own = project(tokens_ref[...], weights)
    taps = [pool_ref[t : t + 1, :] for t in range(9)]
    groups = columns_of(own, halo, range(-1, 16))
    rows = [pooled(groups, taps, 2 * j, 2 * p) for j in range(8) for p in range(2)]
    turned = jnp.concatenate(rows, 0).T.astype(bf16)
    count = width // WIDE
    for g in range(count):
        block = turned[g * WIDE : (g + 1) * WIDE]
        for copy in range(out_ref.shape[0] // count):
            out_ref[copy * count + g] = block


def pool_call(kernel, tokens, halo, w_qkv, taps, out_shape):
    return pl.pallas_call(
        kernel,
        in_specs=[pl.BlockSpec(memory_space=pltpu.VMEM)] * (3 + len(halo)),
        out_specs=pl.BlockSpec(memory_space=pltpu.VMEM),
        out_shape=jax.ShapeDtypeStruct(out_shape, bf16),
        compiler_params=pltpu.CompilerParams(vmem_limit_bytes=24 * 2**20),
        cost_estimate=pl.CostEstimate(flops=1_500_000_000, bytes_accessed=4_000_000, transcendentals=0),
    )(tokens, *halo, w_qkv, taps)


def attend_kernel(first, last, qb, blocks, q_ref, *refs):
    block_refs, refs = refs[:blocks], refs[blocks:]
    if first:
        stat_in, acc_in = None, None
    else:
        stat_in, acc_in, *refs = refs
    if last:
        out_ref, qz, stat, acc = refs
    else:
        stat, acc, qz = refs
    tiles = q_ref.shape[0]
    count = tiles * 128
    zero = jnp.zeros((HEAD, 128), bf16)
    for t in range(tiles):
        lanes = slice(t * 128, (t + 1) * 128)
        for h in range(GROUP):
            here = HEAD * (h % 2)
            qz[h, here : here + HEAD, lanes] = q_ref[t, HEAD * h : HEAD * (h + 1)]
            qz[h, HEAD - here : 2 * HEAD - here, lanes] = zero

    jobs = [(j, h) for j in range(count // qb) for h in range(GROUP)]
    block = jnp.concatenate([r[...] for r in block_refs], 0)
    values = block[:, 128:].T
    ones = jnp.ones((16, block.shape[0]), bf16)
    lefts = [jnp.concatenate([values[HEAD * h : HEAD * (h + 1)], ones], 0) for h in range(1, GROUP + 1)]

    def scores(j, h):
        keys = block[:, 128 * (h // 2) : 128 * (h // 2) + 128]
        return jnp.dot(keys, qz[h, :, j * qb : (j + 1) * qb], preferred_element_type=f32)

    def fold(lazy):
        rise = jnp.zeros((1, qb), f32)
        ready = scores(*jobs[0])
        for place, (j, h) in enumerate(jobs):
            now = ready
            if place + 1 < len(jobs):
                ready = scores(*jobs[place + 1])
            lanes = slice(j * qb, (j + 1) * qb)
            rows = slice(HEAD * h, HEAD * (h + 1))
            new = jnp.max(now, axis=0, keepdims=True)
            if not first:
                old = stat_in[h : h + 1, lanes]
                new = jnp.maximum(old, new)
                rise = jnp.maximum(rise, new - old)
            weights = jnp.exp2((now - (old if lazy else new)) * SCALE).astype(bf16)
            part = jnp.dot(lefts[h], weights, preferred_element_type=f32)
            total, numer = part[HEAD : HEAD + 1], part[:HEAD]
            if not first:
                factor = jnp.exp2((old - new) * SCALE)
                sums = stat_in[8 + h : 9 + h, lanes], acc_in[rows, lanes]
                if lazy:
                    total, numer = (sums[0] + total) * factor, (sums[1] + numer) * factor
                else:
                    total, numer = sums[0] * factor + total, sums[1] * factor + numer
            stat[h : h + 1, lanes] = new
            stat[8 + h : 9 + h, lanes] = total
            acc[rows, lanes] = numer
        return rise

    if first:
        fold(False)
    else:
        rise = fold(True)

        @pl.when(jnp.logical_not(jnp.max(rise) * SCALE < 60.0))
        def _():
            fold(False)

    if last:
        total = stat[8 : 8 + GROUP]
        logs = stat[0:GROUP] * SCALE + jnp.log2(total)
        high = logs.astype(bf16)
        left = logs - high.astype(f32)
        middle = left.astype(bf16)
        low = left - middle.astype(f32)
        three = [high.astype(f32), middle.astype(f32), low]
        packed = jnp.concatenate(three + [jnp.zeros((STATS - 9, count), f32)], 0).astype(bf16)
        for t in range(tiles):
            lanes = slice(t * 128, (t + 1) * 128)
            for h in range(GROUP):
                rows = slice(HEAD * h, HEAD * (h + 1))
                out_ref[t, rows] = (acc[rows, lanes] / total[h : h + 1, lanes]).astype(bf16)
            out_ref[t, WIDE:] = packed[:, lanes]


def attend(queries, blocks, carry, last=False, qb=512):
    tiles = queries.shape[0]
    count = tiles * 128
    keys = sum(b.shape[0] for b in blocks)
    carry_shapes = [(16, count), (WIDE, count)]
    if last:
        out_shape = [jax.ShapeDtypeStruct((tiles, WIDE + STATS, 128), bf16)]
        scratch = [pltpu.VMEM(s, f32) for s in carry_shapes]
    else:
        out_shape = [jax.ShapeDtypeStruct(s, f32) for s in carry_shapes]
        scratch = []
    carry = [] if carry is None else carry
    work = GROUP * count * keys
    outs = pl.pallas_call(
        functools.partial(attend_kernel, not carry, last, qb, len(blocks)),
        in_specs=[pl.BlockSpec(memory_space=pltpu.VMEM)] * (1 + len(blocks) + len(carry)),
        out_specs=[pl.BlockSpec(memory_space=pltpu.VMEM)] * len(out_shape),
        out_shape=out_shape,
        scratch_shapes=[pltpu.VMEM((GROUP, 128, count), bf16)] + scratch,
        compiler_params=pltpu.CompilerParams(vmem_limit_bytes=24 * 2**20),
        cost_estimate=pl.CostEstimate(
            flops=work * 1, bytes_accessed=1024, transcendentals=0
        ),
    )(queries, *blocks, *carry)
    return outs[0] if last else outs


def finish_kernel(parts_ref, w_ref, out_ref, rows):
    groups = parts_ref.shape[0] // 2
    pieces = []
    for g in range(groups):
        pair = [parts_ref[g], parts_ref[groups + g]]
        logs = []
        for p in pair:
            s = p[WIDE:].astype(f32)
            logs.append((s[0:3] + s[3:6]) + s[6:9])
        top = jnp.maximum(logs[0], logs[1])
        shares = [jnp.exp2(a - top) for a in logs]
        total = shares[0] + shares[1]
        for h in range(GROUP):
            head = slice(HEAD * h, HEAD * (h + 1))
            both = [p[head].astype(f32) * (s[h : h + 1] / total[h : h + 1]) for p, s in zip(pair, shares)]
            pieces.append(both[0] + both[1])
    attended = jnp.concatenate(pieces, 0).T.astype(bf16)
    keep(rows, jnp.dot(attended, w_ref[...], preferred_element_type=f32))
    for r in range(out_ref.shape[0]):
        start = 8 * (r % 2) + r // 2
        out_ref[r] = every_nth(rows, start, 16).astype(bf16)


def finish(parts, w_out):
    shape = (parts.shape[2], w_out.shape[1])
    return pl.pallas_call(
        finish_kernel,
        out_shape=jax.ShapeDtypeStruct((16, 8, shape[1]), bf16),
        scratch_shapes=[pltpu.VMEM((shape[1] // 128, shape[0], 128), f32)],
        compiler_params=pltpu.CompilerParams(vmem_limit_bytes=24 * 2**20),
    )(parts, w_out)


def on_device(patches, norm_gain, w_qkv, pool_q, pool_kv, w_out):
    tokens, last_column, last_row, last_token = normalised_tokens(patches, norm_gain)
    halo = (passed_along(last_row, ROW), passed_along(last_column, COL), corner(last_token))
    groups = lax.axis_size("y")
    flat = pool_call(keyvals_kernel, tokens, halo, w_qkv, pool_kv, (groups, 32, 2 * WIDE))
    own = lax.all_to_all(flat, "y", 0, 0, tiled=True).reshape(-1, 2 * WIDE)
    tie = lax.optimization_barrier
    own, tokens = tie((own, tokens))
    line = [own, shifted(own, "zq", 2), shifted(own, "zq", 1), shifted(own, "zq", -1)]
    turned = pool_call(queries_kernel, tokens, halo, w_qkv, pool_q, (2 * groups, WIDE, 128))
    every_query = lax.all_to_all(turned, ("zc", "y"), 0, 0, tiled=True)
    line = jnp.concatenate(line, 0)
    after, before = shifted_x(line, 1), shifted_x(line, -1)
    swap = lambda block: shifted(block, "core", 1)
    carry = attend(every_query, [line], None)
    carry = attend(every_query, [swap(line)], carry)
    after, before, carry = tie((after, before, carry))
    half = line.shape[0] // 2
    far = [shifted_x(after[:half], 1), shifted_x(before[half:], -1)]
    for block in (after, swap(after), before, swap(before)):
        carry = attend(every_query, [block], carry)
    far, carry = tie((far, carry))
    swapped = [swap(block) for block in far]
    carry = attend(every_query, far, carry)
    partial = attend(every_query, swapped, carry, last=True)
    parts = lax.all_to_all(partial, ("zc", "y"), 0, 0, tiled=True)
    return finish(parts, w_out)


def solution(mesh):
    fine = Mesh(mesh.devices.reshape(4, 2, 2, 2, 4, 2), AXES)
    tiles = P(ROW, COL, None)
    return jax.shard_map(
        on_device,
        mesh=fine,
        in_specs=(tiles, P(), P(), P(), P(), P()),
        out_specs=tiles,
        check_vma=False,
    )
```

```python
import functools
import math

import jax
import jax.numpy as jnp
from jax import lax
from jax.experimental import pallas as pl
from jax.experimental.pallas import tpu as pltpu
from jax.sharding import Mesh
from jax.sharding import PartitionSpec as P

AXES = ("zq", "zc", "xl", "xh", "y", "core")
ROW = ("zq", "zc", "xl")
COL = ("xh", "y", "core")
HEAD = 64
GROUP = 3
WIDE = GROUP * HEAD
SCALE = HEAD**-0.5 * math.log2(math.e)
STATS = 16
bf16, f32 = jnp.bfloat16, jnp.float32


def shifted(block, axis, distance):
    count = lax.axis_size(axis)
    return lax.ppermute(block, axis, [(i, (i + distance) % count) for i in range(count)])


def shifted_x(block, distance):
    place = lambda i: (i % 2) * 2 + i // 2
    route = [(place(i), place((i + distance) % 4)) for i in range(4)]
    return lax.ppermute(block, ("xl", "xh"), route)


def passed_along(block, axis):
    count = lax.axis_size(axis)
    return lax.ppermute(block, axis, [(i - 1, i) for i in range(1, count)])


def corner(block):
    rows, cols = lax.axis_size(ROW), lax.axis_size(COL)
    route = [((r - 1) * cols + c - 1, r * cols + c) for r in range(1, rows) for c in range(1, cols)]
    return lax.ppermute(block, AXES, route)


def normalised(values, gain):
    center = values - jnp.mean(values, axis=-1, keepdims=True)
    spread = jnp.mean(center * center, axis=-1, keepdims=True)
    return center * lax.rsqrt(spread + 1e-06) * gain


def project(tokens, weights):
    return jnp.dot(tokens, weights, preferred_element_type=f32).astype(bf16)


ORDER = (0, 1, 3, 4, 5, 7, 8, 9, 11, 12, 13, 2, 6, 10, 14, 15)
KEY_COLUMNS = 11


def keep(plain, values):
    for k in range(plain.shape[0]):
        plain[k] = values[:, 128 * k : 128 * (k + 1)]


def every_nth(plain, start, step):
    picked = [plain[k, pl.ds(start, 8, stride=step), :] for k in range(plain.shape[0])]
    return jnp.concatenate(picked, 1)


def tokens_kernel(patches_ref, gain_ref, tokens_ref, column_ref, row_ref, corner_ref, plain):
    rows, cols, width = patches_ref.shape
    keep(plain, patches_ref[...].astype(f32).reshape(rows * cols, width))
    gain = gain_ref[...].reshape(1, width)
    last = [None] * cols
    for place, c in enumerate(ORDER):
        parts = [every_nth(plain, cols * r + c, 4 * cols) for r in range(4)]
        column = normalised(jnp.concatenate(parts, 0), gain)
        tokens_ref[pl.ds(32 * place, 32), :] = column.astype(bf16)
        last[c] = column[31:]
    column_ref[...] = column.astype(bf16)
    row_ref[...] = jnp.concatenate(last, 0).astype(bf16)
    corner_ref[...] = last[-1].astype(bf16)


def whole(shape):
    return pl.BlockSpec(shape, lambda *_: (0,) * len(shape))


def normalised_tokens(patches, gain):
    rows, cols, width = patches.shape
    shapes = [(rows * cols, width), (rows, width), (cols, width), (1, width)]
    return pl.pallas_call(
        tokens_kernel,
        in_specs=[pl.BlockSpec(memory_space=pltpu.VMEM)] * 2,
        out_specs=[pl.BlockSpec(memory_space=pltpu.VMEM)] * 4,
        out_shape=[jax.ShapeDtypeStruct(s, bf16) for s in shapes],
        scratch_shapes=[pltpu.VMEM((width // 128, rows * cols, 128), f32)],
        compiler_params=pltpu.CompilerParams(vmem_limit_bytes=16 * 2**20),
        cost_estimate=pl.CostEstimate(flops=4_000_000_000, bytes_accessed=1_000_000, transcendentals=0),
    )(patches, gain)


def halo_tokens(upper_ref, left_ref, corner_ref):
    rest = jnp.zeros((15, left_ref.shape[1]), f32)
    every = [left_ref[...].astype(f32), upper_ref[...].astype(f32), corner_ref[...].astype(f32), rest]
    return jnp.concatenate(every, 0).astype(bf16)


def columns_of(own, halo, columns):
    first = lax.broadcasted_iota(jnp.int32, (8, own.shape[1]), 0) == 0
    groups = {}
    for c in columns:
        if c < 0:
            block, above = halo[0:32], halo[48:49]
        else:
            place = ORDER.index(c)
            block, above = own[32 * place : 32 * place + 32].astype(f32), halo[32 + c : 33 + c]
        four = [block[8 * r : 8 * r + 8] for r in range(4)]
        groups[c] = [jnp.where(first, above, pltpu.roll(four[3], 1, 0))] + four
    return groups


def pooled(groups, taps, column, row):
    total = None
    for a in range(3):
        for b in range(3):
            term = taps[3 * a + b] * groups[column + b - 1][row + a]
            total = term if total is None else total + term
    return total


def keyvals_kernel(here_ref, tokens_ref, upper_ref, left_ref, corner_ref, w_ref, pool_ref, *refs):
    out_refs, parts = refs[:-1], refs[-1]
    halo_in = halo_tokens(upper_ref, left_ref, corner_ref)
    width = tokens_ref.shape[1]
    both = []
    for part in range(2):
        cols = pl.ds(part * width, width)
        weights = w_ref[:, (part + 1) * width : (part + 2) * width]
        halo = project(halo_in, weights).astype(f32)
        own = project(tokens_ref[: 32 * KEY_COLUMNS], weights)
        taps = [pool_ref[t : t + 1, cols] for t in range(9)]
        groups = columns_of(own, halo, (-1,) + ORDER[:KEY_COLUMNS])
        both.append(jnp.concatenate([pooled(groups, taps, 4 * j, 0) for j in range(4)], 0))
    count = width // WIDE
    for g in range(count):
        lanes = slice(g * WIDE, (g + 1) * WIDE)
        parts[g] = jnp.concatenate([p[:, lanes] for p in both], 1).astype(bf16)
    here = here_ref[0]
    for distance, out_ref in enumerate(out_refs):
        out_ref[...] = parts[lax.rem(here + distance, count)]


def queries_kernel(tokens_ref, upper_ref, left_ref, corner_ref, w_ref, pool_ref, out_ref):
    width = tokens_ref.shape[1]
    weights = w_ref[:, :width]
    halo = project(halo_tokens(upper_ref, left_ref, corner_ref), weights).astype(f32)
    own = project(tokens_ref[...], weights)
    taps = [pool_ref[t : t + 1, :] for t in range(9)]
    groups = columns_of(own, halo, range(-1, 16))
    rows = [pooled(groups, taps, 2 * j, 2 * p) for j in range(8) for p in range(2)]
    turned = jnp.concatenate(rows, 0).T.astype(bf16)
    count = width // WIDE
    for g in range(count):
        block = turned[g * WIDE : (g + 1) * WIDE]
        for copy in range(out_ref.shape[0] // count):
            out_ref[copy * count + g] = block


def pool_call(kernel, tokens, halo, w_qkv, taps, out_shapes, scratch=(), scalars=()):
    return pl.pallas_call(
        kernel,
        in_specs=[pl.BlockSpec(memory_space=pltpu.SMEM)] * len(scalars)
        + [pl.BlockSpec(memory_space=pltpu.VMEM)] * (3 + len(halo)),
        out_specs=[pl.BlockSpec(memory_space=pltpu.VMEM)] * len(out_shapes),
        out_shape=[jax.ShapeDtypeStruct(s, bf16) for s in out_shapes],
        scratch_shapes=[pltpu.VMEM(s, bf16) for s in scratch],
        compiler_params=pltpu.CompilerParams(vmem_limit_bytes=24 * 2**20),
        cost_estimate=pl.CostEstimate(flops=1_500_000_000, bytes_accessed=4_000_000, transcendentals=0),
    )(*scalars, tokens, *halo, w_qkv, taps)


def attend_kernel(first, last, qb, blocks, q_ref, *refs):
    block_refs, refs = refs[:blocks], refs[blocks:]
    if first:
        stat_in, acc_in = None, None
    else:
        stat_in, acc_in, *refs = refs
    if last:
        out_ref, qz, stat, acc = refs
    else:
        stat, acc, qz = refs
    tiles = q_ref.shape[0]
    count = tiles * 128
    zero = jnp.zeros((HEAD, 128), bf16)
    for t in range(tiles):
        lanes = slice(t * 128, (t + 1) * 128)
        for h in range(GROUP):
            here = HEAD * (h % 2)
            qz[h, here : here + HEAD, lanes] = q_ref[t, HEAD * h : HEAD * (h + 1)]
            qz[h, HEAD - here : 2 * HEAD - here, lanes] = zero

    jobs = [(j, h) for j in range(count // qb) for h in range(GROUP)]

    def operands():
        block = jnp.concatenate([r[...] for r in block_refs], 0)
        values = block[:, 128:].T
        ones = jnp.ones((16, block.shape[0]), bf16)
        lefts = [jnp.concatenate([values[HEAD * h : HEAD * (h + 1)], ones], 0) for h in range(1, GROUP + 1)]
        return block, lefts

    def scores(block, j, h):
        keys = block[:, 128 * (h // 2) : 128 * (h // 2) + 128]
        return jnp.dot(keys, qz[h, :, j * qb : (j + 1) * qb], preferred_element_type=f32)

    def fold_lazily():
        block, lefts = operands()
        rise = jnp.zeros((1, qb), f32)
        ready = scores(block, *jobs[0])
        for place, (j, h) in enumerate(jobs):
            now = ready
            if place + 1 < len(jobs):
                ready = scores(block, *jobs[place + 1])
            lanes = slice(j * qb, (j + 1) * qb)
            rows = slice(HEAD * h, HEAD * (h + 1))
            old = stat_in[h : h + 1, lanes]
            new = jnp.maximum(old, jnp.max(now, axis=0, keepdims=True))
            rise = jnp.maximum(rise, new - old)
            weights = jnp.exp2((now - old) * SCALE).astype(bf16)
            part = jnp.dot(lefts[h], weights, preferred_element_type=f32)
            factor = jnp.exp2((old - new) * SCALE)
            stat[h : h + 1, lanes] = new
            stat[8 + h : 9 + h, lanes] = (stat_in[8 + h : 9 + h, lanes] + part[HEAD : HEAD + 1]) * factor
            acc[rows, lanes] = (acc_in[rows, lanes] + part[:HEAD]) * factor
        return rise

    def fold(wide):
        @pl.loop(0, count // wide)
        def _(t):
            lanes = pl.ds(pl.multiple_of(t * wide, wide), wide)
            block, lefts = operands()
            for h in range(GROUP):
                rows = slice(HEAD * h, HEAD * (h + 1))
                keys = block[:, 128 * (h // 2) : 128 * (h // 2) + 128]
                now = jnp.dot(keys, qz[h, :, lanes], preferred_element_type=f32)
                new = jnp.max(now, axis=0, keepdims=True)
                if not first:
                    old = stat_in[h : h + 1, lanes]
                    new = jnp.maximum(old, new)
                weights = jnp.exp2((now - new) * SCALE).astype(bf16)
                part = jnp.dot(lefts[h], weights, preferred_element_type=f32)
                total, numer = part[HEAD : HEAD + 1], part[:HEAD]
                if not first:
                    factor = jnp.exp2((old - new) * SCALE)
                    total = stat_in[8 + h : 9 + h, lanes] * factor + total
                    numer = acc_in[rows, lanes] * factor + numer
                stat[h : h + 1, lanes] = new
                stat[8 + h : 9 + h, lanes] = total
                acc[rows, lanes] = numer

    if first:
        fold(qb)
    else:
        rise = fold_lazily()

        @pl.when(jnp.logical_not(jnp.max(rise) * SCALE < 60.0))
        def _():
            fold(128)

    if last:
        total = stat[8 : 8 + GROUP]
        logs = stat[0:GROUP] * SCALE + jnp.log2(total)
        high = logs.astype(bf16)
        left = logs - high.astype(f32)
        middle = left.astype(bf16)
        low = left - middle.astype(f32)
        three = [high.astype(f32), middle.astype(f32), low]
        packed = jnp.concatenate(three + [jnp.zeros((STATS - 9, count), f32)], 0).astype(bf16)
        for t in range(tiles):
            lanes = slice(t * 128, (t + 1) * 128)
            for h in range(GROUP):
                rows = slice(HEAD * h, HEAD * (h + 1))
                out_ref[t, rows] = (acc[rows, lanes] / total[h : h + 1, lanes]).astype(bf16)
            out_ref[t, WIDE:] = packed[:, lanes]


def attend(queries, blocks, carry, last=False, qb=512):
    tiles = queries.shape[0]
    count = tiles * 128
    keys = sum(b.shape[0] for b in blocks)
    carry_shapes = [(16, count), (WIDE, count)]
    if last:
        out_shape = [jax.ShapeDtypeStruct((tiles, WIDE + STATS, 128), bf16)]
        scratch = [pltpu.VMEM(s, f32) for s in carry_shapes]
    else:
        out_shape = [jax.ShapeDtypeStruct(s, f32) for s in carry_shapes]
        scratch = []
    carry = [] if carry is None else carry
    work = GROUP * count * keys
    outs = pl.pallas_call(
        functools.partial(attend_kernel, not carry, last, qb, len(blocks)),
        in_specs=[pl.BlockSpec(memory_space=pltpu.VMEM)] * (1 + len(blocks) + len(carry)),
        out_specs=[pl.BlockSpec(memory_space=pltpu.VMEM)] * len(out_shape),
        out_shape=out_shape,
        scratch_shapes=[pltpu.VMEM((GROUP, 128, count), bf16)] + scratch,
        compiler_params=pltpu.CompilerParams(vmem_limit_bytes=24 * 2**20),
        cost_estimate=pl.CostEstimate(
            flops=work * 1, bytes_accessed=1024, transcendentals=0
        ),
    )(queries, *blocks, *carry)
    return outs[0] if last else outs


def finish_kernel(parts_ref, w_ref, out_ref, rows):
    groups = parts_ref.shape[0] // 2
    pieces = []
    for g in range(groups):
        pair = [parts_ref[g], parts_ref[groups + g]]
        logs = []
        for p in pair:
            s = p[WIDE:].astype(f32)
            logs.append((s[0:3] + s[3:6]) + s[6:9])
        top = jnp.maximum(logs[0], logs[1])
        shares = [jnp.exp2(a - top) for a in logs]
        total = shares[0] + shares[1]
        for h in range(GROUP):
            head = slice(HEAD * h, HEAD * (h + 1))
            both = [p[head].astype(f32) * (s[h : h + 1] / total[h : h + 1]) for p, s in zip(pair, shares)]
            pieces.append(both[0] + both[1])
    attended = jnp.concatenate(pieces, 0).T.astype(bf16)
    keep(rows, jnp.dot(attended, w_ref[...], preferred_element_type=f32))
    for r in range(out_ref.shape[0]):
        start = 8 * (r % 2) + r // 2
        out_ref[r] = every_nth(rows, start, 16).astype(bf16)


def finish(parts, w_out):
    shape = (parts.shape[2], w_out.shape[1])
    return pl.pallas_call(
        finish_kernel,
        out_shape=jax.ShapeDtypeStruct((16, 8, shape[1]), bf16),
        scratch_shapes=[pltpu.VMEM((shape[1] // 128, shape[0], 128), f32)],
        compiler_params=pltpu.CompilerParams(vmem_limit_bytes=24 * 2**20),
    )(parts, w_out)


def on_device(patches, norm_gain, w_qkv, pool_q, pool_kv, w_out):
    tokens, last_column, last_row, last_token = normalised_tokens(patches, norm_gain)
    halo = (passed_along(last_row, ROW), passed_along(last_column, COL), corner(last_token))
    groups = lax.axis_size("y")
    part = (32, 2 * WIDE)
    here = [lax.axis_index("y").reshape(1)]
    parts = pool_call(keyvals_kernel, tokens, halo, w_qkv, pool_kv, [part] * groups, [(groups, *part)], here)
    own = [parts[0]] + [shifted(part, "y", d) for d, part in enumerate(parts) if d]
    own = jnp.concatenate(own, 0)
    (turned,) = pool_call(queries_kernel, tokens, halo, w_qkv, pool_q, [(2 * groups, WIDE, 128)])
    every_query = lax.all_to_all(turned, ("zc", "y"), 0, 0, tiled=True)
    tie = lax.optimization_barrier
    line = [own, shifted(own, "zq", 2), shifted(own, "zq", 1), shifted(own, "zq", -1)]
    line = jnp.concatenate(line, 0)
    after, before = shifted_x(line, 1), shifted_x(line, -1)
    swap = lambda block: shifted(block, "core", 1)
    carry = attend(every_query, [line], None)
    carry = attend(every_query, [swap(line)], carry)
    after, before, carry = tie((after, before, carry))
    half = line.shape[0] // 2
    far = [shifted_x(after[:half], 1), shifted_x(before[half:], -1)]
    for block in (after, swap(after), before, swap(before)):
        carry = attend(every_query, [block], carry)
    far, carry = tie((far, carry))
    swapped = [swap(block) for block in far]
    carry = attend(every_query, far, carry)
    partial = attend(every_query, swapped, carry, last=True)
    parts = lax.all_to_all(partial, ("zc", "y"), 0, 0, tiled=True)
    return finish(parts, w_out)


def solution(mesh):
    fine = Mesh(mesh.devices.reshape(4, 2, 2, 2, 4, 2), AXES)
    tiles = P(ROW, COL, None)
    return jax.shard_map(
        on_device,
        mesh=fine,
        in_specs=(tiles, P(), P(), P(), P(), P()),
        out_specs=tiles,
        check_vma=False,
    )
```

```python
import functools
import math

import jax
import jax.numpy as jnp
from jax import lax
from jax.experimental import pallas as pl
from jax.experimental.pallas import tpu as pltpu
from jax.sharding import Mesh
from jax.sharding import PartitionSpec as P

AXES = ("zq", "zc", "xl", "xh", "y", "core")
ROW = ("zq", "zc", "xl")
COL = ("xh", "y", "core")
HEAD = 64
GROUP = 3
WIDE = GROUP * HEAD
SCALE = HEAD**-0.5 * math.log2(math.e)
STATS = 16
bf16, f32 = jnp.bfloat16, jnp.float32


def shifted(block, axis, distance):
    count = lax.axis_size(axis)
    return lax.ppermute(block, axis, [(i, (i + distance) % count) for i in range(count)])


def shifted_x(block, distance):
    place = lambda i: (i % 2) * 2 + i // 2
    route = [(place(i), place((i + distance) % 4)) for i in range(4)]
    return lax.ppermute(block, ("xl", "xh"), route)


def passed_along(block, axis):
    count = lax.axis_size(axis)
    return lax.ppermute(block, axis, [(i - 1, i) for i in range(1, count)])


def corner(block):
    rows, cols = lax.axis_size(ROW), lax.axis_size(COL)
    route = [((r - 1) * cols + c - 1, r * cols + c) for r in range(1, rows) for c in range(1, cols)]
    return lax.ppermute(block, AXES, route)


def normalised(values, gain):
    center = values - jnp.mean(values, axis=-1, keepdims=True)
    spread = jnp.mean(center * center, axis=-1, keepdims=True)
    return center * lax.rsqrt(spread + 1e-06) * gain


def project(tokens, weights):
    return jnp.dot(tokens, weights, preferred_element_type=f32).astype(bf16)


ORDER = (0, 1, 3, 4, 5, 7, 8, 9, 11, 12, 13, 2, 6, 10, 14, 15)
KEY_COLUMNS = 11


def keep(plain, values):
    for k in range(plain.shape[0]):
        plain[k] = values[:, 128 * k : 128 * (k + 1)]


def every_nth(plain, start, step):
    picked = [plain[k, pl.ds(start, 8, stride=step), :] for k in range(plain.shape[0])]
    return jnp.concatenate(picked, 1)


def tokens_kernel(patches_ref, gain_ref, tokens_ref, column_ref, row_ref, corner_ref, plain):
    rows, cols, width = patches_ref.shape
    keep(plain, patches_ref[...].astype(f32).reshape(rows * cols, width))
    gain = gain_ref[...].reshape(1, width)
    last = [None] * cols
    for place, c in enumerate(ORDER):
        parts = [every_nth(plain, cols * r + c, 4 * cols) for r in range(4)]
        column = normalised(jnp.concatenate(parts, 0), gain)
        tokens_ref[pl.ds(32 * place, 32), :] = column.astype(bf16)
        last[c] = column[31:]
    column_ref[...] = column.astype(bf16)
    row_ref[...] = jnp.concatenate(last, 0).astype(bf16)
    corner_ref[...] = last[-1].astype(bf16)


def whole(shape):
    return pl.BlockSpec(shape, lambda *_: (0,) * len(shape))


def normalised_tokens(patches, gain):
    rows, cols, width = patches.shape
    shapes = [(rows * cols, width), (rows, width), (cols, width), (1, width)]
    return pl.pallas_call(
        tokens_kernel,
        in_specs=[pl.BlockSpec(memory_space=pltpu.VMEM)] * 2,
        out_specs=[pl.BlockSpec(memory_space=pltpu.VMEM)] * 4,
        out_shape=[jax.ShapeDtypeStruct(s, bf16) for s in shapes],
        scratch_shapes=[pltpu.VMEM((width // 128, rows * cols, 128), f32)],
        compiler_params=pltpu.CompilerParams(vmem_limit_bytes=16 * 2**20),
        cost_estimate=pl.CostEstimate(flops=4_000_000_000, bytes_accessed=1_000_000, transcendentals=0),
    )(patches, gain)


def own_kernel(tokens_ref, w_ref, q_ref, kv_ref):
    width = tokens_ref.shape[1]
    few = kv_ref.shape[0]
    for part in range(2):
        cols = slice(part * width, (part + 1) * width)
        kv_ref[:, cols] = project(tokens_ref[:few], w_ref[:, (part + 1) * width : (part + 2) * width])
    q_ref[...] = project(tokens_ref[...], w_ref[:, :width])


def project_own(tokens, w_qkv):
    count, width = tokens.shape
    shapes = [(count, width), (32 * KEY_COLUMNS, 2 * width)]
    return pl.pallas_call(
        own_kernel,
        in_specs=[pl.BlockSpec(memory_space=pltpu.VMEM)] * 2,
        out_specs=[pl.BlockSpec(memory_space=pltpu.VMEM)] * 2,
        out_shape=[jax.ShapeDtypeStruct(s, bf16) for s in shapes],
        compiler_params=pltpu.CompilerParams(vmem_limit_bytes=16 * 2**20),
        cost_estimate=pl.CostEstimate(flops=1_500_000_000, bytes_accessed=4_000_000, transcendentals=0),
    )(tokens, w_qkv)


def halo_tokens(upper_ref, left_ref, corner_ref):
    rest = jnp.zeros((15, left_ref.shape[1]), f32)
    every = [left_ref[...].astype(f32), upper_ref[...].astype(f32), corner_ref[...].astype(f32), rest]
    return jnp.concatenate(every, 0).astype(bf16)


def columns_of(own, halo, columns):
    first = lax.broadcasted_iota(jnp.int32, (8, own.shape[1]), 0) == 0
    groups = {}
    for c in columns:
        if c < 0:
            block, above = halo[0:32], halo[48:49]
        else:
            place = ORDER.index(c)
            block, above = own[32 * place : 32 * place + 32].astype(f32), halo[32 + c : 33 + c]
        four = [block[8 * r : 8 * r + 8] for r in range(4)]
        groups[c] = [jnp.where(first, above, pltpu.roll(four[3], 1, 0))] + four
    return groups


def pooled(groups, taps, column, row):
    total = None
    for a in range(3):
        for b in range(3):
            term = taps[3 * a + b] * groups[column + b - 1][row + a]
            total = term if total is None else total + term
    return total


def keyvals_kernel(own_ref, upper_ref, left_ref, corner_ref, w_ref, pool_ref, out_ref):
    halo_in = halo_tokens(upper_ref, left_ref, corner_ref)
    width = own_ref.shape[1] // 2
    both = []
    for part in range(2):
        cols = pl.ds(part * width, width)
        weights = w_ref[:, (part + 1) * width : (part + 2) * width]
        halo = project(halo_in, weights).astype(f32)
        own = own_ref[:, part * width : (part + 1) * width]
        taps = [pool_ref[t : t + 1, cols] for t in range(9)]
        groups = columns_of(own, halo, (-1,) + ORDER[:KEY_COLUMNS])
        both.append(jnp.concatenate([pooled(groups, taps, 4 * j, 0) for j in range(4)], 0))
    count = width // WIDE
    for g in range(count):
        lanes = slice(g * WIDE, (g + 1) * WIDE)
        block = jnp.concatenate([p[:, lanes] for p in both], 1).astype(bf16)
        for copy in range(out_ref.shape[0] // count):
            out_ref[copy * count + g] = block


def queries_kernel(own_ref, upper_ref, left_ref, corner_ref, w_ref, pool_ref, out_ref):
    width = own_ref.shape[1]
    weights = w_ref[:, :width]
    halo = project(halo_tokens(upper_ref, left_ref, corner_ref), weights).astype(f32)
    own = own_ref[...]
    taps = [pool_ref[t : t + 1, :] for t in range(9)]
    groups = columns_of(own, halo, range(-1, 16))
    rows = [pooled(groups, taps, 2 * j, 2 * p) for j in range(8) for p in range(2)]
    turned = jnp.concatenate(rows, 0).T.astype(bf16)
    count = width // WIDE
    for g in range(count):
        block = turned[g * WIDE : (g + 1) * WIDE]
        for copy in range(out_ref.shape[0] // count):
            out_ref[copy * count + g] = block


def pool_call(kernel, own, halo, w_qkv, taps, out_shape):
    return pl.pallas_call(
        kernel,
        in_specs=[pl.BlockSpec(memory_space=pltpu.VMEM)] * (3 + len(halo)),
        out_specs=pl.BlockSpec(memory_space=pltpu.VMEM),
        out_shape=jax.ShapeDtypeStruct(out_shape, bf16),
        compiler_params=pltpu.CompilerParams(vmem_limit_bytes=24 * 2**20),
        cost_estimate=pl.CostEstimate(flops=200_000_000, bytes_accessed=4_000_000, transcendentals=0),
    )(own, *halo, w_qkv, taps)


def attend_kernel(first, last, qb, blocks, q_ref, *refs):
    block_refs, refs = refs[:blocks], refs[blocks:]
    if first:
        stat_in, acc_in = None, None
    else:
        stat_in, acc_in, *refs = refs
    if last:
        out_ref, qz, stat, acc = refs
    else:
        stat, acc, qz = refs
    tiles = q_ref.shape[0]
    count = tiles * 128
    zero = jnp.zeros((HEAD, 128), bf16)
    for t in range(tiles):
        lanes = slice(t * 128, (t + 1) * 128)
        for h in range(GROUP):
            here = HEAD * (h % 2)
            qz[h, here : here + HEAD, lanes] = q_ref[t, HEAD * h : HEAD * (h + 1)]
            qz[h, HEAD - here : 2 * HEAD - here, lanes] = zero

    jobs = [(j, h) for j in range(count // qb) for h in range(GROUP)]

    def operands():
        block = jnp.concatenate([r[...] for r in block_refs], 0)
        values = block[:, 128:].T
        ones = jnp.ones((16, block.shape[0]), bf16)
        lefts = [jnp.concatenate([values[HEAD * h : HEAD * (h + 1)], ones], 0) for h in range(1, GROUP + 1)]
        return block, lefts

    def scores(block, j, h):
        keys = block[:, 128 * (h // 2) : 128 * (h // 2) + 128]
        return jnp.dot(keys, qz[h, :, j * qb : (j + 1) * qb], preferred_element_type=f32)

    def fold_lazily():
        block, lefts = operands()
        rise = jnp.zeros((1, qb), f32)
        ready = scores(block, *jobs[0])
        for place, (j, h) in enumerate(jobs):
            now = ready
            if place + 1 < len(jobs):
                ready = scores(block, *jobs[place + 1])
            lanes = slice(j * qb, (j + 1) * qb)
            rows = slice(HEAD * h, HEAD * (h + 1))
            old = stat_in[h : h + 1, lanes]
            new = jnp.maximum(old, jnp.max(now, axis=0, keepdims=True))
            rise = jnp.maximum(rise, new - old)
            weights = jnp.exp2((now - old) * SCALE).astype(bf16)
            part = jnp.dot(lefts[h], weights, preferred_element_type=f32)
            factor = jnp.exp2((old - new) * SCALE)
            stat[h : h + 1, lanes] = new
            stat[8 + h : 9 + h, lanes] = (stat_in[8 + h : 9 + h, lanes] + part[HEAD : HEAD + 1]) * factor
            acc[rows, lanes] = (acc_in[rows, lanes] + part[:HEAD]) * factor
        return rise

    def fold(wide):
        @pl.loop(0, count // wide)
        def _(t):
            lanes = pl.ds(pl.multiple_of(t * wide, wide), wide)
            block, lefts = operands()
            for h in range(GROUP):
                rows = slice(HEAD * h, HEAD * (h + 1))
                keys = block[:, 128 * (h // 2) : 128 * (h // 2) + 128]
                now = jnp.dot(keys, qz[h, :, lanes], preferred_element_type=f32)
                new = jnp.max(now, axis=0, keepdims=True)
                if not first:
                    old = stat_in[h : h + 1, lanes]
                    new = jnp.maximum(old, new)
                weights = jnp.exp2((now - new) * SCALE).astype(bf16)
                part = jnp.dot(lefts[h], weights, preferred_element_type=f32)
                total, numer = part[HEAD : HEAD + 1], part[:HEAD]
                if not first:
                    factor = jnp.exp2((old - new) * SCALE)
                    total = stat_in[8 + h : 9 + h, lanes] * factor + total
                    numer = acc_in[rows, lanes] * factor + numer
                stat[h : h + 1, lanes] = new
                stat[8 + h : 9 + h, lanes] = total
                acc[rows, lanes] = numer

    if first:
        fold(qb)
    else:
        rise = fold_lazily()

        @pl.when(jnp.logical_not(jnp.max(rise) * SCALE < 60.0))
        def _():
            fold(128)

    if last:
        total = stat[8 : 8 + GROUP]
        logs = stat[0:GROUP] * SCALE + jnp.log2(total)
        high = logs.astype(bf16)
        left = logs - high.astype(f32)
        middle = left.astype(bf16)
        low = left - middle.astype(f32)
        three = [high.astype(f32), middle.astype(f32), low]
        packed = jnp.concatenate(three + [jnp.zeros((STATS - 9, count), f32)], 0).astype(bf16)
        for t in range(tiles):
            lanes = slice(t * 128, (t + 1) * 128)
            for h in range(GROUP):
                rows = slice(HEAD * h, HEAD * (h + 1))
                out_ref[t, rows] = (acc[rows, lanes] / total[h : h + 1, lanes]).astype(bf16)
            out_ref[t, WIDE:] = packed[:, lanes]


def attend(queries, blocks, carry, last=False, qb=512):
    tiles = queries.shape[0]
    count = tiles * 128
    keys = sum(b.shape[0] for b in blocks)
    carry_shapes = [(16, count), (WIDE, count)]
    if last:
        out_shape = [jax.ShapeDtypeStruct((tiles, WIDE + STATS, 128), bf16)]
        scratch = [pltpu.VMEM(s, f32) for s in carry_shapes]
    else:
        out_shape = [jax.ShapeDtypeStruct(s, f32) for s in carry_shapes]
        scratch = []
    carry = [] if carry is None else carry
    work = GROUP * count * keys
    outs = pl.pallas_call(
        functools.partial(attend_kernel, not carry, last, qb, len(blocks)),
        in_specs=[pl.BlockSpec(memory_space=pltpu.VMEM)] * (1 + len(blocks) + len(carry)),
        out_specs=[pl.BlockSpec(memory_space=pltpu.VMEM)] * len(out_shape),
        out_shape=out_shape,
        scratch_shapes=[pltpu.VMEM((GROUP, 128, count), bf16)] + scratch,
        compiler_params=pltpu.CompilerParams(vmem_limit_bytes=24 * 2**20),
        cost_estimate=pl.CostEstimate(
            flops=work * 1, bytes_accessed=1024, transcendentals=0
        ),
    )(queries, *blocks, *carry)
    return outs[0] if last else outs


def finish_kernel(parts_ref, w_ref, out_ref, rows):
    groups = parts_ref.shape[0] // 2
    pieces = []
    for g in range(groups):
        pair = [parts_ref[g], parts_ref[groups + g]]
        logs = []
        for p in pair:
            s = p[WIDE:].astype(f32)
            logs.append((s[0:3] + s[3:6]) + s[6:9])
        top = jnp.maximum(logs[0], logs[1])
        shares = [jnp.exp2(a - top) for a in logs]
        total = shares[0] + shares[1]
        for h in range(GROUP):
            head = slice(HEAD * h, HEAD * (h + 1))
            both = [p[head].astype(f32) * (s[h : h + 1] / total[h : h + 1]) for p, s in zip(pair, shares)]
            pieces.append(both[0] + both[1])
    attended = jnp.concatenate(pieces, 0).T.astype(bf16)
    keep(rows, jnp.dot(attended, w_ref[...], preferred_element_type=f32))
    for r in range(out_ref.shape[0]):
        start = 8 * (r % 2) + r // 2
        out_ref[r] = every_nth(rows, start, 16).astype(bf16)


def finish(parts, w_out):
    shape = (parts.shape[2], w_out.shape[1])
    return pl.pallas_call(
        finish_kernel,
        out_shape=jax.ShapeDtypeStruct((16, 8, shape[1]), bf16),
        scratch_shapes=[pltpu.VMEM((shape[1] // 128, shape[0], 128), f32)],
        compiler_params=pltpu.CompilerParams(vmem_limit_bytes=24 * 2**20),
    )(parts, w_out)


def on_device(patches, norm_gain, w_qkv, pool_q, pool_kv, w_out):
    tokens, last_column, last_row, last_token = normalised_tokens(patches, norm_gain)
    halo = (passed_along(last_row, ROW), passed_along(last_column, COL), corner(last_token))
    own_q, own_kv = project_own(tokens, w_qkv)
    groups = lax.axis_size("y")
    flat = pool_call(keyvals_kernel, own_kv, halo, w_qkv, pool_kv, (groups, 32, 2 * WIDE))
    own = lax.all_to_all(flat, "y", 0, 0, tiled=True).reshape(-1, 2 * WIDE)
    tie = lax.optimization_barrier
    own, own_q = tie((own, own_q))
    line = [own, shifted(own, "zq", 2), shifted(own, "zq", 1), shifted(own, "zq", -1)]
    turned = pool_call(queries_kernel, own_q, halo, w_qkv, pool_q, (2 * groups, WIDE, 128))
    every_query = lax.all_to_all(turned, ("zc", "y"), 0, 0, tiled=True)
    line = jnp.concatenate(line, 0)
    after, before = shifted_x(line, 1), shifted_x(line, -1)
    swap = lambda block: shifted(block, "core", 1)
    carry = attend(every_query, [line], None)
    carry = attend(every_query, [swap(line)], carry)
    after, before, carry = tie((after, before, carry))
    half = line.shape[0] // 2
    far = [shifted_x(after[:half], 1), shifted_x(before[half:], -1)]
    for block in (after, swap(after), before, swap(before)):
        carry = attend(every_query, [block], carry)
    far, carry = tie((far, carry))
    swapped = [swap(block) for block in far]
    carry = attend(every_query, far, carry)
    partial = attend(every_query, swapped, carry, last=True)
    parts = lax.all_to_all(partial, ("zc", "y"), 0, 0, tiled=True)
    return finish(parts, w_out)


def solution(mesh):
    fine = Mesh(mesh.devices.reshape(4, 2, 2, 2, 4, 2), AXES)
    tiles = P(ROW, COL, None)
    return jax.shard_map(
        on_device,
        mesh=fine,
        in_specs=(tiles, P(), P(), P(), P(), P()),
        out_specs=tiles,
        check_vma=False,
    )
```

```python
import functools
import math

import jax
import jax.numpy as jnp
from jax import lax
from jax.experimental import pallas as pl
from jax.experimental.pallas import tpu as pltpu
from jax.sharding import Mesh
from jax.sharding import PartitionSpec as P

AXES = ("zq", "zc", "xl", "xh", "y", "core")
ROW = ("zq", "zc", "xl")
COL = ("xh", "y", "core")
HEAD = 64
GROUP = 3
WIDE = GROUP * HEAD
SCALE = HEAD**-0.5 * math.log2(math.e)
STATS = 16
bf16, f32 = jnp.bfloat16, jnp.float32


def shifted(block, axis, distance):
    count = lax.axis_size(axis)
    return lax.ppermute(block, axis, [(i, (i + distance) % count) for i in range(count)])


def shifted_x(block, distance):
    place = lambda i: (i % 2) * 2 + i // 2
    route = [(place(i), place((i + distance) % 4)) for i in range(4)]
    return lax.ppermute(block, ("xl", "xh"), route)


def passed_along(block, axis):
    count = lax.axis_size(axis)
    return lax.ppermute(block, axis, [(i - 1, i) for i in range(1, count)])


def corner(block):
    rows, cols = lax.axis_size(ROW), lax.axis_size(COL)
    route = [((r - 1) * cols + c - 1, r * cols + c) for r in range(1, rows) for c in range(1, cols)]
    return lax.ppermute(block, AXES, route)


def normalised(values, gain):
    center = values - jnp.mean(values, axis=-1, keepdims=True)
    spread = jnp.mean(center * center, axis=-1, keepdims=True)
    return center * lax.rsqrt(spread + 1e-06) * gain


def project(tokens, weights):
    return jnp.dot(tokens, weights, preferred_element_type=f32).astype(bf16)


ORDER = (0, 1, 3, 4, 5, 7, 8, 9, 11, 12, 13, 2, 6, 10, 14, 15)
KEY_COLUMNS = 11


def keep(plain, values):
    for k in range(plain.shape[0]):
        plain[k] = values[:, 128 * k : 128 * (k + 1)]


def every_nth(plain, start, step):
    picked = [plain[k, pl.ds(start, 8, stride=step), :] for k in range(plain.shape[0])]
    return jnp.concatenate(picked, 1)


def tokens_kernel(patches_ref, gain_ref, tokens_ref, column_ref, row_ref, corner_ref, patches, gains, plain, sems):
    rows, cols, width = patches.shape
    copies = [
        pltpu.make_async_copy(patches_ref, patches, sems.at[0]),
        pltpu.make_async_copy(gain_ref, gains, sems.at[1]),
    ]
    for copy in copies:
        copy.start()
    for copy in copies:
        copy.wait()
    keep(plain, patches[...].astype(f32).reshape(rows * cols, width))
    gain = gains[...].reshape(1, width)
    last = [None] * cols
    for place, c in enumerate(ORDER):
        parts = [every_nth(plain, cols * r + c, 4 * cols) for r in range(4)]
        column = normalised(jnp.concatenate(parts, 0), gain)
        tokens_ref[pl.ds(32 * place, 32), :] = column.astype(bf16)
        last[c] = column[31:]
    column_ref[...] = column.astype(bf16)
    row_ref[...] = jnp.concatenate(last, 0).astype(bf16)
    corner_ref[...] = last[-1].astype(bf16)


def whole(shape):
    return pl.BlockSpec(shape, lambda *_: (0,) * len(shape))


def normalised_tokens(patches, gain):
    rows, cols, width = patches.shape
    shapes = [(rows * cols, width), (rows, width), (cols, width), (1, width)]
    return pl.pallas_call(
        tokens_kernel,
        in_specs=[pl.BlockSpec(memory_space=pl.ANY)] * 2,
        out_specs=[pl.BlockSpec(memory_space=pltpu.VMEM)] * 4,
        out_shape=[jax.ShapeDtypeStruct(s, bf16) for s in shapes],
        scratch_shapes=[
            pltpu.VMEM(patches.shape, bf16),
            pltpu.VMEM(gain.shape, f32),
            pltpu.VMEM((width // 128, rows * cols, 128), f32),
            pltpu.SemaphoreType.DMA((2,)),
        ],
        compiler_params=pltpu.CompilerParams(vmem_limit_bytes=57 * 2**20),
        cost_estimate=pl.CostEstimate(flops=4_000_000_000, bytes_accessed=1_000_000, transcendentals=0),
    )(patches, gain)


def own_kernel(tokens_ref, w_ref, q_ref, kv_ref):
    width = tokens_ref.shape[1]
    few = kv_ref.shape[0]
    for part in range(2):
        cols = slice(part * width, (part + 1) * width)
        kv_ref[:, cols] = project(tokens_ref[:few], w_ref[:, (part + 1) * width : (part + 2) * width])
    q_ref[...] = project(tokens_ref[...], w_ref[:, :width])


def project_own(tokens, w_qkv):
    count, width = tokens.shape
    shapes = [(count, width), (32 * KEY_COLUMNS, 2 * width)]
    return pl.pallas_call(
        own_kernel,
        in_specs=[pl.BlockSpec(memory_space=pltpu.VMEM)] * 2,
        out_specs=[pl.BlockSpec(memory_space=pltpu.VMEM)] * 2,
        out_shape=[jax.ShapeDtypeStruct(s, bf16) for s in shapes],
        compiler_params=pltpu.CompilerParams(vmem_limit_bytes=16 * 2**20),
        cost_estimate=pl.CostEstimate(flops=1_500_000_000, bytes_accessed=4_000_000, transcendentals=0),
    )(tokens, w_qkv)


def halo_tokens(upper_ref, left_ref, corner_ref):
    rest = jnp.zeros((15, left_ref.shape[1]), f32)
    every = [left_ref[...].astype(f32), upper_ref[...].astype(f32), corner_ref[...].astype(f32), rest]
    return jnp.concatenate(every, 0).astype(bf16)


def columns_of(own, halo, columns):
    first = lax.broadcasted_iota(jnp.int32, (8, own.shape[1]), 0) == 0
    groups = {}
    for c in columns:
        if c < 0:
            block, above = halo[0:32], halo[48:49]
        else:
            place = ORDER.index(c)
            block, above = own[32 * place : 32 * place + 32].astype(f32), halo[32 + c : 33 + c]
        four = [block[8 * r : 8 * r + 8] for r in range(4)]
        groups[c] = [jnp.where(first, above, pltpu.roll(four[3], 1, 0))] + four
    return groups


def pooled(groups, taps, column, row):
    total = None
    for a in range(3):
        for b in range(3):
            term = taps[3 * a + b] * groups[column + b - 1][row + a]
            total = term if total is None else total + term
    return total


def keyvals_kernel(own_ref, upper_ref, left_ref, corner_ref, w_ref, pool_ref, out_ref):
    halo_in = halo_tokens(upper_ref, left_ref, corner_ref)
    width = own_ref.shape[1] // 2
    both = []
    for part in range(2):
        cols = pl.ds(part * width, width)
        weights = w_ref[:, (part + 1) * width : (part + 2) * width]
        halo = project(halo_in, weights).astype(f32)
        own = own_ref[:, part * width : (part + 1) * width]
        taps = [pool_ref[t : t + 1, cols] for t in range(9)]
        groups = columns_of(own, halo, (-1,) + ORDER[:KEY_COLUMNS])
        both.append(jnp.concatenate([pooled(groups, taps, 4 * j, 0) for j in range(4)], 0))
    count = width // WIDE
    for g in range(count):
        lanes = slice(g * WIDE, (g + 1) * WIDE)
        block = jnp.concatenate([p[:, lanes] for p in both], 1).astype(bf16)
        for copy in range(out_ref.shape[0] // count):
            out_ref[copy * count + g] = block


def queries_kernel(own_ref, upper_ref, left_ref, corner_ref, w_ref, pool_ref, out_ref):
    width = own_ref.shape[1]
    weights = w_ref[:, :width]
    halo = project(halo_tokens(upper_ref, left_ref, corner_ref), weights).astype(f32)
    own = own_ref[...]
    taps = [pool_ref[t : t + 1, :] for t in range(9)]
    groups = columns_of(own, halo, range(-1, 16))
    rows = [pooled(groups, taps, 2 * j, 2 * p) for j in range(8) for p in range(2)]
    turned = jnp.concatenate(rows, 0).T.astype(bf16)
    count = width // WIDE
    for g in range(count):
        block = turned[g * WIDE : (g + 1) * WIDE]
        for copy in range(out_ref.shape[0] // count):
            out_ref[copy * count + g] = block


def pool_call(kernel, own, halo, w_qkv, taps, out_shape):
    return pl.pallas_call(
        kernel,
        in_specs=[pl.BlockSpec(memory_space=pltpu.VMEM)] * (3 + len(halo)),
        out_specs=pl.BlockSpec(memory_space=pltpu.VMEM),
        out_shape=jax.ShapeDtypeStruct(out_shape, bf16),
        compiler_params=pltpu.CompilerParams(vmem_limit_bytes=24 * 2**20),
        cost_estimate=pl.CostEstimate(flops=200_000_000, bytes_accessed=4_000_000, transcendentals=0),
    )(own, *halo, w_qkv, taps)


def pad_queries(q_ref, padded):
    zero = jnp.zeros((HEAD, 128), bf16)
    for t in range(q_ref.shape[0]):
        lanes = slice(t * 128, (t + 1) * 128)
        for h in range(GROUP):
            here = HEAD * (h % 2)
            padded[h, here : here + HEAD, lanes] = q_ref[t, HEAD * h : HEAD * (h + 1)]
            padded[h, HEAD - here : 2 * HEAD - here, lanes] = zero


def attend_kernel(first, last, qb, blocks, q_ref, *refs):
    block_refs, refs = refs[:blocks], refs[blocks:]
    if first:
        stat, acc, qz = refs
        pad_queries(q_ref, qz)
    else:
        stat_in, acc_in, *refs = refs
        qz = q_ref
        if last:
            out_ref, stat, acc = refs
        else:
            stat, acc = refs
    count = qz.shape[2]
    tiles = count // 128

    jobs = [(j, h) for j in range(count // qb) for h in range(GROUP)]

    def operands():
        block = jnp.concatenate([r[...] for r in block_refs], 0)
        values = block[:, 128:].T
        ones = jnp.ones((16, block.shape[0]), bf16)
        lefts = [jnp.concatenate([values[HEAD * h : HEAD * (h + 1)], ones], 0) for h in range(1, GROUP + 1)]
        return block, lefts

    def scores(block, j, h):
        keys = block[:, 128 * (h // 2) : 128 * (h // 2) + 128]
        return jnp.dot(keys, qz[h, :, j * qb : (j + 1) * qb], preferred_element_type=f32)

    def fold_lazily():
        block, lefts = operands()
        rise = jnp.zeros((1, qb), f32)
        ready = scores(block, *jobs[0])
        for place, (j, h) in enumerate(jobs):
            now = ready
            if place + 1 < len(jobs):
                ready = scores(block, *jobs[place + 1])
            lanes = slice(j * qb, (j + 1) * qb)
            rows = slice(HEAD * h, HEAD * (h + 1))
            old = stat_in[h : h + 1, lanes]
            new = jnp.maximum(old, jnp.max(now, axis=0, keepdims=True))
            rise = jnp.maximum(rise, new - old)
            weights = jnp.exp2((now - old) * SCALE).astype(bf16)
            part = jnp.dot(lefts[h], weights, preferred_element_type=f32)
            factor = jnp.exp2((old - new) * SCALE)
            stat[h : h + 1, lanes] = new
            stat[8 + h : 9 + h, lanes] = (stat_in[8 + h : 9 + h, lanes] + part[HEAD : HEAD + 1]) * factor
            acc[rows, lanes] = (acc_in[rows, lanes] + part[:HEAD]) * factor
        return rise

    def fold(wide):
        @pl.loop(0, count // wide)
        def _(t):
            lanes = pl.ds(pl.multiple_of(t * wide, wide), wide)
            block, lefts = operands()
            for h in range(GROUP):
                rows = slice(HEAD * h, HEAD * (h + 1))
                keys = block[:, 128 * (h // 2) : 128 * (h // 2) + 128]
                now = jnp.dot(keys, qz[h, :, lanes], preferred_element_type=f32)
                new = jnp.max(now, axis=0, keepdims=True)
                if not first:
                    old = stat_in[h : h + 1, lanes]
                    new = jnp.maximum(old, new)
                weights = jnp.exp2((now - new) * SCALE).astype(bf16)
                part = jnp.dot(lefts[h], weights, preferred_element_type=f32)
                total, numer = part[HEAD : HEAD + 1], part[:HEAD]
                if not first:
                    factor = jnp.exp2((old - new) * SCALE)
                    total = stat_in[8 + h : 9 + h, lanes] * factor + total
                    numer = acc_in[rows, lanes] * factor + numer
                stat[h : h + 1, lanes] = new
                stat[8 + h : 9 + h, lanes] = total
                acc[rows, lanes] = numer

    if first:
        fold(qb)
    else:
        rise = fold_lazily()

        @pl.when(jnp.logical_not(jnp.max(rise) * SCALE < 60.0))
        def _():
            fold(128)

    if last:
        total = stat[8 : 8 + GROUP]
        logs = stat[0:GROUP] * SCALE + jnp.log2(total)
        high = logs.astype(bf16)
        left = logs - high.astype(f32)
        middle = left.astype(bf16)
        low = left - middle.astype(f32)
        three = [high.astype(f32), middle.astype(f32), low]
        packed = jnp.concatenate(three + [jnp.zeros((STATS - 9, count), f32)], 0).astype(bf16)
        for t in range(tiles):
            lanes = slice(t * 128, (t + 1) * 128)
            for h in range(GROUP):
                rows = slice(HEAD * h, HEAD * (h + 1))
                out_ref[t, rows] = (acc[rows, lanes] / total[h : h + 1, lanes]).astype(bf16)
            out_ref[t, WIDE:] = packed[:, lanes]


def attend(queries, blocks, carry, last=False, qb=512):
    first = carry is None
    carry = [] if first else carry
    count = queries.shape[0] * 128 if first else queries.shape[2]
    keys = sum(b.shape[0] for b in blocks)
    carry_shapes = [(16, count), (WIDE, count)]
    scratch = []
    if last:
        out_shape = [jax.ShapeDtypeStruct((count // 128, WIDE + STATS, 128), bf16)]
        scratch = [pltpu.VMEM(s, f32) for s in carry_shapes]
    else:
        out_shape = [jax.ShapeDtypeStruct(s, f32) for s in carry_shapes]
        if first:
            out_shape.append(jax.ShapeDtypeStruct((GROUP, 2 * HEAD, count), bf16))
    outs = pl.pallas_call(
        functools.partial(attend_kernel, first, last, qb, len(blocks)),
        in_specs=[pl.BlockSpec(memory_space=pltpu.VMEM)] * (1 + len(blocks) + len(carry)),
        out_specs=[pl.BlockSpec(memory_space=pltpu.VMEM)] * len(out_shape),
        out_shape=out_shape,
        scratch_shapes=scratch,
        compiler_params=pltpu.CompilerParams(vmem_limit_bytes=24 * 2**20),
        cost_estimate=pl.CostEstimate(
            flops=GROUP * count * keys * 1, bytes_accessed=1024, transcendentals=0
        ),
    )(queries, *blocks, *carry)
    return outs[0] if last else outs


def finish_kernel(parts_ref, w_ref, out_ref, rows):
    groups = parts_ref.shape[0] // 2
    pieces = []
    for g in range(groups):
        pair = [parts_ref[g], parts_ref[groups + g]]
        logs = []
        for p in pair:
            s = p[WIDE:].astype(f32)
            logs.append((s[0:3] + s[3:6]) + s[6:9])
        top = jnp.maximum(logs[0], logs[1])
        shares = [jnp.exp2(a - top) for a in logs]
        total = shares[0] + shares[1]
        for h in range(GROUP):
            head = slice(HEAD * h, HEAD * (h + 1))
            both = [p[head].astype(f32) * (s[h : h + 1] / total[h : h + 1]) for p, s in zip(pair, shares)]
            pieces.append(both[0] + both[1])
    attended = jnp.concatenate(pieces, 0).T.astype(bf16)
    keep(rows, jnp.dot(attended, w_ref[...], preferred_element_type=f32))
    for r in range(out_ref.shape[0]):
        start = 8 * (r % 2) + r // 2
        out_ref[r] = every_nth(rows, start, 16).astype(bf16)


def finish(parts, w_out):
    shape = (parts.shape[2], w_out.shape[1])
    return pl.pallas_call(
        finish_kernel,
        out_shape=jax.ShapeDtypeStruct((16, 8, shape[1]), bf16),
        scratch_shapes=[pltpu.VMEM((shape[1] // 128, shape[0], 128), f32)],
        compiler_params=pltpu.CompilerParams(vmem_limit_bytes=24 * 2**20),
    )(parts, w_out)


def on_device(patches, norm_gain, w_qkv, pool_q, pool_kv, w_out):
    tokens, last_column, last_row, last_token = normalised_tokens(patches, norm_gain)
    halo = (passed_along(last_row, ROW), passed_along(last_column, COL), corner(last_token))
    own_q, own_kv = project_own(tokens, w_qkv)
    groups = lax.axis_size("y")
    flat = pool_call(keyvals_kernel, own_kv, halo, w_qkv, pool_kv, (groups, 32, 2 * WIDE))
    own = lax.all_to_all(flat, "y", 0, 0, tiled=True).reshape(-1, 2 * WIDE)
    tie = lax.optimization_barrier
    own, own_q = tie((own, own_q))
    line = [own, shifted(own, "zq", 2), shifted(own, "zq", 1), shifted(own, "zq", -1)]
    turned = pool_call(queries_kernel, own_q, halo, w_qkv, pool_q, (2 * groups, WIDE, 128))
    every_query = lax.all_to_all(turned, ("zc", "y"), 0, 0, tiled=True)
    line = jnp.concatenate(line, 0)
    after, before = shifted_x(line, 1), shifted_x(line, -1)
    swap = lambda block: shifted(block, "core", 1)
    *carry, padded = attend(every_query, [line], None)
    carry = attend(padded, [swap(line)], carry)
    after, before, carry = tie((after, before, carry))
    half = line.shape[0] // 2
    far = [shifted_x(after[:half], 1), shifted_x(before[half:], -1)]
    for block in (after, swap(after), before, swap(before)):
        carry = attend(padded, [block], carry)
    far, carry = tie((far, carry))
    swapped = [swap(block) for block in far]
    carry = attend(padded, far, carry)
    partial = attend(padded, swapped, carry, last=True)
    parts = lax.all_to_all(partial, ("zc", "y"), 0, 0, tiled=True)
    return finish(parts, w_out)


def solution(mesh):
    fine = Mesh(mesh.devices.reshape(4, 2, 2, 2, 4, 2), AXES)
    tiles = P(ROW, COL, None)
    return jax.shard_map(
        on_device,
        mesh=fine,
        in_specs=(tiles, P(), P(), P(), P(), P()),
        out_specs=tiles,
        check_vma=False,
    )
```

```python
import functools
import math

import jax
import jax.numpy as jnp
from jax import lax
from jax.experimental import pallas as pl
from jax.experimental.pallas import tpu as pltpu
from jax.sharding import Mesh
from jax.sharding import PartitionSpec as P

AXES = ("zq", "zc", "xl", "xh", "y", "core")
ROW = ("zq", "zc", "xl")
COL = ("xh", "y", "core")
HEAD = 64
GROUP = 3
WIDE = GROUP * HEAD
SCALE = HEAD**-0.5 * math.log2(math.e)
STATS = 16
bf16, f32 = jnp.bfloat16, jnp.float32


def shifted(block, axis, distance):
    count = lax.axis_size(axis)
    return lax.ppermute(block, axis, [(i, (i + distance) % count) for i in range(count)])


def shifted_x(block, distance):
    place = lambda i: (i % 2) * 2 + i // 2
    route = [(place(i), place((i + distance) % 4)) for i in range(4)]
    return lax.ppermute(block, ("xl", "xh"), route)


def passed_along(block, axis):
    count = lax.axis_size(axis)
    return lax.ppermute(block, axis, [(i - 1, i) for i in range(1, count)])


def corner(block):
    rows, cols = lax.axis_size(ROW), lax.axis_size(COL)
    route = [((r - 1) * cols + c - 1, r * cols + c) for r in range(1, rows) for c in range(1, cols)]
    return lax.ppermute(block, AXES, route)


def normalised(values, gain):
    center = values - jnp.mean(values, axis=-1, keepdims=True)
    spread = jnp.mean(center * center, axis=-1, keepdims=True)
    return center * lax.rsqrt(spread + 1e-06) * gain


def project(tokens, weights):
    return jnp.dot(tokens, weights, preferred_element_type=f32).astype(bf16)


ORDER = (0, 1, 3, 4, 5, 7, 8, 9, 11, 12, 13, 2, 6, 10, 14, 15)
KEY_COLUMNS = 11


def keep(plain, values):
    for k in range(plain.shape[0]):
        plain[k] = values[:, 128 * k : 128 * (k + 1)]


def every_nth(plain, start, step):
    picked = [plain[k, pl.ds(start, 8, stride=step), :] for k in range(plain.shape[0])]
    return jnp.concatenate(picked, 1)


def tokens_kernel(patches_ref, gain_ref, tokens_ref, column_ref, row_ref, corner_ref, plain):
    rows, cols, width = patches_ref.shape
    keep(plain, patches_ref[...].astype(f32).reshape(rows * cols, width))
    gain = gain_ref[...].reshape(1, width)
    last = [None] * cols
    for place, c in enumerate(ORDER):
        parts = [every_nth(plain, cols * r + c, 4 * cols) for r in range(4)]
        column = normalised(jnp.concatenate(parts, 0), gain)
        tokens_ref[pl.ds(32 * place, 32), :] = column.astype(bf16)
        last[c] = column[31:]
    column_ref[...] = column.astype(bf16)
    row_ref[...] = jnp.concatenate(last, 0).astype(bf16)
    corner_ref[...] = last[-1].astype(bf16)


def normalised_tokens(patches, gain):
    rows, cols, width = patches.shape
    shapes = [(rows * cols, width), (rows, width), (cols, width), (1, width)]
    return pl.pallas_call(
        tokens_kernel,
        in_specs=[pl.BlockSpec(memory_space=pltpu.VMEM)] * 2,
        out_specs=[pl.BlockSpec(memory_space=pltpu.VMEM)] * 4,
        out_shape=[jax.ShapeDtypeStruct(s, bf16) for s in shapes],
        scratch_shapes=[pltpu.VMEM((width // 128, rows * cols, 128), f32)],
        compiler_params=pltpu.CompilerParams(vmem_limit_bytes=16 * 2**20),
        cost_estimate=pl.CostEstimate(flops=4_000_000_000, bytes_accessed=1_000_000, transcendentals=0),
    )(patches, gain)


def own_kernel(tokens_ref, w_ref, q_ref, kv_ref):
    width = tokens_ref.shape[1]
    few = kv_ref.shape[0]
    for part in range(2):
        cols = slice(part * width, (part + 1) * width)
        kv_ref[:, cols] = project(tokens_ref[:few], w_ref[:, (part + 1) * width : (part + 2) * width])
    q_ref[...] = project(tokens_ref[...], w_ref[:, :width])


def project_own(tokens, w_qkv):
    count, width = tokens.shape
    shapes = [(count, width), (32 * KEY_COLUMNS, 2 * width)]
    return pl.pallas_call(
        own_kernel,
        in_specs=[pl.BlockSpec(memory_space=pltpu.VMEM)] * 2,
        out_specs=[pl.BlockSpec(memory_space=pltpu.VMEM)] * 2,
        out_shape=[jax.ShapeDtypeStruct(s, bf16) for s in shapes],
        compiler_params=pltpu.CompilerParams(vmem_limit_bytes=16 * 2**20),
        cost_estimate=pl.CostEstimate(flops=1_500_000_000, bytes_accessed=4_000_000, transcendentals=0),
    )(tokens, w_qkv)


def halo_tokens(upper_ref, left_ref, corner_ref):
    rest = jnp.zeros((15, left_ref.shape[1]), f32)
    every = [left_ref[...].astype(f32), upper_ref[...].astype(f32), corner_ref[...].astype(f32), rest]
    return jnp.concatenate(every, 0).astype(bf16)


def columns_of(own, halo, columns):
    first = lax.broadcasted_iota(jnp.int32, (8, own.shape[1]), 0) == 0
    groups = {}
    for c in columns:
        if c < 0:
            block, above = halo[0:32], halo[48:49]
        else:
            place = ORDER.index(c)
            block, above = own[32 * place : 32 * place + 32].astype(f32), halo[32 + c : 33 + c]
        four = [block[8 * r : 8 * r + 8] for r in range(4)]
        groups[c] = [jnp.where(first, above, pltpu.roll(four[3], 1, 0))] + four
    return groups


def pooled(groups, taps, column, row):
    total = None
    for a in range(3):
        for b in range(3):
            term = taps[3 * a + b] * groups[column + b - 1][row + a]
            total = term if total is None else total + term
    return total


def keyvals_kernel(own_ref, upper_ref, left_ref, corner_ref, w_ref, pool_ref, out_ref):
    halo_in = halo_tokens(upper_ref, left_ref, corner_ref)
    width = own_ref.shape[1] // 2
    both = []
    for part in range(2):
        cols = pl.ds(part * width, width)
        weights = w_ref[:, (part + 1) * width : (part + 2) * width]
        halo = project(halo_in, weights).astype(f32)
        own = own_ref[:, part * width : (part + 1) * width]
        taps = [pool_ref[t : t + 1, cols] for t in range(9)]
        groups = columns_of(own, halo, (-1,) + ORDER[:KEY_COLUMNS])
        both.append(jnp.concatenate([pooled(groups, taps, 4 * j, 0) for j in range(4)], 0))
    count = width // WIDE
    for g in range(count):
        lanes = slice(g * WIDE, (g + 1) * WIDE)
        block = jnp.concatenate([p[:, lanes] for p in both], 1).astype(bf16)
        for copy in range(out_ref.shape[0] // count):
            out_ref[copy * count + g] = block


def queries_kernel(own_ref, upper_ref, left_ref, corner_ref, w_ref, pool_ref, out_ref):
    width = own_ref.shape[1]
    weights = w_ref[:, :width]
    halo = project(halo_tokens(upper_ref, left_ref, corner_ref), weights).astype(f32)
    own = own_ref[...]
    taps = [pool_ref[t : t + 1, :] for t in range(9)]
    groups = columns_of(own, halo, range(-1, 16))
    rows = [pooled(groups, taps, 2 * j, 2 * p) for j in range(8) for p in range(2)]
    turned = jnp.concatenate(rows, 0).T.astype(bf16)
    count = width // WIDE
    for g in range(count):
        block = turned[g * WIDE : (g + 1) * WIDE]
        for copy in range(out_ref.shape[0] // count):
            out_ref[copy * count + g] = block


def pool_call(kernel, own, halo, w_qkv, taps, out_shape):
    return pl.pallas_call(
        kernel,
        in_specs=[pl.BlockSpec(memory_space=pltpu.VMEM)] * (3 + len(halo)),
        out_specs=pl.BlockSpec(memory_space=pltpu.VMEM),
        out_shape=jax.ShapeDtypeStruct(out_shape, bf16),
        compiler_params=pltpu.CompilerParams(vmem_limit_bytes=24 * 2**20),
        cost_estimate=pl.CostEstimate(flops=200_000_000, bytes_accessed=4_000_000, transcendentals=0),
    )(own, *halo, w_qkv, taps)


def pad_queries(q_ref, padded):
    zero = jnp.zeros((HEAD, 128), bf16)
    for t in range(q_ref.shape[0]):
        lanes = slice(t * 128, (t + 1) * 128)
        for h in range(GROUP):
            here = HEAD * (h % 2)
            padded[h, here : here + HEAD, lanes] = q_ref[t, HEAD * h : HEAD * (h + 1)]
            padded[h, HEAD - here : 2 * HEAD - here, lanes] = zero


def attend_kernel(first, last, qb, blocks, q_ref, *refs):
    block_refs, refs = refs[:blocks], refs[blocks:]
    if first:
        stat, acc, qz = refs
        pad_queries(q_ref, qz)
    else:
        stat_in, acc_in, *refs = refs
        qz = q_ref
        if last:
            out_ref, stat, acc = refs
        else:
            stat, acc = refs
    count = qz.shape[2]
    tiles = count // 128

    jobs = [(j, h) for j in range(count // qb) for h in range(GROUP)]

    def operands():
        block = jnp.concatenate([r[...] for r in block_refs], 0)
        values = block[:, 128:].T
        ones = jnp.ones((16, block.shape[0]), bf16)
        lefts = [jnp.concatenate([values[HEAD * h : HEAD * (h + 1)], ones], 0) for h in range(1, GROUP + 1)]
        return block, lefts

    def scores(block, j, h):
        keys = block[:, 128 * (h // 2) : 128 * (h // 2) + 128]
        return jnp.dot(keys, qz[h, :, j * qb : (j + 1) * qb], preferred_element_type=f32)

    def fold_lazily():
        block, lefts = operands()
        rise = jnp.zeros((1, qb), f32)
        ready = scores(block, *jobs[0])
        for place, (j, h) in enumerate(jobs):
            now = ready
            if place + 1 < len(jobs):
                ready = scores(block, *jobs[place + 1])
            lanes = slice(j * qb, (j + 1) * qb)
            rows = slice(HEAD * h, HEAD * (h + 1))
            old = stat_in[h : h + 1, lanes]
            new = jnp.maximum(old, jnp.max(now, axis=0, keepdims=True))
            rise = jnp.maximum(rise, new - old)
            weights = jnp.exp2((now - old) * SCALE).astype(bf16)
            part = jnp.dot(lefts[h], weights, preferred_element_type=f32)
            factor = jnp.exp2((old - new) * SCALE)
            stat[h : h + 1, lanes] = new
            stat[8 + h : 9 + h, lanes] = (stat_in[8 + h : 9 + h, lanes] + part[HEAD : HEAD + 1]) * factor
            acc[rows, lanes] = (acc_in[rows, lanes] + part[:HEAD]) * factor
        return rise

    def fold(wide):
        @pl.loop(0, count // wide)
        def _(t):
            lanes = pl.ds(pl.multiple_of(t * wide, wide), wide)
            block, lefts = operands()
            for h in range(GROUP):
                rows = slice(HEAD * h, HEAD * (h + 1))
                keys = block[:, 128 * (h // 2) : 128 * (h // 2) + 128]
                now = jnp.dot(keys, qz[h, :, lanes], preferred_element_type=f32)
                new = jnp.max(now, axis=0, keepdims=True)
                if not first:
                    old = stat_in[h : h + 1, lanes]
                    new = jnp.maximum(old, new)
                weights = jnp.exp2((now - new) * SCALE).astype(bf16)
                part = jnp.dot(lefts[h], weights, preferred_element_type=f32)
                total, numer = part[HEAD : HEAD + 1], part[:HEAD]
                if not first:
                    factor = jnp.exp2((old - new) * SCALE)
                    total = stat_in[8 + h : 9 + h, lanes] * factor + total
                    numer = acc_in[rows, lanes] * factor + numer
                stat[h : h + 1, lanes] = new
                stat[8 + h : 9 + h, lanes] = total
                acc[rows, lanes] = numer

    if first:
        fold(qb)
    else:
        rise = fold_lazily()

        @pl.when(jnp.logical_not(jnp.max(rise) * SCALE < 60.0))
        def _():
            fold(128)

    if last:
        total = stat[8 : 8 + GROUP]
        logs = stat[0:GROUP] * SCALE + jnp.log2(total)
        high = logs.astype(bf16)
        left = logs - high.astype(f32)
        middle = left.astype(bf16)
        low = left - middle.astype(f32)
        three = [high.astype(f32), middle.astype(f32), low]
        packed = jnp.concatenate(three + [jnp.zeros((STATS - 9, count), f32)], 0).astype(bf16)
        for t in range(tiles):
            lanes = slice(t * 128, (t + 1) * 128)
            for h in range(GROUP):
                rows = slice(HEAD * h, HEAD * (h + 1))
                out_ref[t, rows] = (acc[rows, lanes] / total[h : h + 1, lanes]).astype(bf16)
            out_ref[t, WIDE:] = packed[:, lanes]


def attend(queries, blocks, carry, last=False, qb=512):
    first = carry is None
    carry = [] if first else carry
    count = queries.shape[0] * 128 if first else queries.shape[2]
    keys = sum(b.shape[0] for b in blocks)
    carry_shapes = [(16, count), (WIDE, count)]
    scratch = []
    if last:
        out_shape = [jax.ShapeDtypeStruct((count // 128, WIDE + STATS, 128), bf16)]
        scratch = [pltpu.VMEM(s, f32) for s in carry_shapes]
    else:
        out_shape = [jax.ShapeDtypeStruct(s, f32) for s in carry_shapes]
        if first:
            out_shape.append(jax.ShapeDtypeStruct((GROUP, 2 * HEAD, count), bf16))
    outs = pl.pallas_call(
        functools.partial(attend_kernel, first, last, qb, len(blocks)),
        in_specs=[pl.BlockSpec(memory_space=pltpu.VMEM)] * (1 + len(blocks) + len(carry)),
        out_specs=[pl.BlockSpec(memory_space=pltpu.VMEM)] * len(out_shape),
        out_shape=out_shape,
        scratch_shapes=scratch,
        compiler_params=pltpu.CompilerParams(vmem_limit_bytes=24 * 2**20),
        cost_estimate=pl.CostEstimate(
            flops=GROUP * count * keys * 1, bytes_accessed=1024, transcendentals=0
        ),
    )(queries, *blocks, *carry)
    return outs[0] if last else outs


def finish_kernel(parts_ref, w_ref, out_ref, rows):
    groups = parts_ref.shape[0] // 2
    pieces = []
    for g in range(groups):
        pair = [parts_ref[g], parts_ref[groups + g]]
        logs = []
        for p in pair:
            s = p[WIDE:].astype(f32)
            logs.append((s[0:3] + s[3:6]) + s[6:9])
        top = jnp.maximum(logs[0], logs[1])
        shares = [jnp.exp2(a - top) for a in logs]
        total = shares[0] + shares[1]
        for h in range(GROUP):
            head = slice(HEAD * h, HEAD * (h + 1))
            both = [p[head].astype(f32) * (s[h : h + 1] / total[h : h + 1]) for p, s in zip(pair, shares)]
            pieces.append(both[0] + both[1])
    attended = jnp.concatenate(pieces, 0).T.astype(bf16)
    keep(rows, jnp.dot(attended, w_ref[...], preferred_element_type=f32))
    for r in range(out_ref.shape[0]):
        start = 8 * (r % 2) + r // 2
        out_ref[r] = every_nth(rows, start, 16).astype(bf16)


def finish(parts, w_out):
    shape = (parts.shape[2], w_out.shape[1])
    return pl.pallas_call(
        finish_kernel,
        out_shape=jax.ShapeDtypeStruct((16, 8, shape[1]), bf16),
        scratch_shapes=[pltpu.VMEM((shape[1] // 128, shape[0], 128), f32)],
        compiler_params=pltpu.CompilerParams(vmem_limit_bytes=24 * 2**20),
    )(parts, w_out)


def on_device(patches, norm_gain, w_qkv, pool_q, pool_kv, w_out):
    tokens, last_column, last_row, last_token = normalised_tokens(patches, norm_gain)
    halo = (passed_along(last_row, ROW), passed_along(last_column, COL), corner(last_token))
    own_q, own_kv = project_own(tokens, w_qkv)
    groups = lax.axis_size("y")
    flat = pool_call(keyvals_kernel, own_kv, halo, w_qkv, pool_kv, (groups, 32, 2 * WIDE))
    own = lax.all_to_all(flat, "y", 0, 0, tiled=True).reshape(-1, 2 * WIDE)
    tie = lax.optimization_barrier
    own, own_q = tie((own, own_q))
    line = [own, shifted(own, "zq", 2), shifted(own, "zq", 1), shifted(own, "zq", -1)]
    turned = pool_call(queries_kernel, own_q, halo, w_qkv, pool_q, (2 * groups, WIDE, 128))
    every_query = lax.all_to_all(turned, ("zc", "y"), 0, 0, tiled=True)
    line = jnp.concatenate(line, 0)
    after, before = shifted_x(line, 1), shifted_x(line, -1)
    swap = lambda block: shifted(block, "core", 1)
    *carry, padded = attend(every_query, [line], None)
    carry = attend(padded, [swap(line)], carry)
    after, before, carry = tie((after, before, carry))
    half = line.shape[0] // 2
    far = [shifted_x(after[:half], 1), shifted_x(before[half:], -1)]
    for block in (after, swap(after), before, swap(before)):
        carry = attend(padded, [block], carry)
    far, carry = tie((far, carry))
    swapped = [swap(block) for block in far]
    carry = attend(padded, far, carry)
    partial = attend(padded, swapped, carry, last=True)
    parts = lax.all_to_all(partial, ("zc", "y"), 0, 0, tiled=True)
    return finish(parts, w_out)


def solution(mesh):
    fine = Mesh(mesh.devices.reshape(4, 2, 2, 2, 4, 2), AXES)
    tiles = P(ROW, COL, None)
    return jax.shard_map(
        on_device,
        mesh=fine,
        in_specs=(tiles, P(), P(), P(), P(), P()),
        out_specs=tiles,
        check_vma=False,
    )
```

```python
import functools
import math

import jax
import jax.numpy as jnp
from jax import lax
from jax.experimental import pallas as pl
from jax.experimental.pallas import tpu as pltpu
from jax.sharding import Mesh
from jax.sharding import PartitionSpec as P

AXES = ("zq", "zc", "xl", "xh", "y", "core")
ROW = ("zq", "zc", "xl")
COL = ("xh", "y", "core")
HEAD = 64
GROUP = 3
WIDE = GROUP * HEAD
SCALE = HEAD**-0.5 * math.log2(math.e)
STATS = 16
bf16, f32 = jnp.bfloat16, jnp.float32


def shifted(block, axis, distance):
    count = lax.axis_size(axis)
    return lax.ppermute(block, axis, [(i, (i + distance) % count) for i in range(count)])


def shifted_x(block, distance):
    place = lambda i: (i % 2) * 2 + i // 2
    route = [(place(i), place((i + distance) % 4)) for i in range(4)]
    return lax.ppermute(block, ("xl", "xh"), route)


def passed_along(block, axis):
    count = lax.axis_size(axis)
    return lax.ppermute(block, axis, [(i - 1, i) for i in range(1, count)])


def corner(block):
    rows, cols = lax.axis_size(ROW), lax.axis_size(COL)
    route = [((r - 1) * cols + c - 1, r * cols + c) for r in range(1, rows) for c in range(1, cols)]
    return lax.ppermute(block, AXES, route)


def normalised(values, gain):
    center = values - jnp.mean(values, axis=-1, keepdims=True)
    spread = jnp.mean(center * center, axis=-1, keepdims=True)
    return center * lax.rsqrt(spread + 1e-06) * gain


def project(tokens, weights):
    return jnp.dot(tokens, weights, preferred_element_type=f32).astype(bf16)


ORDER = (0, 1, 3, 4, 5, 7, 8, 9, 11, 12, 13, 2, 6, 10, 14, 15)
KEY_COLUMNS = 11


def keep(plain, values):
    for k in range(plain.shape[0]):
        plain[k] = values[:, 128 * k : 128 * (k + 1)]


def every_nth(plain, start, step):
    picked = [plain[k, pl.ds(start, 8, stride=step), :] for k in range(plain.shape[0])]
    return jnp.concatenate(picked, 1)


def tokens_kernel(patches_ref, gain_ref, tokens_ref, column_ref, row_ref, corner_ref, plain):
    rows, cols, width = patches_ref.shape
    keep(plain, patches_ref[...].astype(f32).reshape(rows * cols, width))
    gain = gain_ref[...].reshape(1, width)
    last = [None] * cols
    for place, c in enumerate(ORDER):
        parts = [every_nth(plain, cols * r + c, 4 * cols) for r in range(4)]
        column = normalised(jnp.concatenate(parts, 0), gain)
        tokens_ref[pl.ds(32 * place, 32), :] = column.astype(bf16)
        last[c] = column[31:]
    column_ref[...] = column.astype(bf16)
    row_ref[...] = jnp.concatenate(last, 0).astype(bf16)
    corner_ref[...] = last[-1].astype(bf16)


def normalised_tokens(patches, gain):
    rows, cols, width = patches.shape
    shapes = [(rows * cols, width), (rows, width), (cols, width), (1, width)]
    return pl.pallas_call(
        tokens_kernel,
        in_specs=[pl.BlockSpec(memory_space=pltpu.VMEM)] * 2,
        out_specs=[pl.BlockSpec(memory_space=pltpu.VMEM)] * 4,
        out_shape=[jax.ShapeDtypeStruct(s, bf16) for s in shapes],
        scratch_shapes=[pltpu.VMEM((width // 128, rows * cols, 128), f32)],
        compiler_params=pltpu.CompilerParams(vmem_limit_bytes=16 * 2**20),
        cost_estimate=pl.CostEstimate(flops=4_000_000_000, bytes_accessed=1_000_000, transcendentals=0),
    )(patches, gain)


def own_kernel(tokens_ref, w_ref, q_ref, kv_ref):
    width = tokens_ref.shape[1]
    few = kv_ref.shape[0]
    for part in range(2):
        cols = slice(part * width, (part + 1) * width)
        kv_ref[:, cols] = project(tokens_ref[:few], w_ref[:, (part + 1) * width : (part + 2) * width])
    q_ref[...] = project(tokens_ref[...], w_ref[:, :width])


def project_own(tokens, w_qkv):
    count, width = tokens.shape
    shapes = [(count, width), (32 * KEY_COLUMNS, 2 * width)]
    return pl.pallas_call(
        own_kernel,
        in_specs=[pl.BlockSpec(memory_space=pltpu.VMEM)] * 2,
        out_specs=[pl.BlockSpec(memory_space=pltpu.VMEM)] * 2,
        out_shape=[jax.ShapeDtypeStruct(s, bf16) for s in shapes],
        compiler_params=pltpu.CompilerParams(vmem_limit_bytes=16 * 2**20),
        cost_estimate=pl.CostEstimate(flops=1_500_000_000, bytes_accessed=4_000_000, transcendentals=0),
    )(tokens, w_qkv)


def halo_tokens(upper_ref, left_ref, corner_ref):
    rest = jnp.zeros((15, left_ref.shape[1]), f32)
    every = [left_ref[...].astype(f32), upper_ref[...].astype(f32), corner_ref[...].astype(f32), rest]
    return jnp.concatenate(every, 0).astype(bf16)


def columns_of(own, halo, columns):
    first = lax.broadcasted_iota(jnp.int32, (8, own.shape[1]), 0) == 0
    groups = {}
    for c in columns:
        if c < 0:
            block, above = halo[0:32], halo[48:49]
        else:
            place = ORDER.index(c)
            block, above = own[32 * place : 32 * place + 32].astype(f32), halo[32 + c : 33 + c]
        four = [block[8 * r : 8 * r + 8] for r in range(4)]
        groups[c] = [jnp.where(first, above, pltpu.roll(four[3], 1, 0))] + four
    return groups


def pooled(groups, taps, column, row):
    total = None
    for a in range(3):
        for b in range(3):
            term = taps[3 * a + b] * groups[column + b - 1][row + a]
            total = term if total is None else total + term
    return total


def keyvals_kernel(here_ref, own_ref, upper_ref, left_ref, corner_ref, w_ref, pool_ref, *refs):
    out_refs, parts = refs[:-1], refs[-1]
    halo_in = halo_tokens(upper_ref, left_ref, corner_ref)
    width = own_ref.shape[1] // 2
    both = []
    for part in range(2):
        cols = pl.ds(part * width, width)
        weights = w_ref[:, (part + 1) * width : (part + 2) * width]
        halo = project(halo_in, weights).astype(f32)
        own = own_ref[:, part * width : (part + 1) * width]
        taps = [pool_ref[t : t + 1, cols] for t in range(9)]
        groups = columns_of(own, halo, (-1,) + ORDER[:KEY_COLUMNS])
        both.append(jnp.concatenate([pooled(groups, taps, 4 * j, 0) for j in range(4)], 0))
    count = width // WIDE
    for g in range(count):
        lanes = slice(g * WIDE, (g + 1) * WIDE)
        parts[g] = jnp.concatenate([p[:, lanes] for p in both], 1).astype(bf16)
    here = here_ref[0]
    for distance, out_ref in enumerate(out_refs):
        out_ref[...] = parts[lax.rem(here + distance, count)]


def queries_kernel(own_ref, upper_ref, left_ref, corner_ref, w_ref, pool_ref, out_ref):
    width = own_ref.shape[1]
    weights = w_ref[:, :width]
    halo = project(halo_tokens(upper_ref, left_ref, corner_ref), weights).astype(f32)
    own = own_ref[...]
    taps = [pool_ref[t : t + 1, :] for t in range(9)]
    groups = columns_of(own, halo, range(-1, 16))
    rows = [pooled(groups, taps, 2 * j, 2 * p) for j in range(8) for p in range(2)]
    turned = jnp.concatenate(rows, 0).T.astype(bf16)
    count = width // WIDE
    for g in range(count):
        block = turned[g * WIDE : (g + 1) * WIDE]
        for copy in range(out_ref.shape[0] // count):
            out_ref[copy * count + g] = block


def pool_call(kernel, own, halo, w_qkv, taps, out_shapes, scratch=(), scalars=()):
    return pl.pallas_call(
        kernel,
        in_specs=[pl.BlockSpec(memory_space=pltpu.SMEM)] * len(scalars)
        + [pl.BlockSpec(memory_space=pltpu.VMEM)] * (3 + len(halo)),
        out_specs=[pl.BlockSpec(memory_space=pltpu.VMEM)] * len(out_shapes),
        out_shape=[jax.ShapeDtypeStruct(s, bf16) for s in out_shapes],
        scratch_shapes=[pltpu.VMEM(s, bf16) for s in scratch],
        compiler_params=pltpu.CompilerParams(vmem_limit_bytes=24 * 2**20),
        cost_estimate=pl.CostEstimate(flops=200_000_000, bytes_accessed=4_000_000, transcendentals=0),
    )(*scalars, own, *halo, w_qkv, taps)


def pad_queries(q_ref, padded):
    zero = jnp.zeros((HEAD, 128), bf16)
    for t in range(q_ref.shape[0]):
        lanes = slice(t * 128, (t + 1) * 128)
        for h in range(GROUP):
            here = HEAD * (h % 2)
            padded[h, here : here + HEAD, lanes] = q_ref[t, HEAD * h : HEAD * (h + 1)]
            padded[h, HEAD - here : 2 * HEAD - here, lanes] = zero


def attend_kernel(first, last, qb, blocks, q_ref, *refs):
    block_refs, refs = refs[:blocks], refs[blocks:]
    if first:
        stat, acc, qz = refs
        pad_queries(q_ref, qz)
    else:
        stat_in, acc_in, *refs = refs
        qz = q_ref
        if last:
            out_ref, stat, acc = refs
        else:
            stat, acc = refs
    count = qz.shape[2]
    tiles = count // 128

    jobs = [(j, h) for j in range(count // qb) for h in range(GROUP)]

    def operands():
        block = jnp.concatenate([r[...] for r in block_refs], 0)
        values = block[:, 128:].T
        ones = jnp.ones((16, block.shape[0]), bf16)
        lefts = [jnp.concatenate([values[HEAD * h : HEAD * (h + 1)], ones], 0) for h in range(1, GROUP + 1)]
        return block, lefts

    def scores(block, j, h):
        keys = block[:, 128 * (h // 2) : 128 * (h // 2) + 128]
        return jnp.dot(keys, qz[h, :, j * qb : (j + 1) * qb], preferred_element_type=f32)

    def fold_lazily():
        block, lefts = operands()
        rise = jnp.zeros((1, qb), f32)
        ready = scores(block, *jobs[0])
        for place, (j, h) in enumerate(jobs):
            now = ready
            if place + 1 < len(jobs):
                ready = scores(block, *jobs[place + 1])
            lanes = slice(j * qb, (j + 1) * qb)
            rows = slice(HEAD * h, HEAD * (h + 1))
            old = stat_in[h : h + 1, lanes]
            new = jnp.maximum(old, jnp.max(now, axis=0, keepdims=True))
            rise = jnp.maximum(rise, new - old)
            weights = jnp.exp2((now - old) * SCALE).astype(bf16)
            part = jnp.dot(lefts[h], weights, preferred_element_type=f32)
            factor = jnp.exp2((old - new) * SCALE)
            stat[h : h + 1, lanes] = new
            stat[8 + h : 9 + h, lanes] = (stat_in[8 + h : 9 + h, lanes] + part[HEAD : HEAD + 1]) * factor
            acc[rows, lanes] = (acc_in[rows, lanes] + part[:HEAD]) * factor
        return rise

    def fold(wide):
        @pl.loop(0, count // wide)
        def _(t):
            lanes = pl.ds(pl.multiple_of(t * wide, wide), wide)
            block, lefts = operands()
            for h in range(GROUP):
                rows = slice(HEAD * h, HEAD * (h + 1))
                keys = block[:, 128 * (h // 2) : 128 * (h // 2) + 128]
                now = jnp.dot(keys, qz[h, :, lanes], preferred_element_type=f32)
                new = jnp.max(now, axis=0, keepdims=True)
                if not first:
                    old = stat_in[h : h + 1, lanes]
                    new = jnp.maximum(old, new)
                weights = jnp.exp2((now - new) * SCALE).astype(bf16)
                part = jnp.dot(lefts[h], weights, preferred_element_type=f32)
                total, numer = part[HEAD : HEAD + 1], part[:HEAD]
                if not first:
                    factor = jnp.exp2((old - new) * SCALE)
                    total = stat_in[8 + h : 9 + h, lanes] * factor + total
                    numer = acc_in[rows, lanes] * factor + numer
                stat[h : h + 1, lanes] = new
                stat[8 + h : 9 + h, lanes] = total
                acc[rows, lanes] = numer

    if first:
        fold(qb)
    else:
        rise = fold_lazily()

        @pl.when(jnp.logical_not(jnp.max(rise) * SCALE < 60.0))
        def _():
            fold(128)

    if last:
        total = stat[8 : 8 + GROUP]
        logs = stat[0:GROUP] * SCALE + jnp.log2(total)
        high = logs.astype(bf16)
        left = logs - high.astype(f32)
        middle = left.astype(bf16)
        low = left - middle.astype(f32)
        three = [high.astype(f32), middle.astype(f32), low]
        packed = jnp.concatenate(three + [jnp.zeros((STATS - 9, count), f32)], 0).astype(bf16)
        for t in range(tiles):
            lanes = slice(t * 128, (t + 1) * 128)
            for h in range(GROUP):
                rows = slice(HEAD * h, HEAD * (h + 1))
                out_ref[t, rows] = (acc[rows, lanes] / total[h : h + 1, lanes]).astype(bf16)
            out_ref[t, WIDE:] = packed[:, lanes]


def attend(queries, blocks, carry, last=False, qb=512):
    first = carry is None
    carry = [] if first else carry
    count = queries.shape[0] * 128 if first else queries.shape[2]
    keys = sum(b.shape[0] for b in blocks)
    carry_shapes = [(16, count), (WIDE, count)]
    scratch = []
    if last:
        out_shape = [jax.ShapeDtypeStruct((count // 128, WIDE + STATS, 128), bf16)]
        scratch = [pltpu.VMEM(s, f32) for s in carry_shapes]
    else:
        out_shape = [jax.ShapeDtypeStruct(s, f32) for s in carry_shapes]
        if first:
            out_shape.append(jax.ShapeDtypeStruct((GROUP, 2 * HEAD, count), bf16))
    outs = pl.pallas_call(
        functools.partial(attend_kernel, first, last, qb, len(blocks)),
        in_specs=[pl.BlockSpec(memory_space=pltpu.VMEM)] * (1 + len(blocks) + len(carry)),
        out_specs=[pl.BlockSpec(memory_space=pltpu.VMEM)] * len(out_shape),
        out_shape=out_shape,
        scratch_shapes=scratch,
        compiler_params=pltpu.CompilerParams(vmem_limit_bytes=24 * 2**20),
        cost_estimate=pl.CostEstimate(
            flops=GROUP * count * keys * 1, bytes_accessed=1024, transcendentals=0
        ),
    )(queries, *blocks, *carry)
    return outs[0] if last else outs


def finish_kernel(parts_ref, w_ref, out_ref, rows):
    groups = parts_ref.shape[0] // 2
    pieces = []
    for g in range(groups):
        pair = [parts_ref[g], parts_ref[groups + g]]
        logs = []
        for p in pair:
            s = p[WIDE:].astype(f32)
            logs.append((s[0:3] + s[3:6]) + s[6:9])
        top = jnp.maximum(logs[0], logs[1])
        shares = [jnp.exp2(a - top) for a in logs]
        total = shares[0] + shares[1]
        for h in range(GROUP):
            head = slice(HEAD * h, HEAD * (h + 1))
            both = [p[head].astype(f32) * (s[h : h + 1] / total[h : h + 1]) for p, s in zip(pair, shares)]
            pieces.append(both[0] + both[1])
    attended = jnp.concatenate(pieces, 0).T.astype(bf16)
    keep(rows, jnp.dot(attended, w_ref[...], preferred_element_type=f32))
    for r in range(out_ref.shape[0]):
        start = 8 * (r % 2) + r // 2
        out_ref[r] = every_nth(rows, start, 16).astype(bf16)


def finish(parts, w_out):
    shape = (parts.shape[2], w_out.shape[1])
    return pl.pallas_call(
        finish_kernel,
        out_shape=jax.ShapeDtypeStruct((16, 8, shape[1]), bf16),
        scratch_shapes=[pltpu.VMEM((shape[1] // 128, shape[0], 128), f32)],
        compiler_params=pltpu.CompilerParams(vmem_limit_bytes=24 * 2**20),
    )(parts, w_out)


def on_device(patches, norm_gain, w_qkv, pool_q, pool_kv, w_out):
    here = [lax.axis_index("y").reshape(1)]
    patches, here = lax.optimization_barrier((patches, here))
    tokens, last_column, last_row, last_token = normalised_tokens(patches, norm_gain)
    halo = (passed_along(last_row, ROW), passed_along(last_column, COL), corner(last_token))
    own_q, own_kv = project_own(tokens, w_qkv)
    groups = lax.axis_size("y")
    part = (32, 2 * WIDE)
    parts = pool_call(keyvals_kernel, own_kv, halo, w_qkv, pool_kv, [part] * groups, [(groups, *part)], here)
    own = jnp.concatenate([parts[0]] + [shifted(p, "y", d) for d, p in enumerate(parts) if d], 0)
    tie = lax.optimization_barrier
    own, own_q = tie((own, own_q))
    line = [own, shifted(own, "zq", 2), shifted(own, "zq", 1), shifted(own, "zq", -1)]
    (turned,) = pool_call(queries_kernel, own_q, halo, w_qkv, pool_q, [(2 * groups, WIDE, 128)])
    every_query = lax.all_to_all(turned, ("zc", "y"), 0, 0, tiled=True)
    line = jnp.concatenate(line, 0)
    after, before = shifted_x(line, 1), shifted_x(line, -1)
    swap = lambda block: shifted(block, "core", 1)
    *carry, padded = attend(every_query, [line], None)
    carry = attend(padded, [swap(line)], carry)
    after, before, carry = tie((after, before, carry))
    half = line.shape[0] // 2
    far = [shifted_x(after[:half], 1), shifted_x(before[half:], -1)]
    for block in (after, swap(after), before, swap(before)):
        carry = attend(padded, [block], carry)
    far, carry = tie((far, carry))
    swapped = [swap(block) for block in far]
    carry = attend(padded, far, carry)
    partial = attend(padded, swapped, carry, last=True)
    parts = lax.all_to_all(partial, ("zc", "y"), 0, 0, tiled=True)
    return finish(parts, w_out)


def solution(mesh):
    fine = Mesh(mesh.devices.reshape(4, 2, 2, 2, 4, 2), AXES)
    tiles = P(ROW, COL, None)
    return jax.shard_map(
        on_device,
        mesh=fine,
        in_specs=(tiles, P(), P(), P(), P(), P()),
        out_specs=tiles,
        check_vma=False,
    )
```

```python
import functools
import math

import jax
import jax.numpy as jnp
from jax import lax
from jax.experimental import pallas as pl
from jax.experimental.pallas import tpu as pltpu
from jax.sharding import Mesh
from jax.sharding import PartitionSpec as P

AXES = ("zq", "zc", "xl", "xh", "y", "core")
ROW = ("zq", "zc", "xl")
COL = ("xh", "y", "core")
HEAD = 64
GROUP = 3
WIDE = GROUP * HEAD
SCALE = HEAD**-0.5 * math.log2(math.e)
STATS = 16
bf16, f32 = jnp.bfloat16, jnp.float32


def shifted(block, axis, distance):
    count = lax.axis_size(axis)
    return lax.ppermute(block, axis, [(i, (i + distance) % count) for i in range(count)])


def shifted_x(block, distance):
    place = lambda i: (i % 2) * 2 + i // 2
    route = [(place(i), place((i + distance) % 4)) for i in range(4)]
    return lax.ppermute(block, ("xl", "xh"), route)


def passed_along(block, axis):
    count = lax.axis_size(axis)
    return lax.ppermute(block, axis, [(i - 1, i) for i in range(1, count)])


def corner(block):
    rows, cols = lax.axis_size(ROW), lax.axis_size(COL)
    route = [((r - 1) * cols + c - 1, r * cols + c) for r in range(1, rows) for c in range(1, cols)]
    return lax.ppermute(block, AXES, route)


def normalised(values, gain):
    center = values - jnp.mean(values, axis=-1, keepdims=True)
    spread = jnp.mean(center * center, axis=-1, keepdims=True)
    return center * lax.rsqrt(spread + 1e-06) * gain


def project(tokens, weights):
    return jnp.dot(tokens, weights, preferred_element_type=f32).astype(bf16)


ORDER = (0, 1, 3, 4, 5, 7, 8, 9, 11, 12, 13, 2, 6, 10, 14, 15)
KEY_COLUMNS = 11


def keep(plain, values):
    for k in range(plain.shape[0]):
        plain[k] = values[:, 128 * k : 128 * (k + 1)]


def every_nth(plain, start, step):
    picked = [plain[k, pl.ds(start, 8, stride=step), :] for k in range(plain.shape[0])]
    return jnp.concatenate(picked, 1)


def tokens_kernel(patches_ref, gain_ref, tokens_ref, column_ref, row_ref, corner_ref, plain):
    rows, cols, width = patches_ref.shape
    keep(plain, patches_ref[...].astype(f32).reshape(rows * cols, width))
    gain = gain_ref[...].reshape(1, width)
    last = [None] * cols
    for place, c in enumerate(ORDER):
        parts = [every_nth(plain, cols * r + c, 4 * cols) for r in range(4)]
        column = normalised(jnp.concatenate(parts, 0), gain)
        tokens_ref[pl.ds(32 * place, 32), :] = column.astype(bf16)
        last[c] = column[31:]
    column_ref[...] = column.astype(bf16)
    row_ref[...] = jnp.concatenate(last, 0).astype(bf16)
    corner_ref[...] = last[-1].astype(bf16)


def normalised_tokens(patches, gain):
    rows, cols, width = patches.shape
    shapes = [(rows * cols, width), (rows, width), (cols, width), (1, width)]
    return pl.pallas_call(
        tokens_kernel,
        in_specs=[pl.BlockSpec(memory_space=pltpu.VMEM)] * 2,
        out_specs=[pl.BlockSpec(memory_space=pltpu.VMEM)] * 4,
        out_shape=[jax.ShapeDtypeStruct(s, bf16) for s in shapes],
        scratch_shapes=[pltpu.VMEM((width // 128, rows * cols, 128), f32)],
        compiler_params=pltpu.CompilerParams(vmem_limit_bytes=16 * 2**20),
        cost_estimate=pl.CostEstimate(flops=4_000_000_000, bytes_accessed=1_000_000, transcendentals=0),
    )(patches, gain)


def own_kernel(tokens_ref, w_ref, q_ref, kv_ref):
    width = tokens_ref.shape[1]
    few = kv_ref.shape[0]
    for part in range(2):
        cols = slice(part * width, (part + 1) * width)
        kv_ref[:, cols] = project(tokens_ref[:few], w_ref[:, (part + 1) * width : (part + 2) * width])
    q_ref[...] = project(tokens_ref[...], w_ref[:, :width])


def project_own(tokens, w_qkv):
    count, width = tokens.shape
    shapes = [(count, width), (32 * KEY_COLUMNS, 2 * width)]
    return pl.pallas_call(
        own_kernel,
        in_specs=[pl.BlockSpec(memory_space=pltpu.VMEM)] * 2,
        out_specs=[pl.BlockSpec(memory_space=pltpu.VMEM)] * 2,
        out_shape=[jax.ShapeDtypeStruct(s, bf16) for s in shapes],
        compiler_params=pltpu.CompilerParams(vmem_limit_bytes=16 * 2**20),
        cost_estimate=pl.CostEstimate(flops=1_500_000_000, bytes_accessed=4_000_000, transcendentals=0),
    )(tokens, w_qkv)


def halo_tokens(upper_ref, left_ref, corner_ref):
    rest = jnp.zeros((15, left_ref.shape[1]), f32)
    every = [left_ref[...].astype(f32), upper_ref[...].astype(f32), corner_ref[...].astype(f32), rest]
    return jnp.concatenate(every, 0).astype(bf16)


def columns_of(own, halo, columns):
    first = lax.broadcasted_iota(jnp.int32, (8, own.shape[1]), 0) == 0
    groups = {}
    for c in columns:
        if c < 0:
            block, above = halo[0:32], halo[48:49]
        else:
            place = ORDER.index(c)
            block, above = own[32 * place : 32 * place + 32].astype(f32), halo[32 + c : 33 + c]
        four = [block[8 * r : 8 * r + 8] for r in range(4)]
        groups[c] = [jnp.where(first, above, pltpu.roll(four[3], 1, 0))] + four
    return groups


def pooled(groups, taps, column, row):
    total = None
    for a in range(3):
        for b in range(3):
            term = taps[3 * a + b] * groups[column + b - 1][row + a]
            total = term if total is None else total + term
    return total


def keyvals_kernel(here_ref, own_ref, upper_ref, left_ref, corner_ref, w_ref, pool_ref, *refs):
    out_refs, parts = refs[:-1], refs[-1]
    halo_in = halo_tokens(upper_ref, left_ref, corner_ref)
    width = own_ref.shape[1] // 2
    both = []
    for part in range(2):
        cols = pl.ds(part * width, width)
        weights = w_ref[:, (part + 1) * width : (part + 2) * width]
        halo = project(halo_in, weights).astype(f32)
        own = own_ref[:, part * width : (part + 1) * width]
        taps = [pool_ref[t : t + 1, cols] for t in range(9)]
        groups = columns_of(own, halo, (-1,) + ORDER[:KEY_COLUMNS])
        both.append(jnp.concatenate([pooled(groups, taps, 4 * j, 0) for j in range(4)], 0))
    count = width // WIDE
    for g in range(count):
        lanes = slice(g * WIDE, (g + 1) * WIDE)
        parts[g] = jnp.concatenate([p[:, lanes] for p in both], 1).astype(bf16)
    here = here_ref[0]
    for distance, out_ref in enumerate(out_refs):
        out_ref[...] = parts[lax.rem(here + distance, count)]


def queries_kernel(own_ref, upper_ref, left_ref, corner_ref, w_ref, pool_ref, out_ref):
    width = own_ref.shape[1]
    weights = w_ref[:, :width]
    halo = project(halo_tokens(upper_ref, left_ref, corner_ref), weights).astype(f32)
    own = own_ref[...]
    taps = [pool_ref[t : t + 1, :] for t in range(9)]
    groups = columns_of(own, halo, range(-1, 16))
    rows = [pooled(groups, taps, 2 * j, 2 * p) for j in range(8) for p in range(2)]
    turned = jnp.concatenate(rows, 0).T.astype(bf16)
    count = width // WIDE
    for g in range(count):
        block = turned[g * WIDE : (g + 1) * WIDE]
        for copy in range(out_ref.shape[0] // count):
            out_ref[copy * count + g] = block


def pool_call(kernel, own, halo, w_qkv, taps, out_shapes, scratch=(), scalars=()):
    return pl.pallas_call(
        kernel,
        in_specs=[pl.BlockSpec(memory_space=pltpu.SMEM)] * len(scalars)
        + [pl.BlockSpec(memory_space=pltpu.VMEM)] * (3 + len(halo)),
        out_specs=[pl.BlockSpec(memory_space=pltpu.VMEM)] * len(out_shapes),
        out_shape=[jax.ShapeDtypeStruct(s, bf16) for s in out_shapes],
        scratch_shapes=[pltpu.VMEM(s, bf16) for s in scratch],
        compiler_params=pltpu.CompilerParams(vmem_limit_bytes=24 * 2**20),
        cost_estimate=pl.CostEstimate(flops=200_000_000, bytes_accessed=4_000_000, transcendentals=0),
    )(*scalars, own, *halo, w_qkv, taps)


def pad_queries(q_ref, padded):
    zero = jnp.zeros((HEAD, 128), bf16)
    for t in range(q_ref.shape[0]):
        lanes = slice(t * 128, (t + 1) * 128)
        for h in range(GROUP):
            here = HEAD * (h % 2)
            padded[h, here : here + HEAD, lanes] = q_ref[t, HEAD * h : HEAD * (h + 1)]
            padded[h, HEAD - here : 2 * HEAD - here, lanes] = zero


def attend_kernel(first, last, qb, blocks, q_ref, *refs):
    block_refs, refs = refs[:blocks], refs[blocks:]
    if first:
        stat, acc, qz = refs
        pad_queries(q_ref, qz)
    else:
        stat_in, acc_in, *refs = refs
        qz = q_ref
        if last:
            out_ref, stat, acc = refs
        else:
            stat, acc = refs
    count = qz.shape[2]
    tiles = count // 128

    jobs = [(j, h) for j in range(count // qb) for h in range(GROUP)]

    def operands():
        block = jnp.concatenate([r[...] for r in block_refs], 0)
        values = block[:, 128:].T
        ones = jnp.ones((16, block.shape[0]), bf16)
        lefts = [jnp.concatenate([values[HEAD * h : HEAD * (h + 1)], ones], 0) for h in range(1, GROUP + 1)]
        return block, lefts

    def scores(block, j, h):
        keys = block[:, 128 * (h // 2) : 128 * (h // 2) + 128]
        return jnp.dot(keys, qz[h, :, j * qb : (j + 1) * qb], preferred_element_type=f32)

    def fold_lazily():
        block, lefts = operands()
        rise = jnp.zeros((1, qb), f32)
        ready = scores(block, *jobs[0])
        for place, (j, h) in enumerate(jobs):
            now = ready
            if place + 1 < len(jobs):
                ready = scores(block, *jobs[place + 1])
            lanes = slice(j * qb, (j + 1) * qb)
            rows = slice(HEAD * h, HEAD * (h + 1))
            old = stat_in[h : h + 1, lanes]
            new = jnp.maximum(old, jnp.max(now, axis=0, keepdims=True))
            rise = jnp.maximum(rise, new - old)
            weights = jnp.exp2((now - old) * SCALE).astype(bf16)
            part = jnp.dot(lefts[h], weights, preferred_element_type=f32)
            factor = jnp.exp2((old - new) * SCALE)
            stat[h : h + 1, lanes] = new
            stat[8 + h : 9 + h, lanes] = (stat_in[8 + h : 9 + h, lanes] + part[HEAD : HEAD + 1]) * factor
            acc[rows, lanes] = (acc_in[rows, lanes] + part[:HEAD]) * factor
        return rise

    def fold(wide):
        @pl.loop(0, count // wide)
        def _(t):
            lanes = pl.ds(pl.multiple_of(t * wide, wide), wide)
            block, lefts = operands()
            for h in range(GROUP):
                rows = slice(HEAD * h, HEAD * (h + 1))
                keys = block[:, 128 * (h // 2) : 128 * (h // 2) + 128]
                now = jnp.dot(keys, qz[h, :, lanes], preferred_element_type=f32)
                new = jnp.max(now, axis=0, keepdims=True)
                if not first:
                    old = stat_in[h : h + 1, lanes]
                    new = jnp.maximum(old, new)
                weights = jnp.exp2((now - new) * SCALE).astype(bf16)
                part = jnp.dot(lefts[h], weights, preferred_element_type=f32)
                total, numer = part[HEAD : HEAD + 1], part[:HEAD]
                if not first:
                    factor = jnp.exp2((old - new) * SCALE)
                    total = stat_in[8 + h : 9 + h, lanes] * factor + total
                    numer = acc_in[rows, lanes] * factor + numer
                stat[h : h + 1, lanes] = new
                stat[8 + h : 9 + h, lanes] = total
                acc[rows, lanes] = numer

    if first:
        fold(qb)
    else:
        rise = fold_lazily()

        @pl.when(jnp.logical_not(jnp.max(rise) * SCALE < 60.0))
        def _():
            fold(128)

    if last:
        total = stat[8 : 8 + GROUP]
        logs = stat[0:GROUP] * SCALE + jnp.log2(total)
        high = logs.astype(bf16)
        left = logs - high.astype(f32)
        middle = left.astype(bf16)
        low = left - middle.astype(f32)
        three = [high.astype(f32), middle.astype(f32), low]
        packed = jnp.concatenate(three + [jnp.zeros((STATS - 9, count), f32)], 0).astype(bf16)
        for t in range(tiles):
            lanes = slice(t * 128, (t + 1) * 128)
            for h in range(GROUP):
                rows = slice(HEAD * h, HEAD * (h + 1))
                out_ref[t, rows] = (acc[rows, lanes] / total[h : h + 1, lanes]).astype(bf16)
            out_ref[t, WIDE:] = packed[:, lanes]


def attend(queries, blocks, carry, last=False, qb=512):
    first = carry is None
    carry = [] if first else carry
    count = queries.shape[0] * 128 if first else queries.shape[2]
    keys = sum(b.shape[0] for b in blocks)
    carry_shapes = [(16, count), (WIDE, count)]
    scratch = []
    if last:
        out_shape = [jax.ShapeDtypeStruct((count // 128, WIDE + STATS, 128), bf16)]
        scratch = [pltpu.VMEM(s, f32) for s in carry_shapes]
    else:
        out_shape = [jax.ShapeDtypeStruct(s, f32) for s in carry_shapes]
        if first:
            out_shape.append(jax.ShapeDtypeStruct((GROUP, 2 * HEAD, count), bf16))
    outs = pl.pallas_call(
        functools.partial(attend_kernel, first, last, qb, len(blocks)),
        in_specs=[pl.BlockSpec(memory_space=pltpu.VMEM)] * (1 + len(blocks) + len(carry)),
        out_specs=[pl.BlockSpec(memory_space=pltpu.VMEM)] * len(out_shape),
        out_shape=out_shape,
        scratch_shapes=scratch,
        compiler_params=pltpu.CompilerParams(vmem_limit_bytes=24 * 2**20),
        cost_estimate=pl.CostEstimate(
            flops=GROUP * count * keys * 1, bytes_accessed=1024, transcendentals=0
        ),
    )(queries, *blocks, *carry)
    return outs[0] if last else outs


def finish_kernel(parts_ref, w_ref, out_ref, rows):
    groups = parts_ref.shape[0] // 2
    pieces = []
    for g in range(groups):
        pair = [parts_ref[g], parts_ref[groups + g]]
        logs = []
        for p in pair:
            s = p[WIDE:].astype(f32)
            logs.append((s[0:3] + s[3:6]) + s[6:9])
        top = jnp.maximum(logs[0], logs[1])
        shares = [jnp.exp2(a - top) for a in logs]
        total = shares[0] + shares[1]
        for h in range(GROUP):
            head = slice(HEAD * h, HEAD * (h + 1))
            both = [p[head].astype(f32) * (s[h : h + 1] / total[h : h + 1]) for p, s in zip(pair, shares)]
            pieces.append(both[0] + both[1])
    attended = jnp.concatenate(pieces, 0).T.astype(bf16)
    keep(rows, jnp.dot(attended, w_ref[...], preferred_element_type=f32))
    for r in range(out_ref.shape[0]):
        start = 8 * (r % 2) + r // 2
        out_ref[r] = every_nth(rows, start, 16).astype(bf16)


def finish(parts, w_out):
    shape = (parts.shape[2], w_out.shape[1])
    return pl.pallas_call(
        finish_kernel,
        out_shape=jax.ShapeDtypeStruct((16, 8, shape[1]), bf16),
        scratch_shapes=[pltpu.VMEM((shape[1] // 128, shape[0], 128), f32)],
        compiler_params=pltpu.CompilerParams(vmem_limit_bytes=24 * 2**20),
    )(parts, w_out)


def on_device(patches, norm_gain, w_qkv, pool_q, pool_kv, w_out):
    here = [lax.axis_index("y").reshape(1)]
    patches, here = lax.optimization_barrier((patches, here))
    tokens, last_column, last_row, last_token = normalised_tokens(patches, norm_gain)
    halo = (passed_along(last_row, ROW), passed_along(last_column, COL), corner(last_token))
    own_q, own_kv = project_own(tokens, w_qkv)
    groups = lax.axis_size("y")
    part = (32, 2 * WIDE)
    parts = pool_call(keyvals_kernel, own_kv, halo, w_qkv, pool_kv, [part] * groups, [(groups, *part)], here)
    own = jnp.concatenate([parts[0]] + [shifted(p, "y", d) for d, p in enumerate(parts) if d], 0)
    tie = lax.optimization_barrier
    (turned,) = pool_call(queries_kernel, own_q, halo, w_qkv, pool_q, [(2 * groups, WIDE, 128)])
    own, turned = tie((own, turned))
    line = [own, shifted(own, "zq", 2), shifted(own, "zq", 1), shifted(own, "zq", -1)]
    every_query = lax.all_to_all(turned, ("zc", "y"), 0, 0, tiled=True)
    line = jnp.concatenate(line, 0)
    after, before = shifted_x(line, 1), shifted_x(line, -1)
    swap = lambda block: shifted(block, "core", 1)
    *carry, padded = attend(every_query, [line], None)
    carry = attend(padded, [swap(line)], carry)
    after, before, carry = tie((after, before, carry))
    half = line.shape[0] // 2
    far = [shifted_x(after[:half], 1), shifted_x(before[half:], -1)]
    for block in (after, swap(after), before, swap(before)):
        carry = attend(padded, [block], carry)
    far, carry = tie((far, carry))
    swapped = [swap(block) for block in far]
    carry = attend(padded, far, carry)
    partial = attend(padded, swapped, carry, last=True)
    parts = lax.all_to_all(partial, ("zc", "y"), 0, 0, tiled=True)
    return finish(parts, w_out)


def solution(mesh):
    fine = Mesh(mesh.devices.reshape(4, 2, 2, 2, 4, 2), AXES)
    tiles = P(ROW, COL, None)
    return jax.shard_map(
        on_device,
        mesh=fine,
        in_specs=(tiles, P(), P(), P(), P(), P()),
        out_specs=tiles,
        check_vma=False,
    )
```
